32 devices in a mesh: dp: 8 (over y, x, core), ctx: 4 (over z).
Axes of the slice: x: 2, y: 2, z: 4, core: 2. Of those that a mesh axis runs over, the one named last changes fastest.
Arguments:
- value: bfloat16 [8, 512, 512], P('dp', 'ctx'), may hold values from -6 to 6
- gate_one: bfloat16 [8, 512, 512], P('dp', 'ctx'), may hold values from -6 to 6
- gate_two: bfloat16 [8, 512, 512], P('dp', 'ctx'), may hold values from -6 to 6
- filters: bfloat16 [2, 512, 512], replicated, may hold values from -0.25 to 0.25
- out_weight: bfloat16 [512, 512], replicated, may hold values from -0.25 to 0.25
- grad_out: bfloat16 [8, 512, 512], P('dp', 'ctx'), may hold values from -6 to 6
Outputs:
- mixed: bfloat16 [8, 512, 512], P('dp', 'ctx')
- grad_value: bfloat16 [8, 512, 512], P('dp', 'ctx')
- grad_gate_one: bfloat16 [8, 512, 512], P('dp', 'ctx')
- grad_gate_two: bfloat16 [8, 512, 512], P('dp', 'ctx')
- filter_grad: float32 [2, 512, 512], P(None, 'ctx', 'dp')
- weight_grad: float32 [512, 512], P('dp', 'ctx')
The draws below stay inside these ranges and needn't reach their ends.
All inputs are finite; a program needn't handle non-finite values.
Results may differ from the reference program's by a relative error of at most 0.019.
Values may be sent and summed in bfloat16 or wider, within the bound.
No kernel may reach another device: no remote copies, remote signals or barrier semaphores. Data moves between devices by JAX's collectives and lax.ppermute only.
A program may use at most 128 MiB of HBM per device.

```python
import jax
import jax.numpy as jnp

D = 512
LENGTH = 512
DOCS = 8


def levels(stream_key, shape, pieces, smallest, high):
    loudness = 1.0
    for dim, parts in pieces:
        steps = jax.random.uniform(jax.random.fold_in(jax.random.fold_in(stream_key, 6), dim), (parts,), jnp.float32, smallest / len(pieces), high / len(pieces))
        loudness = loudness * jnp.repeat(jnp.exp(steps), shape[dim] // parts).reshape((-1,) + (1,) * (len(shape) - 1 - dim))
    return loudness


def bell_draw(own_key, dims, scale, most, pieces=(), held_as=jnp.bfloat16):
    array = jax.random.normal(own_key, dims, jnp.float32) * scale
    if len(pieces) > 0:
        array = levels(own_key, dims, pieces, -0.22, 0.18) * array
    return jnp.clip(array, min=-most, max=most).astype(held_as)


def setup_inputs(seed: int = 0) -> dict:
    seeds = jax.random.split(jax.random.key(seed), 7)
    value = bell_draw(seeds[0], (DOCS, LENGTH, D), 1.0, 6.0, ((0, 8), (1, 4)))
    gate_one = bell_draw(seeds[1], (DOCS, LENGTH, D), 1.0, 6.0, ((0, 8), (1, 4)))
    gate_two = bell_draw(seeds[2], (DOCS, LENGTH, D), 1.0, 6.0, ((0, 8), (1, 4)))
    filters = bell_draw(seeds[3], (2, LENGTH, D), LENGTH ** -0.5, 0.25)
    out_weight = bell_draw(seeds[4], (D, D), D ** -0.5, 0.25)
    grad_out = bell_draw(seeds[5], (DOCS, LENGTH, D), 1.0, 6.0, ((0, 8), (1, 4)))
    return dict(value=value, gate_one=gate_one, gate_two=gate_two, filters=filters, out_weight=out_weight, grad_out=grad_out)


def causal(filt, stream):
    length = stream.shape[1]
    width = 2 * length
    filter_freq = jnp.fft.rfft(filt.astype(jnp.float32), n=width, axis=0)
    stream_freq = jnp.fft.rfft(stream.astype(jnp.float32), n=width, axis=1)
    return jnp.fft.irfft(filter_freq[None] * stream_freq, n=width, axis=1)[:, :length]


def anti_causal(filt, grads):
    return jnp.flip(causal(filt, jnp.flip(grads, 1)), 1)


def filter_terms(stream, grads):
    length = stream.shape[1]
    width = 2 * length
    stream_freq = jnp.fft.rfft(stream.astype(jnp.float32), n=width, axis=1)
    grad_freq = jnp.fft.rfft(grads.astype(jnp.float32), n=width, axis=1)
    summed = jnp.sum(jnp.conj(stream_freq) * grad_freq, axis=0)
    return jnp.fft.irfft(summed, n=width, axis=0)[:length]


def reference(value, gate_one, gate_two, filters, out_weight, grad_out):
    first_conv = causal(filters[0], value)
    mixed_input = (gate_one.astype(jnp.float32) * first_conv).astype(jnp.bfloat16)
    second_conv = causal(filters[1], mixed_input)
    gated = (gate_two.astype(jnp.float32) * second_conv).astype(jnp.bfloat16)
    flat_gated = gated.reshape(-1, D)
    flat_grad = grad_out.reshape(-1, D)
    mixed = jnp.dot(flat_gated, out_weight, preferred_element_type=jnp.float32).astype(jnp.bfloat16).reshape(value.shape)
    grad_gated = jnp.dot(flat_grad, out_weight.T, preferred_element_type=jnp.float32).reshape(value.shape)
    grad_gate_two = (grad_gated * second_conv).astype(jnp.bfloat16)
    grad_second = (grad_gated * gate_two.astype(jnp.float32)).astype(jnp.bfloat16)
    grad_mixed = anti_causal(filters[1], grad_second)
    grad_gate_one = (grad_mixed * first_conv).astype(jnp.bfloat16)
    grad_first = (grad_mixed * gate_one.astype(jnp.float32)).astype(jnp.bfloat16)
    grad_value = anti_causal(filters[0], grad_first).astype(jnp.bfloat16)
    filter_grad = jnp.stack([filter_terms(value, grad_first), filter_terms(mixed_input, grad_second)]) / DOCS
    weight_grad = jnp.dot(flat_gated.T, flat_grad, preferred_element_type=jnp.float32) / DOCS
    return mixed, grad_value, grad_gate_one, grad_gate_two, filter_grad, weight_grad
```

```python
import functools
import math

import jax
import jax.numpy as jnp
import ml_dtypes
import numpy as np
from jax import lax
from jax.experimental import pallas as pl
from jax.experimental.pallas import tpu as pltpu
from jax.sharding import PartitionSpec as P

F32 = jnp.float32
BF16 = jnp.bfloat16


def split_table(table):
    high = table.astype(ml_dtypes.bfloat16)
    low = (table - high.astype(np.float64)).astype(ml_dtypes.bfloat16)
    return high, low


@functools.lru_cache(maxsize=None)
def make_tables(length):
    period = 2 * length
    bins = np.arange(length)
    moments = np.arange(length)
    radians = (bins[:, None] * moments[None, :] % period) * (2.0 * math.pi / period)
    cosines, sines = np.cos(radians), -np.sin(radians)
    sines[0] = np.where(moments % 2 == 0, 1.0, -1.0)
    forward = np.concatenate([cosines, sines], axis=0)
    weights = np.full((period,), 2.0 / period)
    weights[0] = weights[length] = 1.0 / period
    inverse = forward.T * weights[None, :]
    return split_table(forward), split_table(inverse)


def product(left, right, conj_left):
    half = left.shape[0] // 2
    left_re, left_im = left[:half], left[half:]
    right_re, right_im = right[:half], right[half:]
    border = lax.broadcasted_iota(jnp.int32, left_re.shape, 0) == 0
    cross = left_im * right_im
    straight = left_re * right_re
    if conj_left:
        real = straight + jnp.where(border, 0.0, cross)
        imag = left_re * right_im - left_im * right_re
    else:
        real = straight - jnp.where(border, 0.0, cross)
        imag = left_re * right_im + left_im * right_re
    return jnp.concatenate([real, jnp.where(border, cross, imag)], axis=0)


def mxu(left, right):
    return jnp.dot(left, right, preferred_element_type=F32)


def to_spectrum(high, low, stream):
    return mxu(high[...], stream) + mxu(low[...], stream)


def from_spectrum(high, spectrum):
    return mxu(high[...], spectrum.astype(BF16))


def pick_columns(ref, index, width, count):
    if width % 128 == 0:
        return ref[:, pl.ds(pl.multiple_of(index * width, width), width)]
    whole = ref[...]
    out = whole[:, :width]
    for other in range(1, count):
        out = jnp.where(index == other, whole[:, other * width : (other + 1) * width], out)
    return out


def pick_rows(ref, index, rows):
    return ref[pl.ds(pl.multiple_of(index * rows, rows), rows), :]


def put_rows(ref, index, rows, block):
    ref[pl.ds(pl.multiple_of(index * rows, rows), rows), :] = block


def call(kernel, out_shape, args, scratch=(), flops=0, limit=16):
    vmem = pl.BlockSpec(memory_space=pltpu.VMEM)
    total = sum(math.prod(a.shape) * a.dtype.itemsize for a in args)
    return pl.pallas_call(
        kernel,
        out_shape=out_shape,
        in_specs=[vmem] * len(args),
        out_specs=jax.tree.map(lambda _: vmem, out_shape),
        scratch_shapes=list(scratch),
        compiler_params=pltpu.CompilerParams(vmem_limit_bytes=limit * 2**20),
        cost_estimate=pl.CostEstimate(flops=flops, bytes_accessed=total, transcendentals=0),
    )(*args)


def on_device(value, gate_one, gate_two, filters, out_weight, grad_out):
    rows, width = value.shape[1:]
    seq = lax.axis_size("ctx")
    data = lax.axis_size("dp")
    here = lax.axis_index("ctx")
    length = rows * seq
    cols = width // seq
    limit = 16 if length <= 512 else 56
    (fwd_high, fwd_low), (inv_high, _) = make_tables(length)
    fwd_high, fwd_low, inv_high = map(jnp.asarray, (fwd_high, fwd_low, inv_high))
    table_flops = 2 * 2 * length * length * cols

    def ahead(step):
        return lax.rem(lax.axis_index("ctx") + step, seq)

    def behind(step):
        return lax.rem(lax.axis_index("ctx") + seq - step, seq)

    def around(blocks):
        out = [blocks[0]]
        for step in range(1, seq):
            pairs = [(i, (i + step) % seq) for i in range(seq)]
            out.append(lax.ppermute(blocks[step], "ctx", pairs))
        return out

    value, gate_one, gate_two, cotangent = value[0], gate_one[0], gate_two[0], grad_out[0]

    def pack_kernel(value_ref, gate_ref, *outs):
        for step, out in enumerate(outs):
            out[0] = pick_columns(value_ref, ahead(step), cols, seq)
            out[1] = pick_columns(gate_ref, ahead(step), cols, seq)

    pair = jax.ShapeDtypeStruct((2, rows, cols), BF16)
    single = jax.ShapeDtypeStruct((rows, cols), BF16)
    with jax.named_scope("pack_value"):
        sends = call(pack_kernel, [pair] * seq, (value, gate_one))
    value_parts = around(sends)

    def grad_kernel(cot_ref, weight_ref, gate_ref, grad_ref, *rest):
        outs, scratch = rest[:-1], rest[-1]
        grad = lax.dot_general(
            cot_ref[...], weight_ref[...], (((1,), (1,)), ((), ())), preferred_element_type=F32
        )
        grad_ref[...] = grad
        scratch[...] = grad * gate_ref[...].astype(F32)
        for step, out in enumerate(outs):
            out[...] = pick_columns(scratch, ahead(step), cols, seq).astype(BF16)

    with jax.named_scope("grad_second"):
        grad_gated, *sends = call(
            grad_kernel,
            [jax.ShapeDtypeStruct((rows, width), F32)] + [single] * seq,
            (cotangent, out_weight, gate_two),
            scratch=[pltpu.VMEM((rows, width), F32)],
            flops=2 * rows * width * width,
        )
    grad_parts = around(sends)

    def filter_kernel(filters_ref, high, low, out):
        for index in range(2):
            out[index] = to_spectrum(high, low, filters_ref[index])

    with jax.named_scope("filter_spectra"):
        own_filters = lax.dynamic_slice_in_dim(filters, here * cols, cols, 2)
        spectra = call(
            filter_kernel,
            jax.ShapeDtypeStruct((2, 2 * length, cols), F32),
            (own_filters, fwd_high, fwd_low),
            flops=4 * table_flops,
            limit=limit,
        )

    def forward_kernel(*refs):
        parts, refs = refs[:seq], refs[seq:]
        filt, high, low, back, first_ref, value_spec, mixed_spec = refs[:7]
        outs, (stream, second) = refs[7:-2], refs[-2:]
        for step, part in enumerate(parts):
            put_rows(stream, behind(step), rows, part[0])
        value_spec[...] = to_spectrum(high, low, stream[...])
        first_ref[...] = from_spectrum(back, product(filt[0], value_spec[...], False))
        for step, part in enumerate(parts):
            gated = part[1].astype(F32) * pick_rows(first_ref, behind(step), rows)
            put_rows(stream, behind(step), rows, gated.astype(BF16))
        mixed_spec[...] = to_spectrum(high, low, stream[...])
        second[...] = from_spectrum(back, product(filt[1], mixed_spec[...], False))
        for step, out in enumerate(outs):
            out[...] = pick_rows(second, ahead(step), rows).astype(BF16)

    stream_f32 = jax.ShapeDtypeStruct((length, cols), F32)
    spectrum_f32 = jax.ShapeDtypeStruct((2 * length, cols), F32)
    with jax.named_scope("forward_convolutions"):
        first_conv, value_spectrum, mixed_spectrum, *sends = call(
            forward_kernel,
            [stream_f32, spectrum_f32, spectrum_f32] + [single] * seq,
            (*value_parts, spectra, fwd_high, fwd_low, inv_high),
            scratch=[pltpu.VMEM((length, cols), BF16), pltpu.VMEM((length, cols), F32)],
            flops=6 * table_flops,
            limit=limit,
        )
    second_parts = around(sends)

    per_ctx = data // seq
    fine = cols // per_ctx
    packed = fine == 64 and per_ctx == 2

    def backward_kernel(*refs):
        parts, values, refs = refs[:seq], refs[seq : 2 * seq], refs[2 * seq :]
        filt, first_ref, value_spec, mixed_spec, high, low, back, lags = refs[:8]
        outs, (stream, wide, total) = refs[8:-3], refs[-3:]
        for step, part in enumerate(parts):
            put_rows(stream, behind(step), rows, part[...])
        spectrum = to_spectrum(high, low, stream[...])
        wide[:, :cols] = product(filt[1], spectrum, True).astype(BF16)
        wide[:, cols:] = product(mixed_spec[...], spectrum, True).astype(BF16)
        both = mxu(back[...], wide[...])
        total[...] = both[:, :cols]
        lag_second = both[:, cols:]
        for step, part in enumerate(values):
            grad = pick_rows(total, behind(step), rows)
            put_rows(stream, behind(step), rows, (grad * part[1].astype(F32)).astype(BF16))
        for step, out in enumerate(outs):
            grad = pick_rows(total, ahead(step), rows) * pick_rows(first_ref, ahead(step), rows)
            out[0] = grad.astype(BF16)
        spectrum = to_spectrum(high, low, stream[...])
        wide[:, :cols] = product(filt[0], spectrum, True).astype(BF16)
        wide[:, cols:] = product(value_spec[...], spectrum, True).astype(BF16)
        both = mxu(back[...], wide[...])
        total[...] = both[:, :cols]
        lag_first = both[:, cols:]
        for step, out in enumerate(outs):
            out[1] = pick_rows(total, ahead(step), rows).astype(BF16)
        if packed:
            low_lanes = lax.broadcasted_iota(jnp.int32, lag_first.shape, 1) < fine
            turned_first = pltpu.roll(lag_first, fine, axis=1)
            turned_second = pltpu.roll(lag_second, fine, axis=1)
            lags[0] = jnp.where(low_lanes, lag_first, turned_second).astype(BF16)
            lags[1] = jnp.where(low_lanes, turned_first, lag_second).astype(BF16)
        else:
            lags[0] = lag_first.astype(BF16)
            lags[1] = lag_second.astype(BF16)

    with jax.named_scope("backward_convolutions"):
        lags, *sends = call(
            backward_kernel,
            [jax.ShapeDtypeStruct((2, length, cols), BF16)] + [pair] * seq,
            (
                *grad_parts,
                *value_parts,
                spectra,
                first_conv,
                value_spectrum,
                mixed_spectrum,
                fwd_high,
                fwd_low,
                inv_high,
            ),
            scratch=[
                pltpu.VMEM((length, cols), BF16),
                pltpu.VMEM((2 * length, 2 * cols), BF16),
                pltpu.VMEM((length, cols), F32),
            ],
            flops=8 * table_flops,
            limit=limit,
        )
    result_parts = around(sends)

    def gated_kernel(*refs):
        parts, (gate_ref, cot_ref, second_ref, gated_ref, weight_ref) = refs[:seq], refs[seq:]
        for step, part in enumerate(parts):
            if cols % 128 == 0:
                start = pl.multiple_of(behind(step) * cols, cols)
                second_ref[:, pl.ds(start, cols)] = part[...]
            else:
                for index in range(seq):

                    @pl.when(behind(step) == index)
                    def _():
                        second_ref[:, index * cols : (index + 1) * cols] = part[...]

        gated = (gate_ref[...].astype(F32) * second_ref[...].astype(F32)).astype(BF16)
        gated_ref[...] = gated
        weight_ref[...] = lax.dot_general(
            gated, cot_ref[...], (((0,), (0,)), ((), ())), preferred_element_type=F32
        ).astype(BF16)

    wide_bf16 = jax.ShapeDtypeStruct((rows, width), BF16)
    with jax.named_scope("weight_partial"):
        second_conv, gated, weight_part = call(
            gated_kernel,
            [wide_bf16, wide_bf16, jax.ShapeDtypeStruct((width, width), BF16)],
            (*second_parts, gate_two, cotangent),
            flops=2 * rows * width * width,
        )
    mixed = mxu(gated, out_weight).astype(BF16)
    grad_gate_two = (grad_gated * second_conv.astype(F32)).astype(BF16)

    core = lax.rem(lax.axis_index("dp"), 2)
    chip = lax.div(lax.axis_index("dp"), 2)
    chips = data // 2

    def over_documents(terms):
        shape = terms.shape[1:]
        by_core = terms.reshape(chips, 2, *shape)
        kept = lax.dynamic_index_in_dim(by_core, core, 1, keepdims=False)
        given = lax.dynamic_index_in_dim(by_core, 1 - core, 1, keepdims=False)
        swap = [(i, i ^ 1) for i in range(data)]
        kept = kept.astype(F32) + lax.ppermute(given, "dp", swap).astype(F32)
        total = lax.dynamic_index_in_dim(kept, chip, 0, keepdims=False)
        for step in range(1, chips):
            pairs = [(i, (i + 2 * step) % data) for i in range(data)]
            block = lax.dynamic_index_in_dim(kept, lax.rem(chip + step, chips), 0, keepdims=False)
            total = total + lax.ppermute(block.astype(BF16), "dp", pairs).astype(F32)
        return total

    if packed:
        lag_terms = lags.reshape(2, seq, rows, cols).transpose(1, 0, 2, 3)
    else:
        lag_terms = lags.reshape(2, seq, rows, per_ctx, fine).transpose(1, 3, 2, 0, 4)
    lag_terms = lag_terms.reshape(data, rows, 2 * fine)
    lag_sum = over_documents(lag_terms)
    weight_sum = over_documents(weight_part.reshape(data, width // data, width))

    pairs = []
    for i in range(data):
        for j in range(seq):
            pairs.append((i * seq + j, (per_ctx * j + i % per_ctx) * seq + i // per_ctx))
    lag_own = lax.ppermute(lag_sum.astype(BF16), ("dp", "ctx"), pairs)
    filter_grad = lag_own.reshape(rows, 2, fine).transpose(1, 0, 2).astype(F32) / data

    weight_blocks = weight_sum.reshape(width // data, seq, cols)
    total = lax.dynamic_index_in_dim(weight_blocks, here, 1, keepdims=False)
    for step in range(1, seq):
        block = lax.dynamic_index_in_dim(weight_blocks, ahead(step), 1, keepdims=False)
        ring = [(i, (i + step) % seq) for i in range(seq)]
        total = total + lax.ppermute(block.astype(BF16), "ctx", ring).astype(F32)
    weight_grad = total / data

    def unpack_kernel(*refs):
        parts, (gate_ref, value_ref) = refs[:seq], refs[seq:]
        for step, part in enumerate(parts):
            if cols % 128 == 0:
                start = pl.multiple_of(behind(step) * cols, cols)
                gate_ref[:, pl.ds(start, cols)] = part[0]
                value_ref[:, pl.ds(start, cols)] = part[1]
            else:
                for index in range(seq):

                    @pl.when(behind(step) == index)
                    def _():
                        gate_ref[:, index * cols : (index + 1) * cols] = part[0]
                        value_ref[:, index * cols : (index + 1) * cols] = part[1]

    with jax.named_scope("unpack_results"):
        grad_gate_one, grad_value = call(unpack_kernel, [wide_bf16, wide_bf16], result_parts)
    return (
        mixed[None],
        grad_value[None],
        grad_gate_one[None],
        grad_gate_two[None],
        filter_grad,
        weight_grad,
    )


def solution(mesh):
    stream = P("dp", "ctx", None)
    return jax.shard_map(
        on_device,
        mesh=mesh,
        in_specs=(stream, stream, stream, P(), P(), stream),
        out_specs=(stream, stream, stream, stream, P(None, "ctx", "dp"), P("dp", "ctx")),
        check_vma=False,
    )
```

```python
import functools
import math

import jax
import jax.numpy as jnp
import ml_dtypes
import numpy as np
from jax import lax
from jax.experimental import pallas as pl
from jax.experimental.pallas import tpu as pltpu
from jax.sharding import PartitionSpec as P

F32 = jnp.float32
BF16 = jnp.bfloat16


def split_table(table):
    high = table.astype(ml_dtypes.bfloat16)
    low = (table - high.astype(np.float64)).astype(ml_dtypes.bfloat16)
    return jnp.asarray(high), jnp.asarray(low)


@functools.lru_cache(maxsize=None)
def table_values(block):
    period = 2 * block
    bins = np.arange(block)
    radians = (bins[:, None] * bins[None, :] % period) * (2.0 * math.pi / period)
    cosines, sines = np.cos(radians), -np.sin(radians)
    sines[0] = np.where(bins % 2 == 0, 1.0, -1.0)
    forward = np.concatenate([cosines, sines], axis=0)
    weights = np.full((period,), 2.0 / period)
    weights[0] = weights[block] = 1.0 / period
    return forward, forward.T * weights[None, :]


def mxu(left, right):
    return jnp.dot(left, right, preferred_element_type=F32)


def beside(stream, block):
    return jnp.concatenate(
        [stream[i : i + block] for i in range(0, stream.shape[0], block)], axis=1
    )


def to_spectra(high, low, stream):
    blocks = beside(stream, high.shape[1])
    return mxu(high[...], blocks) + mxu(low[...], blocks)


def from_spectra(high, spectra):
    return mxu(high[...], spectra.astype(BF16))


def parity(shape):
    row = lax.broadcasted_iota(jnp.int32, shape, 0)
    return jnp.where(row % 2 == 0, 1.0, -1.0)


def with_previous(spectra, cols):
    sign = parity((spectra.shape[0], cols))
    out = [spectra[:, :cols]]
    for i in range(cols, spectra.shape[1], cols):
        out.append(spectra[:, i : i + cols] + sign * spectra[:, i - cols : i])
    return jnp.concatenate(out, axis=1)


def sum_of_products(terms, conj_left):
    half = terms[0][0].shape[0] // 2
    border = lax.broadcasted_iota(jnp.int32, (half, terms[0][0].shape[1]), 0) == 0
    straight = cross = imag = 0.0
    for left, right in terms:
        left_re, left_im, right_re, right_im = left[:half], left[half:], right[:half], right[half:]
        straight += left_re * right_re
        cross += left_im * right_im
        if conj_left:
            imag += left_re * right_im - left_im * right_re
        else:
            imag += left_re * right_im + left_im * right_re
    inner = jnp.where(border, 0.0, cross)
    real = straight + inner if conj_left else straight - inner
    return jnp.concatenate([real, jnp.where(border, cross, imag)], axis=0)


def columns(ref, index, cols):
    return ref[:, index * cols : (index + 1) * cols]


def causal_product(filt, spectra, cols):
    count = spectra.shape[1] // cols
    out = []
    for i in range(count):
        terms = [(columns(filt, i - a, cols), columns(spectra, a, cols)) for a in range(i + 1)]
        out.append(sum_of_products(terms, False))
    return jnp.concatenate(out, axis=1)


def anti_product(left, spectra, cols):
    count = spectra.shape[1] // cols
    out = []
    for i in range(count):
        terms = [
            (columns(left, a - i, cols), columns(spectra, a, cols)) for a in range(i, count)
        ]
        out.append(sum_of_products(terms, True))
    return jnp.concatenate(out, axis=1)


def pick_columns(ref, index, width, count):
    if width % 128 == 0:
        return ref[:, pl.ds(pl.multiple_of(index * width, width), width)]
    whole = ref[...]
    out = whole[:, :width]
    for other in range(1, count):
        out = jnp.where(index == other, whole[:, other * width : (other + 1) * width], out)
    return out


def put_columns(ref, index, width, count, block):
    if width % 128 == 0:
        ref[:, pl.ds(pl.multiple_of(index * width, width), width)] = block
        return
    for other in range(count):

        @pl.when(index == other)
        def _():
            ref[:, other * width : (other + 1) * width] = block


def pick_rows(ref, index, rows):
    return ref[pl.ds(pl.multiple_of(index * rows, rows), rows), :]


def put_rows(ref, index, rows, block):
    ref[pl.ds(pl.multiple_of(index * rows, rows), rows), :] = block


def call(kernel, outs, args, scratch=(), flops=0, limit=16, anywhere=False):
    vmem = pl.BlockSpec(memory_space=pltpu.VMEM)
    source = pl.BlockSpec(memory_space=pl.ANY) if anywhere else vmem
    total = sum(math.prod(a.shape) * a.dtype.itemsize for a in args)
    return pl.pallas_call(
        kernel,
        out_shape=[jax.ShapeDtypeStruct(shape, dtype) for shape, dtype in outs],
        in_specs=[source] * len(args),
        out_specs=[vmem] * len(outs),
        scratch_shapes=list(scratch),
        compiler_params=pltpu.CompilerParams(vmem_limit_bytes=limit * 2**20),
        cost_estimate=pl.CostEstimate(flops=flops, bytes_accessed=total, transcendentals=0),
    )(*args)


def on_device(value, gate_one, gate_two, filters, out_weight, grad_out):
    rows, width = value.shape[1:]
    seq = lax.axis_size("ctx")
    data = lax.axis_size("dp")
    length = rows * seq
    cols = width // seq
    block = math.gcd(length, 256)
    per_ctx = data // seq
    fine = cols // per_ctx
    chips = data // 2
    own_rows = width // data
    fast = cols == 128 and per_ctx == 2 and rows % (width // cols) == 0
    limit = 16 if length <= 512 else 48
    forward, inverse = table_values(block)
    (fwd_high, fwd_low), (inv_high, _) = split_table(forward), split_table(inverse)
    spectra_shape = (2 * block, length // block * cols)
    table_flops = 4 * block * length * cols

    def ahead(step):
        return lax.rem(lax.axis_index("ctx") + step, seq)

    def behind(step):
        return lax.rem(lax.axis_index("ctx") + seq - step, seq)

    def around(blocks):
        out = [blocks[0]]
        for step in range(1, seq):
            pairs = [(i, (i + step) % seq) for i in range(seq)]
            out.append(lax.ppermute(blocks[step], "ctx", pairs))
        return out

    def load_kernel(value_ref, gate_ref, *refs):
        sources, refs = refs[:3], refs[3:]
        outs, copies, (whole, sems) = refs[:seq], refs[seq : seq + 3], refs[seq + 3 :]
        started = []
        if cols % 128 == 0:
            for step, out in enumerate(outs):
                lanes = pl.ds(pl.multiple_of(ahead(step) * cols, cols), cols)
                started.append((value_ref.at[0, :, lanes], out.at[0]))
                started.append((gate_ref.at[0, :, lanes], out.at[1]))
        else:
            started.append((value_ref.at[0], whole.at[0]))
            started.append((gate_ref.at[0], whole.at[1]))
        for source, copy in zip(sources, copies):
            started.append((source.at[0] if len(source.shape) == 3 else source, copy))
        started = [
            pltpu.make_async_copy(source, target, sems.at[index])
            for index, (source, target) in enumerate(started)
        ]
        for copy in started:
            copy.start()
        for copy in started:
            copy.wait()
        if cols % 128 != 0:
            for step, out in enumerate(outs):
                for index in range(2):
                    out[index] = pick_columns(whole.at[index], ahead(step), cols, seq)

    pair, single = ((2, rows, cols), BF16), ((rows, cols), BF16)
    wide_bf16, wide_f32 = ((rows, width), BF16), ((rows, width), F32)
    with jax.named_scope("load"):
        *sends, cotangent, weight, gate = call(
            load_kernel,
            [pair] * seq + [wide_bf16, ((width, width), BF16), wide_bf16],
            (value, gate_one, grad_out, out_weight, gate_two),
            scratch=[pltpu.VMEM((2, rows, width), BF16), pltpu.SemaphoreType.DMA((2 * seq + 3,))],
            anywhere=True,
        )
    value_parts = around(sends)

    def grad_kernel(cot_ref, weight_ref, gate_ref, grad_ref, *rest):
        outs, scratch = rest[:-1], rest[-1]
        grad = lax.dot_general(
            cot_ref[...], weight_ref[...], (((1,), (1,)), ((), ())), preferred_element_type=F32
        )
        grad_ref[...] = grad
        scratch[...] = grad * gate_ref[...].astype(F32)
        for step, out in enumerate(outs):
            out[...] = pick_columns(scratch, ahead(step), cols, seq).astype(BF16)

    with jax.named_scope("grad_second"):
        grad_gated, *sends = call(
            grad_kernel,
            [wide_f32] + [single] * seq,
            (cotangent, weight, gate),
            scratch=[pltpu.VMEM((rows, width), F32)],
            flops=2 * rows * width * width,
        )
    grad_parts = around(sends)

    def filter_kernel(filters_ref, high, low, out):
        for index in range(2):
            out[index] = with_previous(to_spectra(high, low, filters_ref[index]), cols)

    with jax.named_scope("filter_spectra"):
        own_filters = lax.dynamic_slice_in_dim(filters, lax.axis_index("ctx") * cols, cols, 2)
        (filter_spectra,) = call(
            filter_kernel,
            [((2, *spectra_shape), F32)],
            (own_filters, fwd_high, fwd_low),
            flops=4 * table_flops,
            limit=limit,
        )

    def forward_kernel(*refs):
        parts, refs = refs[:seq], refs[seq:]
        filt, high, low, back, first_ref, value_spec, mixed_spec = refs[:7]
        outs, (stream, second) = refs[7:-2], refs[-2:]
        for step, part in enumerate(parts):
            put_rows(stream, behind(step), rows, part[0])
        spectra = to_spectra(high, low, stream[...])
        value_spec[...] = with_previous(spectra, cols)
        conv = from_spectra(back, causal_product(filt[0], spectra, cols))
        for i in range(length // block):
            first_ref[i * block : (i + 1) * block] = columns(conv, i, cols)
        for step, part in enumerate(parts):
            gated = part[1].astype(F32) * pick_rows(first_ref, behind(step), rows)
            put_rows(stream, behind(step), rows, gated.astype(BF16))
        spectra = to_spectra(high, low, stream[...])
        mixed_spec[...] = with_previous(spectra, cols)
        conv = from_spectra(back, causal_product(filt[1], spectra, cols))
        for i in range(length // block):
            second[i * block : (i + 1) * block] = columns(conv, i, cols)
        for step, out in enumerate(outs):
            out[...] = pick_rows(second, ahead(step), rows).astype(BF16)

    with jax.named_scope("forward_convolutions"):
        first_conv, value_spectra, mixed_spectra, *sends = call(
            forward_kernel,
            [((length, cols), F32), (spectra_shape, F32), (spectra_shape, F32)] + [single] * seq,
            (*value_parts, filter_spectra, fwd_high, fwd_low, inv_high),
            scratch=[pltpu.VMEM((length, cols), BF16), pltpu.VMEM((length, cols), F32)],
            flops=6 * table_flops,
            limit=limit,
        )
    second_parts = around(sends)

    def backward_kernel(*refs):
        parts, values, refs = refs[:seq], refs[seq : 2 * seq], refs[2 * seq :]
        filt, first_ref, value_spec, mixed_spec, high, low, back = refs[:7]
        lags, gate_grad, value_grad, stream, total = refs[7:]
        count = length // block
        for step, part in enumerate(parts):
            put_rows(stream, behind(step), rows, part[...])

        def both(left, other):
            spectra = to_spectra(high, low, stream[...])
            grads = anti_product(left, spectra, cols)
            terms = anti_product(other, spectra, cols)
            return from_spectra(back, jnp.concatenate([grads, terms], axis=1))

        def put_lags(index, out):
            for i in range(count):
                piece = columns(out, count + i, cols)
                lags[index, i * block : (i + 1) * block] = piece

        out = both(filt[1], mixed_spec[...])
        for i in range(count):
            total[i * block : (i + 1) * block] = columns(out, i, cols)
        put_lags(1, out)
        for step, part in enumerate(values):
            grad = pick_rows(total, behind(step), rows)
            put_rows(stream, behind(step), rows, (grad * part[1].astype(F32)).astype(BF16))
        gate_grad[...] = (total[...] * first_ref[...]).astype(BF16)
        out = both(filt[0], value_spec[...])
        for i in range(count):
            value_grad[i * block : (i + 1) * block] = columns(out, i, cols).astype(BF16)
        put_lags(0, out)

    with jax.named_scope("backward_convolutions"):
        lags, gate_grad, value_grad = call(
            backward_kernel,
            [((2, length, cols), F32), ((length, cols), BF16), ((length, cols), BF16)],
            (
                *grad_parts,
                *value_parts,
                filter_spectra,
                first_conv,
                value_spectra,
                mixed_spectra,
                fwd_high,
                fwd_low,
                inv_high,
            ),
            scratch=[pltpu.VMEM((length, cols), BF16), pltpu.VMEM((length, cols), F32)],
            flops=8 * table_flops,
            limit=limit,
        )

    core = lax.rem(lax.axis_index("dp"), 2)
    chip = lax.div(lax.axis_index("dp"), 2)
    lag_rows = rows * cols // width if fast else 0
    term_shape = (chips, own_rows + lag_rows, width)

    def gated_kernel(*refs):
        parts, refs = refs[:seq], refs[seq:]
        gate_ref, cot_ref, lags, second_ref, gated_ref = refs[:5]
        for step, part in enumerate(parts):
            put_columns(second_ref, behind(step), cols, seq, part[...])
        gated = (gate_ref[...].astype(F32) * second_ref[...].astype(F32)).astype(BF16)
        gated_ref[...] = gated
        partial = lax.dot_general(
            gated, cot_ref[...], (((0,), (0,)), ((), ())), preferred_element_type=F32
        )
        if not fast:
            refs[5][...] = partial
            return
        kept, given, whole, packed = refs[5:]
        whole[...] = partial
        lower = lax.broadcasted_iota(jnp.int32, (length, cols), 1) < fine
        packed[0] = jnp.where(lower, lags[0], pltpu.roll(lags[1], fine, axis=1))
        packed[1] = jnp.where(lower, pltpu.roll(lags[0], fine, axis=1), lags[1])
        own_core = lax.rem(lax.axis_index("dp"), 2)
        for out, which in ((kept, own_core), (given, 1 - own_core)):
            for index in range(chips):
                start = pl.multiple_of((2 * index + which) * own_rows, own_rows)
                out[index, :own_rows] = whole[pl.ds(start, own_rows), :].astype(out.dtype)
                for part in range(width // cols):
                    first = index * rows + part * lag_rows
                    out[index, own_rows:, part * cols : (part + 1) * cols] = packed[
                        which, first : first + lag_rows
                    ].astype(out.dtype)

    with jax.named_scope("weight_partial"):
        second_conv, gated, *terms = call(
            gated_kernel,
            [wide_bf16, wide_bf16]
            + ([(term_shape, F32), (term_shape, BF16)] if fast else [((width, width), F32)]),
            (*second_parts, gate, cotangent, lags),
            scratch=[pltpu.VMEM((width, width), F32), pltpu.VMEM((2, length, cols), F32)]
            if fast
            else [],
            flops=2 * rows * width * width,
            limit=limit,
        )

    if not fast:
        lag_terms = lags.reshape(2, seq, rows, per_ctx, fine).transpose(1, 3, 2, 0, 4)
        terms = jnp.concatenate(
            [
                terms[0].reshape(data, own_rows, width),
                lag_terms.reshape(data, rows * 2 * fine // width, width),
            ],
            axis=1,
        )
        by_core = terms.reshape(chips, 2, *terms.shape[1:])
        kept = lax.dynamic_index_in_dim(by_core, core, 1, keepdims=False)
        given = lax.dynamic_index_in_dim(by_core, 1 - core, 1, keepdims=False).astype(BF16)
        lag_rows = rows * 2 * fine // width
    else:
        kept, given = terms
    taken = lax.ppermute(given, "dp", [(i, i ^ 1) for i in range(data)])

    def chip_kernel(kept_ref, taken_ref, own, *outs):
        place = lax.div(lax.axis_index("dp"), 2)
        own[...] = kept_ref[place] + taken_ref[place].astype(F32)
        for step, out in enumerate(outs, 1):
            there = lax.rem(place + step, chips)
            out[...] = (kept_ref[there] + taken_ref[there].astype(F32)).astype(BF16)

    term = (own_rows + lag_rows, width)
    with jax.named_scope("core_sum"):
        own_term, *sends = call(
            chip_kernel,
            [(term, F32)] + [(term, BF16)] * (chips - 1),
            (kept, taken),
            limit=limit,
        )
    chip_terms = []
    for step, block_out in enumerate(sends, 1):
        pairs = [(i, (i + 2 * step) % data) for i in range(data)]
        chip_terms.append(lax.ppermute(block_out, "dp", pairs))

    def mixed_kernel(*refs):
        gated_ref, weight_ref, grad_ref, second_ref, gate_grad, value_grad, _ = refs[:7]
        mixed_ref, gate_ref, outs = refs[7], refs[8], refs[9:]
        mixed_ref[...] = mxu(gated_ref[...], weight_ref[...]).astype(BF16)
        gate_ref[...] = (grad_ref[...] * second_ref[...].astype(F32)).astype(BF16)
        for step, out in enumerate(outs):
            out[0] = pick_rows(gate_grad, ahead(step), rows)
            out[1] = pick_rows(value_grad, ahead(step), rows)

    with jax.named_scope("mixed"):
        mixed, grad_gate_two, *sends = call(
            mixed_kernel,
            [wide_bf16, wide_bf16] + [pair] * seq,
            (gated, weight, grad_gated, second_conv, gate_grad, value_grad, own_term),
            flops=2 * rows * width * width,
            limit=limit,
        )
    result_parts = around(sends)

    if fast:

        def place_kernel(own, *refs):
            arrived, outs, lag, total = refs[: chips - 1], refs[chips - 1 : -2], refs[-2], refs[-1]
            summed = own[...]
            for part in arrived:
                summed = summed + part[...].astype(F32)
            total[...] = summed[:own_rows]
            for step, out in enumerate(outs):
                out[...] = pick_columns(total, ahead(step), cols, seq).astype(out.dtype)
            for part in range(width // cols):
                piece = summed[own_rows:, part * cols : (part + 1) * cols]
                lag[part * lag_rows : (part + 1) * lag_rows] = piece.astype(BF16)

        small = (own_rows, cols)
        with jax.named_scope("chip_sum"):
            *sends, lag_sum = call(
                place_kernel,
                [(small, F32)] + [(small, BF16)] * (seq - 1) + [((rows, 2 * fine), BF16)],
                (own_term, *chip_terms),
                scratch=[pltpu.VMEM((own_rows, width), F32)],
            )
    else:
        total = own_term
        for part in chip_terms:
            total = total + part.astype(F32)
        weight_blocks = total[:own_rows].reshape(own_rows, seq, cols)
        sends = [
            lax.dynamic_index_in_dim(weight_blocks, ahead(step), 1, keepdims=False)
            for step in range(seq)
        ]
        sends = sends[:1] + [part.astype(BF16) for part in sends[1:]]
        lag_sum = total[own_rows:].reshape(rows, 2 * fine).astype(BF16)
    weight_terms = around(sends)
    pairs = []
    for i in range(data):
        for j in range(seq):
            pairs.append((i * seq + j, (per_ctx * j + i % per_ctx) * seq + i // per_ctx))
    lag_own = lax.ppermute(lag_sum, ("dp", "ctx"), pairs)

    def unpack_kernel(*refs):
        parts, (gate_ref, value_ref) = refs[:seq], refs[seq:]
        for step, part in enumerate(parts):
            put_columns(gate_ref, behind(step), cols, seq, part[0])
            put_columns(value_ref, behind(step), cols, seq, part[1])

    with jax.named_scope("unpack_results"):
        grad_gate_one, grad_value = call(unpack_kernel, [wide_bf16, wide_bf16], result_parts)

    if fast:

        def final_kernel(lag_ref, *refs):
            arrived, (filter_ref, weight_ref) = refs[:seq], refs[seq:]
            lag = lag_ref[...].astype(F32) * (1.0 / data)
            filter_ref[0] = lag[:, :fine]
            filter_ref[1] = pltpu.roll(lag, fine, axis=1)[:, :fine]
            total = arrived[0][...]
            for part in arrived[1:]:
                total = total + part[...].astype(F32)
            weight_ref[...] = total * (1.0 / data)

        with jax.named_scope("means"):
            filter_grad, weight_grad = call(
                final_kernel,
                [((2, rows, fine), F32), ((own_rows, cols), F32)],
                (lag_own, *weight_terms),
            )
    else:
        filter_grad = lag_own.reshape(rows, 2, fine).transpose(1, 0, 2).astype(F32) / data
        weight_grad = sum(part.astype(F32) for part in weight_terms) / data
    return (
        mixed[None],
        grad_value[None],
        grad_gate_one[None],
        grad_gate_two[None],
        filter_grad,
        weight_grad,
    )


def solution(mesh):
    stream = P("dp", "ctx", None)
    return jax.shard_map(
        on_device,
        mesh=mesh,
        in_specs=(stream, stream, stream, P(), P(), stream),
        out_specs=(stream, stream, stream, stream, P(None, "ctx", "dp"), P("dp", "ctx")),
        check_vma=False,
    )
```

```python
import functools
import math

import jax
import jax.numpy as jnp
import ml_dtypes
import numpy as np
from jax import lax
from jax.experimental import pallas as pl
from jax.experimental.pallas import tpu as pltpu
from jax.sharding import PartitionSpec as P

F32 = jnp.float32
BF16 = jnp.bfloat16


def split_table(table):
    high = table.astype(ml_dtypes.bfloat16)
    low = (table - high.astype(np.float64)).astype(ml_dtypes.bfloat16)
    return jnp.asarray(high), jnp.asarray(low)


@functools.lru_cache(maxsize=None)
def table_values(block):
    period = 2 * block
    bins = np.arange(block)
    radians = (bins[:, None] * bins[None, :] % period) * (2.0 * math.pi / period)
    cosines, sines = np.cos(radians), -np.sin(radians)
    sines[0] = np.where(bins % 2 == 0, 1.0, -1.0)
    forward = np.concatenate([cosines, sines], axis=0)
    weights = np.full((period,), 2.0 / period)
    weights[0] = weights[block] = 1.0 / period
    return forward, forward.T * weights[None, :]


def mxu(left, right):
    return jnp.dot(left, right, preferred_element_type=F32)


def beside(stream, block):
    return jnp.concatenate(
        [stream[i : i + block] for i in range(0, stream.shape[0], block)], axis=1
    )


def to_spectra(high, low, stream):
    blocks = beside(stream, high.shape[1])
    return mxu(high[...], blocks) + mxu(low[...], blocks)


def from_spectra(high, spectra):
    return mxu(high[...], spectra.astype(BF16))


def parity(shape):
    row = lax.broadcasted_iota(jnp.int32, shape, 0)
    return jnp.where(row % 2 == 0, 1.0, -1.0)


def with_previous(spectra, cols):
    sign = parity((spectra.shape[0], cols))
    out = [spectra[:, :cols]]
    for i in range(cols, spectra.shape[1], cols):
        out.append(spectra[:, i : i + cols] + sign * spectra[:, i - cols : i])
    return jnp.concatenate(out, axis=1)


def sum_of_products(terms, conj_left):
    half = terms[0][0].shape[0] // 2
    border = lax.broadcasted_iota(jnp.int32, (half, terms[0][0].shape[1]), 0) == 0
    straight = cross = imag = 0.0
    for left, right in terms:
        left_re, left_im, right_re, right_im = left[:half], left[half:], right[:half], right[half:]
        straight += left_re * right_re
        cross += left_im * right_im
        if conj_left:
            imag += left_re * right_im - left_im * right_re
        else:
            imag += left_re * right_im + left_im * right_re
    inner = jnp.where(border, 0.0, cross)
    real = straight + inner if conj_left else straight - inner
    return jnp.concatenate([real, jnp.where(border, cross, imag)], axis=0)


def columns(ref, index, cols):
    return ref[:, index * cols : (index + 1) * cols]


def causal_product(filt, spectra, cols):
    count = spectra.shape[1] // cols
    out = []
    for i in range(count):
        terms = [(columns(filt, i - a, cols), columns(spectra, a, cols)) for a in range(i + 1)]
        out.append(sum_of_products(terms, False))
    return jnp.concatenate(out, axis=1)


def anti_product(left, spectra, cols):
    count = spectra.shape[1] // cols
    out = []
    for i in range(count):
        terms = [
            (columns(left, a - i, cols), columns(spectra, a, cols)) for a in range(i, count)
        ]
        out.append(sum_of_products(terms, True))
    return jnp.concatenate(out, axis=1)


def pick_columns(ref, index, width, count):
    if width % 128 == 0:
        return ref[:, pl.ds(pl.multiple_of(index * width, width), width)]
    whole = ref[...]
    out = whole[:, :width]
    for other in range(1, count):
        out = jnp.where(index == other, whole[:, other * width : (other + 1) * width], out)
    return out


def put_columns(ref, index, width, count, block):
    if width % 128 == 0:
        ref[:, pl.ds(pl.multiple_of(index * width, width), width)] = block
        return
    for other in range(count):

        @pl.when(index == other)
        def _():
            ref[:, other * width : (other + 1) * width] = block


def pick_rows(ref, index, rows):
    return ref[pl.ds(pl.multiple_of(index * rows, rows), rows), :]


def put_rows(ref, index, rows, block):
    ref[pl.ds(pl.multiple_of(index * rows, rows), rows), :] = block


def call(kernel, outs, args, scratch=(), flops=0, limit=16, in_hbm=False):
    vmem = pl.BlockSpec(memory_space=pltpu.VMEM)
    source = pl.BlockSpec(memory_space=pltpu.HBM) if in_hbm else vmem
    total = sum(math.prod(a.shape) * a.dtype.itemsize for a in args)
    return pl.pallas_call(
        kernel,
        out_shape=[jax.ShapeDtypeStruct(shape, dtype) for shape, dtype in outs],
        in_specs=[source] * len(args),
        out_specs=[vmem] * len(outs),
        scratch_shapes=list(scratch),
        compiler_params=pltpu.CompilerParams(vmem_limit_bytes=limit * 2**20),
        cost_estimate=pl.CostEstimate(flops=flops, bytes_accessed=total, transcendentals=0),
    )(*args)


def on_device(value, gate_one, gate_two, filters, out_weight, grad_out):
    rows, width = value.shape[1:]
    seq = lax.axis_size("ctx")
    data = lax.axis_size("dp")
    length = rows * seq
    cols = width // seq
    block = math.gcd(length, 256)
    per_ctx = data // seq
    fine = cols // per_ctx
    chips = data // 2
    own_rows = width // data
    fast = cols == 128 and per_ctx == 2 and chips == seq and seq & (seq - 1) == 0
    limit = 16 if length <= 512 else 48
    forward, inverse = table_values(block)
    (fwd_high, fwd_low), (inv_high, _) = split_table(forward), split_table(inverse)
    spectra_shape = (2 * block, length // block * cols)
    table_flops = 4 * block * length * cols

    def ahead(step):
        return lax.rem(lax.axis_index("ctx") + step, seq)

    def behind(step):
        return lax.rem(lax.axis_index("ctx") + seq - step, seq)

    def held(place):
        return place ^ lax.div(lax.axis_index("dp"), 2) if fast else place

    def around(blocks):
        out = [blocks[0]]
        for step in range(1, seq):
            pairs = [(i, (i + step) % seq) for i in range(seq)]
            out.append(lax.ppermute(blocks[step], "ctx", pairs))
        return out

    def load_kernel(*refs):
        value_ref, gate_ref, cot_arg, weight_arg, gate_arg = refs[:5]
        outs, refs = refs[5 : 5 + seq], refs[5 + seq :]
        cot_ref, weight_ref, gate_two_ref, grad_ref, second, whole, sems = refs
        started = [
            (cot_arg.at[0], cot_ref),
            (weight_arg, weight_ref),
            (gate_arg.at[0], gate_two_ref),
        ]
        if cols % 128 == 0:
            for step, out in enumerate(outs):
                start = pl.multiple_of(held(ahead(step)) * cols, cols)
                started.append((value_ref.at[0, :, pl.ds(start, cols)], out.at[0]))
                started.append((gate_ref.at[0, :, pl.ds(start, cols)], out.at[1]))
        else:
            started.append((value_ref.at[0], whole.at[0]))
            started.append((gate_ref.at[0], whole.at[1]))
        started = [
            pltpu.make_async_copy(source, target, sems.at[index])
            for index, (source, target) in enumerate(started)
        ]
        for copy in started:
            copy.start()
        for copy in started[:3]:
            copy.wait()
        grad = lax.dot_general(
            cot_ref[...], weight_ref[...], (((1,), (1,)), ((), ())), preferred_element_type=F32
        )
        grad_ref[...] = grad
        second[...] = grad * gate_two_ref[...].astype(F32)
        for step, out in enumerate(outs):
            out[2] = pick_columns(second, held(ahead(step)), cols, seq).astype(BF16)
        for copy in started[3:]:
            copy.wait()
        if cols % 128 != 0:
            for step, out in enumerate(outs):
                for index in range(2):
                    out[index] = pick_columns(whole.at[index], held(ahead(step)), cols, seq)

    triple, pair = [((count, rows, cols), BF16) for count in (3, 2)]
    single = ((rows, cols), BF16)
    wide_bf16, wide_f32 = ((rows, width), BF16), ((rows, width), F32)
    with jax.named_scope("load"):
        *sends, cotangent, weight, gate, grad_gated = call(
            load_kernel,
            [triple] * seq + [wide_bf16, ((width, width), BF16), wide_bf16, wide_f32],
            (value, gate_one, grad_out, out_weight, gate_two),
            scratch=[
                pltpu.VMEM((rows, width), F32),
                pltpu.VMEM((2, rows, width), BF16),
                pltpu.SemaphoreType.DMA((2 * seq + 3,)),
            ],
            flops=2 * rows * width * width,
            in_hbm=True,
        )
    parts_in = around(sends)

    def filter_kernel(filters_ref, high, low, out):
        for index in range(2):
            out[index] = with_previous(to_spectra(high, low, filters_ref[index]), cols)

    with jax.named_scope("filter_spectra"):
        own_filters = lax.dynamic_slice_in_dim(filters, held(lax.axis_index("ctx")) * cols, cols, 2)
        (filter_spectra,) = call(
            filter_kernel,
            [((2, *spectra_shape), F32)],
            (own_filters, fwd_high, fwd_low),
            flops=4 * table_flops,
            limit=limit,
        )

    def forward_kernel(*refs):
        parts, refs = refs[:seq], refs[seq:]
        filt, high, low, back, first_ref, value_spec, mixed_spec = refs[:7]
        outs, (stream, second) = refs[7:-2], refs[-2:]
        for step, part in enumerate(parts):
            put_rows(stream, behind(step), rows, part[0])
        spectra = to_spectra(high, low, stream[...])
        value_spec[...] = with_previous(spectra, cols)
        conv = from_spectra(back, causal_product(filt[0], spectra, cols))
        for i in range(length // block):
            first_ref[i * block : (i + 1) * block] = columns(conv, i, cols)
        for step, part in enumerate(parts):
            gated = part[1].astype(F32) * pick_rows(first_ref, behind(step), rows)
            put_rows(stream, behind(step), rows, gated.astype(BF16))
        spectra = to_spectra(high, low, stream[...])
        mixed_spec[...] = with_previous(spectra, cols)
        conv = from_spectra(back, causal_product(filt[1], spectra, cols))
        for i in range(length // block):
            second[i * block : (i + 1) * block] = columns(conv, i, cols)
        for step, out in enumerate(outs):
            out[...] = pick_rows(second, ahead(step), rows).astype(BF16)

    with jax.named_scope("forward_convolutions"):
        first_conv, value_spectra, mixed_spectra, *sends = call(
            forward_kernel,
            [((length, cols), F32), (spectra_shape, F32), (spectra_shape, F32)] + [single] * seq,
            (*parts_in, filter_spectra, fwd_high, fwd_low, inv_high),
            scratch=[pltpu.VMEM((length, cols), BF16), pltpu.VMEM((length, cols), F32)],
            flops=6 * table_flops,
            limit=limit,
        )
    second_parts = around(sends)

    def backward_kernel(*refs):
        parts, refs = refs[:seq], refs[seq:]
        filt, first_ref, value_spec, mixed_spec, high, low, back = refs[:7]
        lags, gate_grad, value_grad, stream, total = refs[7:]
        count = length // block
        for step, part in enumerate(parts):
            put_rows(stream, behind(step), rows, part[2])

        def both(left, other):
            spectra = to_spectra(high, low, stream[...])
            grads = anti_product(left, spectra, cols)
            terms = anti_product(other, spectra, cols)
            return from_spectra(back, jnp.concatenate([grads, terms], axis=1))

        def put_lags(index, out):
            for i in range(count):
                piece = columns(out, count + i, cols)
                lags[index, i * block : (i + 1) * block] = piece

        out = both(filt[1], mixed_spec[...])
        for i in range(count):
            total[i * block : (i + 1) * block] = columns(out, i, cols)
        put_lags(1, out)
        for step, part in enumerate(parts):
            grad = pick_rows(total, behind(step), rows)
            put_rows(stream, behind(step), rows, (grad * part[1].astype(F32)).astype(BF16))
        gate_grad[...] = (total[...] * first_ref[...]).astype(BF16)
        out = both(filt[0], value_spec[...])
        for i in range(count):
            value_grad[i * block : (i + 1) * block] = columns(out, i, cols).astype(BF16)
        put_lags(0, out)

    with jax.named_scope("backward_convolutions"):
        lags, gate_grad, value_grad = call(
            backward_kernel,
            [((2, length, cols), F32), ((length, cols), BF16), ((length, cols), BF16)],
            (
                *parts_in,
                filter_spectra,
                first_conv,
                value_spectra,
                mixed_spectra,
                fwd_high,
                fwd_low,
                inv_high,
            ),
            scratch=[pltpu.VMEM((length, cols), BF16), pltpu.VMEM((length, cols), F32)],
            flops=8 * table_flops,
            limit=limit,
        )

    core = lax.rem(lax.axis_index("dp"), 2)
    chip = lax.div(lax.axis_index("dp"), 2)
    term_shape = (width // 2 + rows, width)

    def gated_kernel(*refs):
        parts, refs = refs[:seq], refs[seq:]
        gate_ref, cot_ref, lags, second_ref, gated_ref = refs[:5]
        for step, part in enumerate(parts):
            put_columns(second_ref, held(behind(step)), cols, seq, part[...])
        gated = (gate_ref[...].astype(F32) * second_ref[...].astype(F32)).astype(BF16)
        gated_ref[...] = gated
        partial = lax.dot_general(
            gated, cot_ref[...], (((0,), (0,)), ((), ())), preferred_element_type=F32
        )
        if not fast:
            refs[5][...] = partial
            return
        kept, given, whole, packed = refs[5:]
        whole[...] = partial
        lower = lax.broadcasted_iota(jnp.int32, (length, cols), 1) < fine
        packed[0] = jnp.where(lower, lags[0], pltpu.roll(lags[1], fine, axis=1))
        packed[1] = jnp.where(lower, pltpu.roll(lags[0], fine, axis=1), lags[1])
        own_core = lax.rem(lax.axis_index("dp"), 2)
        for out, which in ((kept, own_core), (given, 1 - own_core)):
            for index in range(chips):
                start = pl.multiple_of((2 * index + which) * own_rows, own_rows)
                piece = whole[pl.ds(start, own_rows), :]
                out[index * own_rows : (index + 1) * own_rows] = piece.astype(out.dtype)
            for index in range(seq):
                piece = packed[which, index * rows : (index + 1) * rows]
                out[width // 2 :, index * cols : (index + 1) * cols] = piece.astype(out.dtype)

    with jax.named_scope("weight_partial"):
        second_conv, gated, *terms = call(
            gated_kernel,
            [wide_bf16, wide_bf16]
            + ([(term_shape, F32), (term_shape, BF16)] if fast else [((width, width), F32)]),
            (*second_parts, gate, cotangent, lags),
            scratch=[pltpu.VMEM((width, width), F32), pltpu.VMEM((2, length, cols), F32)]
            if fast
            else [],
            flops=2 * rows * width * width,
            limit=limit,
        )

    if not fast:
        lag_terms = lags.reshape(2, seq, rows, per_ctx, fine).transpose(1, 3, 2, 0, 4)
        lag_rows = rows * 2 * fine // width
        terms = jnp.concatenate(
            [
                terms[0].reshape(data, own_rows, width),
                lag_terms.reshape(data, lag_rows, width),
            ],
            axis=1,
        )
        by_core = terms.reshape(chips, 2, *terms.shape[1:])
        kept = lax.dynamic_index_in_dim(by_core, core, 1, keepdims=False)
        given = lax.dynamic_index_in_dim(by_core, 1 - core, 1, keepdims=False).astype(BF16)
        given, kept = (a.reshape(-1, width) for a in (given, kept))
    else:
        kept, given = terms
        lag_rows = 0
    taken = lax.ppermute(given, "dp", [(i, i ^ 1) for i in range(data)])
    term_rows = own_rows + lag_rows

    def chip_kernel(kept_ref, taken_ref, own, *outs):
        place = lax.div(lax.axis_index("dp"), 2)

        def summed(index):
            start = pl.multiple_of(index * term_rows, term_rows)
            taken = taken_ref[pl.ds(start, term_rows), :]
            return kept_ref[pl.ds(start, term_rows), :] + taken.astype(F32)

        own[...] = summed(place)
        for step in range(1, chips):
            outs[step - 1][...] = summed(place ^ step).astype(BF16)
        if fast:
            outs[-1][...] = (kept_ref[width // 2 :] + taken_ref[width // 2 :].astype(F32)).astype(
                BF16
            )

    term = (term_rows, width)
    with jax.named_scope("core_sum"):
        own_term, *sends = call(
            chip_kernel,
            [(term, F32)] + [(term, BF16)] * (chips - 1) + [((rows, width), BF16)] * fast,
            (kept, taken),
            limit=limit,
        )
    chip_terms = []
    for step in range(1, chips):
        pairs = [(i, i ^ (2 * step)) for i in range(data)]
        chip_terms.append(lax.ppermute(sends[step - 1], "dp", pairs))
    if fast:
        pairs = [(i * seq + j, (i ^ (2 * j)) * seq + j) for i in range(data) for j in range(seq)]
        lag_term = lax.ppermute(sends[-1], ("dp", "ctx"), pairs)

    def mixed_kernel(*refs):
        gated_ref, weight_ref, grad_ref, second_ref, gate_grad, value_grad, _ = refs[:7]
        mixed_ref, gate_ref, outs = refs[7], refs[8], refs[9:]
        mixed_ref[...] = mxu(gated_ref[...], weight_ref[...]).astype(BF16)
        gate_ref[...] = (grad_ref[...] * second_ref[...].astype(F32)).astype(BF16)
        for step, out in enumerate(outs):
            out[0] = pick_rows(gate_grad, ahead(step), rows)
            out[1] = pick_rows(value_grad, ahead(step), rows)

    with jax.named_scope("mixed"):
        mixed, grad_gate_two, *sends = call(
            mixed_kernel,
            [wide_bf16, wide_bf16] + [pair] * seq,
            (gated, weight, grad_gated, second_conv, gate_grad, value_grad, own_term),
            flops=2 * rows * width * width,
            limit=limit,
        )
    result_parts = around(sends)

    if fast:

        def place_kernel(own, lag, *refs):
            arrived, outs, total = refs[: chips - 1], refs[chips - 1 : -1], refs[-1]
            summed = own[...]
            for part in arrived:
                summed = summed + part[...].astype(F32)
            total[...] = summed
            for step, out in enumerate(outs):
                out[:own_rows] = pick_columns(total, ahead(step), cols, seq).astype(out.dtype)
                out[own_rows:] = pick_columns(lag, ahead(step), cols, seq).astype(out.dtype)

        small = (own_rows + rows, cols)
        with jax.named_scope("chip_sum"):
            sends = call(
                place_kernel,
                [(small, F32)] + [(small, BF16)] * (seq - 1),
                (own_term, lag_term, *chip_terms),
                scratch=[pltpu.VMEM((own_rows, width), F32)],
            )
    else:
        total = own_term
        for part in chip_terms:
            total = total + part.astype(F32)
        weight_blocks = total[:own_rows].reshape(own_rows, seq, cols)
        sends = [
            lax.dynamic_index_in_dim(weight_blocks, ahead(step), 1, keepdims=False)
            for step in range(seq)
        ]
        sends = sends[:1] + [part.astype(BF16) for part in sends[1:]]
        lag_sum = total[own_rows:].reshape(rows, 2 * fine).astype(BF16)
        pairs = []
        for i in range(data):
            for j in range(seq):
                pairs.append((i * seq + j, (per_ctx * j + i % per_ctx) * seq + i // per_ctx))
        lag_own = lax.ppermute(lag_sum, ("dp", "ctx"), pairs)
    last_terms = around(sends)

    def unpack_kernel(*refs):
        parts, (gate_ref, value_ref) = refs[:seq], refs[seq:]
        for step, part in enumerate(parts):
            put_columns(gate_ref, held(behind(step)), cols, seq, part[0])
            put_columns(value_ref, held(behind(step)), cols, seq, part[1])

    with jax.named_scope("unpack_results"):
        grad_gate_one, grad_value = call(unpack_kernel, [wide_bf16, wide_bf16], result_parts)

    if fast:

        def final_kernel(*refs):
            arrived, (filter_ref, weight_ref) = refs[:seq], refs[seq:]
            total = arrived[0][...]
            for part in arrived[1:]:
                total = total + part[...].astype(F32)
            total = total * (1.0 / data)
            weight_ref[...] = total[:own_rows]
            turned = total[own_rows:].T
            filter_ref[0] = turned[:fine]
            filter_ref[1] = turned[fine:]

        with jax.named_scope("means"):
            filter_grad, weight_grad = call(
                final_kernel, [((2, fine, rows), F32), ((own_rows, cols), F32)], last_terms
            )
        filter_grad = jnp.swapaxes(filter_grad, 1, 2)
    else:
        filter_grad = lag_own.reshape(rows, 2, fine).transpose(1, 0, 2).astype(F32) / data
        weight_grad = sum(part.astype(F32) for part in last_terms) / data
    return (
        mixed[None],
        grad_value[None],
        grad_gate_one[None],
        grad_gate_two[None],
        filter_grad,
        weight_grad,
    )


def solution(mesh):
    stream = P("dp", "ctx", None)
    return jax.shard_map(
        on_device,
        mesh=mesh,
        in_specs=(stream, stream, stream, P(), P(), stream),
        out_specs=(stream, stream, stream, stream, P(None, "ctx", "dp"), P("dp", "ctx")),
        check_vma=False,
    )
```

```python
import functools
import math

import jax
import jax.numpy as jnp
import ml_dtypes
import numpy as np
from jax import lax
from jax.experimental import pallas as pl
from jax.experimental.pallas import tpu as pltpu
from jax.sharding import PartitionSpec as P

F32 = jnp.float32
BF16 = jnp.bfloat16


def split_table(table):
    high = table.astype(ml_dtypes.bfloat16)
    low = (table - high.astype(np.float64)).astype(ml_dtypes.bfloat16)
    return jnp.asarray(high), jnp.asarray(low)


@functools.lru_cache(maxsize=None)
def table_values(block):
    period = 2 * block
    bins = np.arange(block)
    radians = (bins[:, None] * bins[None, :] % period) * (2.0 * math.pi / period)
    cosines, sines = np.cos(radians), -np.sin(radians)
    sines[0] = np.where(bins % 2 == 0, 1.0, -1.0)
    forward = np.concatenate([cosines, sines], axis=0)
    weights = np.full((period,), 2.0 / period)
    weights[0] = weights[block] = 1.0 / period
    return forward, forward.T * weights[None, :]


def mxu(left, right):
    return jnp.dot(left, right, preferred_element_type=F32)


def beside(stream, block):
    return jnp.concatenate(
        [stream[i : i + block] for i in range(0, stream.shape[0], block)], axis=1
    )


def to_spectra(high, low, stream):
    blocks = beside(stream, high.shape[1])
    return mxu(high[...], blocks) + mxu(low[...], blocks)


def from_spectra(high, spectra):
    return mxu(high[...], spectra.astype(BF16))


def parity(shape):
    row = lax.broadcasted_iota(jnp.int32, shape, 0)
    return jnp.where(row % 2 == 0, 1.0, -1.0)


def with_previous(spectra, cols):
    sign = parity((spectra.shape[0], cols))
    out = [spectra[:, :cols]]
    for i in range(cols, spectra.shape[1], cols):
        out.append(spectra[:, i : i + cols] + sign * spectra[:, i - cols : i])
    return jnp.concatenate(out, axis=1)


def sum_of_products(terms, conj_left):
    half = terms[0][0].shape[0] // 2
    border = lax.broadcasted_iota(jnp.int32, (half, terms[0][0].shape[1]), 0) == 0
    straight = cross = imag = 0.0
    for left, right in terms:
        left_re, left_im, right_re, right_im = left[:half], left[half:], right[:half], right[half:]
        straight += left_re * right_re
        cross += left_im * right_im
        if conj_left:
            imag += left_re * right_im - left_im * right_re
        else:
            imag += left_re * right_im + left_im * right_re
    inner = jnp.where(border, 0.0, cross)
    real = straight + inner if conj_left else straight - inner
    return jnp.concatenate([real, jnp.where(border, cross, imag)], axis=0)


def columns(ref, index, cols):
    return ref[:, index * cols : (index + 1) * cols]


def causal_product(filt, spectra, cols):
    count = spectra.shape[1] // cols
    out = []
    for i in range(count):
        terms = [(columns(filt, i - a, cols), columns(spectra, a, cols)) for a in range(i + 1)]
        out.append(sum_of_products(terms, False))
    return jnp.concatenate(out, axis=1)


def anti_product(left, spectra, cols):
    count = spectra.shape[1] // cols
    out = []
    for i in range(count):
        terms = [
            (columns(left, a - i, cols), columns(spectra, a, cols)) for a in range(i, count)
        ]
        out.append(sum_of_products(terms, True))
    return jnp.concatenate(out, axis=1)


def pick_columns(ref, index, width, count):
    if width % 128 == 0:
        return ref[:, pl.ds(pl.multiple_of(index * width, width), width)]
    whole = ref[...]
    out = whole[:, :width]
    for other in range(1, count):
        out = jnp.where(index == other, whole[:, other * width : (other + 1) * width], out)
    return out


def put_columns(ref, index, width, count, block):
    if width % 128 == 0:
        ref[:, pl.ds(pl.multiple_of(index * width, width), width)] = block
        return
    for other in range(count):

        @pl.when(index == other)
        def _():
            ref[:, other * width : (other + 1) * width] = block


def pick_rows(ref, index, rows):
    return ref[pl.ds(pl.multiple_of(index * rows, rows), rows), :]


def put_rows(ref, index, rows, block):
    ref[pl.ds(pl.multiple_of(index * rows, rows), rows), :] = block


def call(kernel, outs, args, scratch=(), flops=0, limit=16, in_hbm=False):
    vmem = pl.BlockSpec(memory_space=pltpu.VMEM)
    source = pl.BlockSpec(memory_space=pltpu.HBM) if in_hbm else vmem
    total = sum(math.prod(a.shape) * a.dtype.itemsize for a in args)
    return pl.pallas_call(
        kernel,
        out_shape=[jax.ShapeDtypeStruct(shape, dtype) for shape, dtype in outs],
        in_specs=[source] * len(args),
        out_specs=[vmem] * len(outs),
        scratch_shapes=list(scratch),
        compiler_params=pltpu.CompilerParams(vmem_limit_bytes=int(limit * 2**20)),
        cost_estimate=pl.CostEstimate(flops=flops, bytes_accessed=total, transcendentals=0),
    )(*args)


def on_device(value, gate_one, gate_two, filters, out_weight, grad_out):
    rows, width = value.shape[1:]
    seq = lax.axis_size("ctx")
    data = lax.axis_size("dp")
    length = rows * seq
    cols = width // seq
    block = math.gcd(length, 256)
    per_ctx = data // seq
    fine = cols // per_ctx
    chips = data // 2
    own_rows = width // data
    fast = cols == 128 and per_ctx == 2 and chips == seq == 4
    limit = 16 if length <= 512 else 48
    load_limit = 53.5
    forward, inverse = table_values(block)
    (fwd_high, fwd_low), (inv_high, _) = split_table(forward), split_table(inverse)
    spectra_shape = (2 * block, length // block * cols)
    table_flops = 4 * block * length * cols

    def ahead(step):
        return lax.rem(lax.axis_index("ctx") + step, seq)

    def behind(step):
        return lax.rem(lax.axis_index("ctx") + seq - step, seq)

    def held(place):
        return place ^ lax.div(lax.axis_index("dp"), 2) if fast else place

    def around(blocks):
        out = [blocks[0]]
        for step in range(1, seq):
            pairs = [(i, (i + step) % seq) for i in range(seq)]
            out.append(lax.ppermute(blocks[step], "ctx", pairs))
        return out

    def grad_gated(cot_ref, weight_ref):
        return lax.dot_general(
            cot_ref[...], weight_ref[...], (((1,), (1,)), ((), ())), preferred_element_type=F32
        )

    def load_kernel(*refs):
        value_ref, gate_ref, cot_arg, weight_arg, gate_arg = refs[:5]
        outs, refs = refs[5 : 5 + seq], refs[5 + seq :]
        cot_ref, weight_ref, gate_two_ref, second, whole, sems = refs
        started = [
            (cot_arg.at[0], cot_ref),
            (weight_arg, weight_ref),
            (gate_arg.at[0], gate_two_ref),
        ]
        if cols % 128 == 0:
            for step, out in enumerate(outs):
                start = pl.multiple_of(held(ahead(step)) * cols, cols)
                started.append((value_ref.at[0, :, pl.ds(start, cols)], out.at[0]))
                started.append((gate_ref.at[0, :, pl.ds(start, cols)], out.at[1]))
        else:
            started.append((value_ref.at[0], whole.at[0]))
            started.append((gate_ref.at[0], whole.at[1]))
        started = [
            pltpu.make_async_copy(source, target, sems.at[index])
            for index, (source, target) in enumerate(started)
        ]
        for copy in started:
            copy.start()
        for copy in started[:3]:
            copy.wait()
        second[...] = grad_gated(cot_ref, weight_ref) * gate_two_ref[...].astype(F32)
        for step, out in enumerate(outs):
            out[2] = pick_columns(second, held(ahead(step)), cols, seq).astype(BF16)
        for copy in started[3:]:
            copy.wait()
        if cols % 128 != 0:
            for step, out in enumerate(outs):
                for index in range(2):
                    out[index] = pick_columns(whole.at[index], held(ahead(step)), cols, seq)

    triple, pair = [((count, rows, cols), BF16) for count in (3, 2)]
    single = ((rows, cols), BF16)
    wide_bf16 = ((rows, width), BF16)
    with jax.named_scope("load"):
        sends = call(
            load_kernel,
            [triple] * seq,
            (value, gate_one, grad_out, out_weight, gate_two),
            scratch=[
                pltpu.VMEM((rows, width), BF16),
                pltpu.VMEM((width, width), BF16),
                pltpu.VMEM((rows, width), BF16),
                pltpu.VMEM((rows, width), F32),
                pltpu.VMEM((2, rows, width), BF16),
                pltpu.SemaphoreType.DMA((2 * seq + 3,)),
            ],
            flops=2 * rows * width * width,
            in_hbm=True,
            limit=load_limit,
        )
    parts_in = around(sends)

    def filter_kernel(filters_ref, high, low, out):
        for index in range(2):
            out[index] = with_previous(to_spectra(high, low, filters_ref[index]), cols)

    with jax.named_scope("filter_spectra"):
        own_filters = lax.dynamic_slice_in_dim(filters, held(lax.axis_index("ctx")) * cols, cols, 2)
        (filter_spectra,) = call(
            filter_kernel,
            [((2, *spectra_shape), F32)],
            (own_filters, fwd_high, fwd_low),
            flops=4 * table_flops,
            limit=limit,
        )

    def forward_kernel(*refs):
        parts, refs = refs[:seq], refs[seq:]
        filt, high, low, back, first_ref, value_spec, mixed_spec = refs[:7]
        outs, (stream, second) = refs[7:-2], refs[-2:]
        for step, part in enumerate(parts):
            put_rows(stream, behind(step), rows, part[0])
        spectra = to_spectra(high, low, stream[...])
        value_spec[...] = with_previous(spectra, cols)
        conv = from_spectra(back, causal_product(filt[0], spectra, cols))
        for i in range(length // block):
            first_ref[i * block : (i + 1) * block] = columns(conv, i, cols)
        for step, part in enumerate(parts):
            gated = part[1].astype(F32) * pick_rows(first_ref, behind(step), rows)
            put_rows(stream, behind(step), rows, gated.astype(BF16))
        spectra = to_spectra(high, low, stream[...])
        mixed_spec[...] = with_previous(spectra, cols)
        conv = from_spectra(back, causal_product(filt[1], spectra, cols))
        for i in range(length // block):
            second[i * block : (i + 1) * block] = columns(conv, i, cols)
        for step, out in enumerate(outs):
            out[...] = pick_rows(second, ahead(step), rows).astype(BF16)

    with jax.named_scope("forward_convolutions"):
        first_conv, value_spectra, mixed_spectra, *sends = call(
            forward_kernel,
            [((length, cols), F32), (spectra_shape, F32), (spectra_shape, F32)] + [single] * seq,
            (*parts_in, filter_spectra, fwd_high, fwd_low, inv_high),
            scratch=[pltpu.VMEM((length, cols), BF16), pltpu.VMEM((length, cols), F32)],
            flops=6 * table_flops,
            limit=limit,
        )
    second_parts = around(sends)

    def put_result(outs, index, total):
        if not fast:
            for step, out in enumerate(outs):
                out[index] = pick_rows(total, ahead(step), rows).astype(BF16)
            return
        for far in range(4):
            place = lax.axis_index("ctx") ^ far
            outs[far % 2][far // 2 * 2 + index] = pick_rows(total, place, rows).astype(BF16)

    def backward_kernel(*refs):
        parts, refs = refs[:seq], refs[seq:]
        filt, first_ref, value_spec, mixed_spec, high, low, back = refs[:7]
        lags, *outs, stream, total = refs[7:]
        count = length // block
        for step, part in enumerate(parts):
            put_rows(stream, behind(step), rows, part[2])

        def both(left, other):
            spectra = to_spectra(high, low, stream[...])
            grads = anti_product(left, spectra, cols)
            terms = anti_product(other, spectra, cols)
            return from_spectra(back, jnp.concatenate([grads, terms], axis=1))

        def put_lags(index, out):
            for i in range(count):
                piece = columns(out, count + i, cols)
                lags[index, i * block : (i + 1) * block] = piece

        out = both(filt[1], mixed_spec[...])
        for i in range(count):
            total[i * block : (i + 1) * block] = columns(out, i, cols)
        put_lags(1, out)
        for step, part in enumerate(parts):
            grad = pick_rows(total, behind(step), rows)
            put_rows(stream, behind(step), rows, (grad * part[1].astype(F32)).astype(BF16))
        total[...] = total[...] * first_ref[...]
        put_result(outs, 0, total)
        out = both(filt[0], value_spec[...])
        for i in range(count):
            total[i * block : (i + 1) * block] = columns(out, i, cols)
        put_result(outs, 1, total)
        put_lags(0, out)

    with jax.named_scope("backward_convolutions"):
        lags, *sends_home = call(
            backward_kernel,
            [((2, length, cols), F32)] + ([((4, rows, cols), BF16)] * 2 if fast else [pair] * seq),
            (
                *parts_in,
                filter_spectra,
                first_conv,
                value_spectra,
                mixed_spectra,
                fwd_high,
                fwd_low,
                inv_high,
            ),
            scratch=[pltpu.VMEM((length, cols), BF16), pltpu.VMEM((length, cols), F32)],
            flops=8 * table_flops,
            limit=limit,
        )

    def home_core(core):
        return jnp.where(lax.axis_index("ctx") == 0, 1 - core, core)

    core = lax.rem(lax.axis_index("dp"), 2)
    chip = lax.div(lax.axis_index("dp"), 2)
    term_shape = (width // 2 + rows, width)

    def gated_kernel(*refs):
        parts, refs = refs[:seq], refs[seq:]
        gate_ref, cot_ref, lags, second_ref, gated_ref = refs[:5]
        for step, part in enumerate(parts):
            put_columns(second_ref, held(behind(step)), cols, seq, part[...])
        gated = (gate_ref[...].astype(F32) * second_ref[...].astype(F32)).astype(BF16)
        gated_ref[...] = gated
        partial = lax.dot_general(
            gated, cot_ref[...], (((0,), (0,)), ((), ())), preferred_element_type=F32
        )
        if not fast:
            refs[5][...] = partial
            return
        kept, given, whole, packed = refs[5:]
        whole[...] = partial
        lower = lax.broadcasted_iota(jnp.int32, (length, cols), 1) < fine
        packed[0] = jnp.where(lower, lags[0], pltpu.roll(lags[1], fine, axis=1))
        packed[1] = jnp.where(lower, pltpu.roll(lags[0], fine, axis=1), lags[1])
        own_core = lax.rem(lax.axis_index("dp"), 2)
        turn = home_core(own_core)
        for out, which, lag_which in ((kept, own_core, turn), (given, 1 - own_core, 1 - turn)):
            for index in range(chips):
                start = pl.multiple_of((2 * index + which) * own_rows, own_rows)
                piece = whole[pl.ds(start, own_rows), :]
                out[index * own_rows : (index + 1) * own_rows] = piece.astype(out.dtype)
            for index in range(seq):
                piece = packed[lag_which, index * rows : (index + 1) * rows]
                out[width // 2 :, index * cols : (index + 1) * cols] = piece.astype(out.dtype)

    with jax.named_scope("weight_partial"):
        second_conv, gated, *terms = call(
            gated_kernel,
            [wide_bf16, wide_bf16]
            + ([(term_shape, F32), (term_shape, BF16)] if fast else [((width, width), F32)]),
            (*second_parts, gate_two[0], grad_out[0], lags),
            scratch=[pltpu.VMEM((width, width), F32), pltpu.VMEM((2, length, cols), F32)]
            if fast
            else [],
            flops=2 * rows * width * width,
            limit=limit,
        )

    if not fast:
        lag_terms = lags.reshape(2, seq, rows, per_ctx, fine).transpose(1, 3, 2, 0, 4)
        lag_rows = rows * 2 * fine // width
        terms = jnp.concatenate(
            [
                terms[0].reshape(data, own_rows, width),
                lag_terms.reshape(data, lag_rows, width),
            ],
            axis=1,
        )
        by_core = terms.reshape(chips, 2, *terms.shape[1:])
        kept = lax.dynamic_index_in_dim(by_core, core, 1, keepdims=False)
        given = lax.dynamic_index_in_dim(by_core, 1 - core, 1, keepdims=False).astype(BF16)
        given, kept = (a.reshape(-1, width) for a in (given, kept))
    else:
        kept, given = terms
        lag_rows = 0
    taken = lax.ppermute(given, "dp", [(i, i ^ 1) for i in range(data)])
    term_rows = own_rows + lag_rows

    def chip_kernel(kept_ref, taken_ref, own, *outs):
        place = lax.div(lax.axis_index("dp"), 2)

        def summed(index):
            start = pl.multiple_of(index * term_rows, term_rows)
            taken = taken_ref[pl.ds(start, term_rows), :]
            return kept_ref[pl.ds(start, term_rows), :] + taken.astype(F32)

        own[...] = summed(place)
        for step in range(1, chips):
            outs[step - 1][...] = summed(place ^ step).astype(BF16)
        if fast:
            outs[-1][...] = (kept_ref[width // 2 :] + taken_ref[width // 2 :].astype(F32)).astype(
                BF16
            )

    term = (term_rows, width)
    with jax.named_scope("core_sum"):
        own_term, *sends = call(
            chip_kernel,
            [(term, F32)] + [(term, BF16)] * (chips - 1) + [((rows, width), BF16)] * fast,
            (kept, taken),
            limit=limit,
        )
    chip_terms = []
    for step in range(1, chips):
        pairs = [(i, i ^ (2 * step)) for i in range(data)]
        chip_terms.append(lax.ppermute(sends[step - 1], "dp", pairs))
    if fast:
        pairs = []
        for i in range(data):
            pairs.append((i * seq, (i ^ 1) * seq))
            pairs += [(i * seq + j, (i ^ (2 * j)) * seq + j) for j in range(1, seq)]
        lag_term = lax.ppermute(sends[-1], ("dp", "ctx"), pairs)

    def across(far):
        return [(i, i ^ far) for i in range(seq)]

    if fast:
        stays, goes = sends_home
        near = lax.ppermute(goes, "ctx", across(1))

        def turn_kernel(stays_ref, near_ref, _, out):
            out[:2] = stays_ref[2:]
            out[2:] = near_ref[2:]

        with jax.named_scope("turn"):
            (goes,) = call(turn_kernel, [((4, rows, cols), BF16)], (stays, near, chip_terms[0]))
        home = [stays, near, lax.ppermute(goes, "ctx", across(2))]
    else:
        home = around(sends_home)

    def mixed_kernel(gated_ref, weight_ref, cot_ref, second_ref, mixed_ref, gate_ref, mark):
        mark[...] = jnp.zeros_like(mark)
        mixed_ref[...] = mxu(gated_ref[...], weight_ref[...]).astype(BF16)
        grad = grad_gated(cot_ref, weight_ref)
        gate_ref[...] = (grad * second_ref[...].astype(F32)).astype(BF16)

    with jax.named_scope("mixed"):
        mixed, grad_gate_two, mark = call(
            mixed_kernel,
            [wide_bf16, wide_bf16, ((8, 128), F32)],
            (gated, out_weight, grad_out[0], second_conv),
            flops=4 * rows * width * width,
            limit=limit,
        )

    if fast:

        def place_kernel(mark, own, lag, *refs):
            arrived, outs, total = refs[: chips - 1], refs[chips - 1 : -1], refs[-1]
            summed = own[...]
            for part in arrived:
                summed = summed + part[...].astype(F32)
            total[...] = summed
            for step, out in enumerate(outs):
                out[:own_rows] = pick_columns(total, ahead(step), cols, seq).astype(out.dtype)
                out[own_rows:] = pick_columns(lag, ahead(step), cols, seq).astype(out.dtype)

        small = (own_rows + rows, cols)
        with jax.named_scope("chip_sum"):
            sends = call(
                place_kernel,
                [(small, F32)] + [(small, BF16)] * (seq - 1),
                (mark, own_term, lag_term, *chip_terms),
                scratch=[pltpu.VMEM((own_rows, width), F32)],
            )
    else:
        total = own_term
        for part in chip_terms:
            total = total + part.astype(F32)
        weight_blocks = total[:own_rows].reshape(own_rows, seq, cols)
        sends = [
            lax.dynamic_index_in_dim(weight_blocks, ahead(step), 1, keepdims=False)
            for step in range(seq)
        ]
        sends = sends[:1] + [part.astype(BF16) for part in sends[1:]]
        lag_sum = total[own_rows:].reshape(rows, 2 * fine).astype(BF16)
        pairs = []
        for i in range(data):
            for j in range(seq):
                pairs.append((i * seq + j, (per_ctx * j + i % per_ctx) * seq + i // per_ctx))
        lag_own = lax.ppermute(lag_sum, ("dp", "ctx"), pairs)
    last_terms = around(sends)

    def unpack_kernel(*refs):
        parts, (gate_ref, value_ref) = refs[:-2], refs[-2:]
        if fast:
            stays_ref, near_ref, far_ref = parts
            blocks = [(stays_ref, 0), (near_ref, 0), (far_ref, 0), (far_ref, 2)]
            blocks = [(lax.axis_index("ctx") ^ far, *block) for far, block in enumerate(blocks)]
        else:
            blocks = [(behind(step), part, 0) for step, part in enumerate(parts)]
        for place, part, first in blocks:
            put_columns(gate_ref, held(place), cols, seq, part[first])
            put_columns(value_ref, held(place), cols, seq, part[first + 1])

    with jax.named_scope("unpack_results"):
        grad_gate_one, grad_value = call(unpack_kernel, [wide_bf16, wide_bf16], home)

    if fast:

        def final_kernel(*refs):
            arrived, (filter_ref, weight_ref) = refs[:seq], refs[seq:]
            total = arrived[0][...]
            for part in arrived[1:]:
                total = total + part[...].astype(F32)
            total = total * (1.0 / data)
            weight_ref[...] = total[:own_rows]
            turned = total[own_rows:].T
            filter_ref[0] = turned[:fine]
            filter_ref[1] = turned[fine:]

        with jax.named_scope("means"):
            filter_grad, weight_grad = call(
                final_kernel, [((2, fine, rows), F32), ((own_rows, cols), F32)], last_terms
            )
        filter_grad = jnp.swapaxes(filter_grad, 1, 2)
    else:
        filter_grad = lag_own.reshape(rows, 2, fine).transpose(1, 0, 2).astype(F32) / data
        weight_grad = sum(part.astype(F32) for part in last_terms) / data
    return (
        mixed[None],
        grad_value[None],
        grad_gate_one[None],
        grad_gate_two[None],
        filter_grad,
        weight_grad,
    )


def solution(mesh):
    stream = P("dp", "ctx", None)
    return jax.shard_map(
        on_device,
        mesh=mesh,
        in_specs=(stream, stream, stream, P(), P(), stream),
        out_specs=(stream, stream, stream, stream, P(None, "ctx", "dp"), P("dp", "ctx")),
        check_vma=False,
    )
```

```python
import functools
import math

import jax
import jax.numpy as jnp
import ml_dtypes
import numpy as np
from jax import lax
from jax.experimental import pallas as pl
from jax.experimental.pallas import tpu as pltpu
from jax.sharding import PartitionSpec as P

F32 = jnp.float32
BF16 = jnp.bfloat16


def split_table(table):
    high = table.astype(ml_dtypes.bfloat16)
    low = (table - high.astype(np.float64)).astype(ml_dtypes.bfloat16)
    return jnp.asarray(high), jnp.asarray(low)


@functools.lru_cache(maxsize=None)
def table_values(block):
    period = 2 * block
    bins = np.arange(block)
    radians = (bins[:, None] * bins[None, :] % period) * (2.0 * math.pi / period)
    cosines, sines = np.cos(radians), -np.sin(radians)
    sines[0] = np.where(bins % 2 == 0, 1.0, -1.0)
    forward = np.concatenate([cosines, sines], axis=0)
    weights = np.full((period,), 2.0 / period)
    weights[0] = weights[block] = 1.0 / period
    return forward, forward.T * weights[None, :]


def mxu(left, right):
    return jnp.dot(left, right, preferred_element_type=F32)


def beside(stream, block):
    return jnp.concatenate(
        [stream[i : i + block] for i in range(0, stream.shape[0], block)], axis=1
    )


def to_spectra(high, low, stream):
    blocks = beside(stream, high.shape[1])
    return mxu(high[...], blocks) + mxu(low[...], blocks)


def from_spectra(high, spectra):
    return mxu(high[...], spectra.astype(BF16))


def parity(shape):
    row = lax.broadcasted_iota(jnp.int32, shape, 0)
    return jnp.where(row % 2 == 0, 1.0, -1.0)


def with_previous(spectra, cols):
    sign = parity((spectra.shape[0], cols))
    out = [spectra[:, :cols]]
    for i in range(cols, spectra.shape[1], cols):
        out.append(spectra[:, i : i + cols] + sign * spectra[:, i - cols : i])
    return jnp.concatenate(out, axis=1)


def sum_of_products(terms, conj_left):
    half = terms[0][0].shape[0] // 2
    border = lax.broadcasted_iota(jnp.int32, (half, terms[0][0].shape[1]), 0) == 0
    straight = cross = imag = 0.0
    for left, right in terms:
        left_re, left_im, right_re, right_im = left[:half], left[half:], right[:half], right[half:]
        straight += left_re * right_re
        cross += left_im * right_im
        if conj_left:
            imag += left_re * right_im - left_im * right_re
        else:
            imag += left_re * right_im + left_im * right_re
    inner = jnp.where(border, 0.0, cross)
    real = straight + inner if conj_left else straight - inner
    return jnp.concatenate([real, jnp.where(border, cross, imag)], axis=0)


def columns(ref, index, cols):
    return ref[:, index * cols : (index + 1) * cols]


def causal_product(filt, spectra, cols):
    count = spectra.shape[1] // cols
    out = []
    for i in range(count):
        terms = [(columns(filt, i - a, cols), columns(spectra, a, cols)) for a in range(i + 1)]
        out.append(sum_of_products(terms, False))
    return jnp.concatenate(out, axis=1)


def anti_product(left, spectra, cols):
    count = spectra.shape[1] // cols
    out = []
    for i in range(count):
        terms = [
            (columns(left, a - i, cols), columns(spectra, a, cols)) for a in range(i, count)
        ]
        out.append(sum_of_products(terms, True))
    return jnp.concatenate(out, axis=1)


def pick_columns(ref, index, width, count):
    if width % 128 == 0:
        return ref[:, pl.ds(pl.multiple_of(index * width, width), width)]
    whole = ref[...]
    out = whole[:, :width]
    for other in range(1, count):
        out = jnp.where(index == other, whole[:, other * width : (other + 1) * width], out)
    return out


def put_columns(ref, index, width, count, block):
    if width % 128 == 0:
        ref[:, pl.ds(pl.multiple_of(index * width, width), width)] = block
        return
    for other in range(count):

        @pl.when(index == other)
        def _():
            ref[:, other * width : (other + 1) * width] = block


def pick_rows(ref, index, rows):
    return ref[pl.ds(pl.multiple_of(index * rows, rows), rows), :]


def put_rows(ref, index, rows, block):
    ref[pl.ds(pl.multiple_of(index * rows, rows), rows), :] = block


def call(kernel, outs, args, scratch=(), flops=0, limit=16, in_hbm=False):
    vmem = pl.BlockSpec(memory_space=pltpu.VMEM)
    source = pl.BlockSpec(memory_space=pltpu.HBM) if in_hbm else vmem
    total = sum(math.prod(a.shape) * a.dtype.itemsize for a in args)
    return pl.pallas_call(
        kernel,
        out_shape=[jax.ShapeDtypeStruct(shape, dtype) for shape, dtype in outs],
        in_specs=[source] * len(args),
        out_specs=[vmem] * len(outs),
        scratch_shapes=list(scratch),
        compiler_params=pltpu.CompilerParams(vmem_limit_bytes=int(limit * 2**20)),
        cost_estimate=pl.CostEstimate(flops=flops, bytes_accessed=total, transcendentals=0),
    )(*args)


def on_device(value, gate_one, gate_two, filters, out_weight, grad_out):
    rows, width = value.shape[1:]
    seq = lax.axis_size("ctx")
    data = lax.axis_size("dp")
    length = rows * seq
    cols = width // seq
    block = math.gcd(length, 256)
    per_ctx = data // seq
    fine = cols // per_ctx
    chips = data // 2
    own_rows = width // data
    fast = cols == 128 and per_ctx == 2 and chips == seq == 4
    limit = 16 if length <= 512 else 48
    load_limit = 53.5
    forward, inverse = table_values(block)
    (fwd_high, fwd_low), (inv_high, _) = split_table(forward), split_table(inverse)
    spectra_shape = (2 * block, length // block * cols)
    table_flops = 4 * block * length * cols

    def ahead(step):
        return lax.rem(lax.axis_index("ctx") + step, seq)

    def behind(step):
        return lax.rem(lax.axis_index("ctx") + seq - step, seq)

    def held(place):
        return place ^ lax.div(lax.axis_index("dp"), 2) if fast else place

    def around(blocks):
        out = [blocks[0]]
        for step in range(1, seq):
            pairs = [(i, (i + step) % seq) for i in range(seq)]
            out.append(lax.ppermute(blocks[step], "ctx", pairs))
        return out

    def grad_gated(cot_ref, weight_ref):
        return lax.dot_general(
            cot_ref[...], weight_ref[...], (((1,), (1,)), ((), ())), preferred_element_type=F32
        )

    def load_kernel(*refs):
        value_ref, gate_ref, cot_arg, weight_arg, gate_arg = refs[:5]
        outs, refs = refs[5 : 5 + seq], refs[5 + seq :]
        cot_ref, weight_ref, gate_two_ref, second, whole, sems = refs
        started = [
            (cot_arg.at[0], cot_ref),
            (weight_arg, weight_ref),
            (gate_arg.at[0], gate_two_ref),
        ]
        if cols % 128 == 0:
            for step, out in enumerate(outs):
                start = pl.multiple_of(held(ahead(step)) * cols, cols)
                started.append((value_ref.at[0, :, pl.ds(start, cols)], out.at[0]))
                started.append((gate_ref.at[0, :, pl.ds(start, cols)], out.at[1]))
        else:
            started.append((value_ref.at[0], whole.at[0]))
            started.append((gate_ref.at[0], whole.at[1]))
        started = [
            pltpu.make_async_copy(source, target, sems.at[index])
            for index, (source, target) in enumerate(started)
        ]
        for copy in started:
            copy.start()
        for copy in started[:3]:
            copy.wait()
        second[...] = grad_gated(cot_ref, weight_ref) * gate_two_ref[...].astype(F32)
        for step, out in enumerate(outs):
            out[2] = pick_columns(second, held(ahead(step)), cols, seq).astype(BF16)
        for copy in started[3:]:
            copy.wait()
        if cols % 128 != 0:
            for step, out in enumerate(outs):
                for index in range(2):
                    out[index] = pick_columns(whole.at[index], held(ahead(step)), cols, seq)

    triple, pair = [((count, rows, cols), BF16) for count in (3, 2)]
    single = ((rows, cols), BF16)
    wide_bf16 = ((rows, width), BF16)
    with jax.named_scope("load"):
        sends = call(
            load_kernel,
            [triple] * seq,
            (value, gate_one, grad_out, out_weight, gate_two),
            scratch=[
                pltpu.VMEM((rows, width), BF16),
                pltpu.VMEM((width, width), BF16),
                pltpu.VMEM((rows, width), BF16),
                pltpu.VMEM((rows, width), F32),
                pltpu.VMEM((2, rows, width), BF16),
                pltpu.SemaphoreType.DMA((2 * seq + 3,)),
            ],
            flops=2 * rows * width * width,
            in_hbm=True,
            limit=load_limit,
        )
    parts_in = around(sends)

    def filter_kernel(filters_ref, high, low, out):
        for index in range(2):
            out[index] = with_previous(to_spectra(high, low, filters_ref[index]), cols)

    with jax.named_scope("filter_spectra"):
        own_filters = lax.dynamic_slice_in_dim(filters, held(lax.axis_index("ctx")) * cols, cols, 2)
        (filter_spectra,) = call(
            filter_kernel,
            [((2, *spectra_shape), F32)],
            (own_filters, fwd_high, fwd_low),
            flops=4 * table_flops,
            limit=limit,
        )

    def forward_kernel(*refs):
        parts, refs = refs[:seq], refs[seq:]
        filt, high, low, back, first_ref, value_spec, mixed_spec = refs[:7]
        outs, (stream, second) = refs[7:-2], refs[-2:]
        for step, part in enumerate(parts):
            put_rows(stream, behind(step), rows, part[0])
        spectra = to_spectra(high, low, stream[...])
        value_spec[...] = with_previous(spectra, cols)
        conv = from_spectra(back, causal_product(filt[0], spectra, cols))
        for i in range(length // block):
            first_ref[i * block : (i + 1) * block] = columns(conv, i, cols)
        for step, part in enumerate(parts):
            gated = part[1].astype(F32) * pick_rows(first_ref, behind(step), rows)
            put_rows(stream, behind(step), rows, gated.astype(BF16))
        spectra = to_spectra(high, low, stream[...])
        mixed_spec[...] = with_previous(spectra, cols)
        conv = from_spectra(back, causal_product(filt[1], spectra, cols))
        for i in range(length // block):
            second[i * block : (i + 1) * block] = columns(conv, i, cols)
        for step, out in enumerate(outs):
            out[...] = pick_rows(second, ahead(step), rows).astype(BF16)

    with jax.named_scope("forward_convolutions"):
        first_conv, value_spectra, mixed_spectra, *sends = call(
            forward_kernel,
            [((length, cols), F32), (spectra_shape, F32), (spectra_shape, F32)] + [single] * seq,
            (*parts_in, filter_spectra, fwd_high, fwd_low, inv_high),
            scratch=[pltpu.VMEM((length, cols), BF16), pltpu.VMEM((length, cols), F32)],
            flops=6 * table_flops,
            limit=limit,
        )
    second_parts = around(sends)

    def put_result(outs, index, total):
        if not fast:
            for step, out in enumerate(outs):
                out[index] = pick_rows(total, ahead(step), rows).astype(BF16)
            return
        for far in range(4):
            place = lax.axis_index("ctx") ^ far
            outs[far // 2][far % 2 * 2 + index] = pick_rows(total, place, rows).astype(BF16)

    def backward_kernel(*refs):
        parts, refs = refs[:seq], refs[seq:]
        filt, first_ref, value_spec, mixed_spec, high, low, back = refs[:7]
        lags, *outs, stream, total = refs[7:]
        count = length // block
        for step, part in enumerate(parts):
            put_rows(stream, behind(step), rows, part[2])

        def both(left, other):
            spectra = to_spectra(high, low, stream[...])
            grads = anti_product(left, spectra, cols)
            terms = anti_product(other, spectra, cols)
            return from_spectra(back, jnp.concatenate([grads, terms], axis=1))

        def put_lags(index, out):
            for i in range(count):
                piece = columns(out, count + i, cols)
                lags[index, i * block : (i + 1) * block] = piece

        out = both(filt[1], mixed_spec[...])
        for i in range(count):
            total[i * block : (i + 1) * block] = columns(out, i, cols)
        put_lags(1, out)
        for step, part in enumerate(parts):
            grad = pick_rows(total, behind(step), rows)
            put_rows(stream, behind(step), rows, (grad * part[1].astype(F32)).astype(BF16))
        total[...] = total[...] * first_ref[...]
        put_result(outs, 0, total)
        out = both(filt[0], value_spec[...])
        for i in range(count):
            total[i * block : (i + 1) * block] = columns(out, i, cols)
        put_result(outs, 1, total)
        put_lags(0, out)

    with jax.named_scope("backward_convolutions"):
        lags, *sends_home = call(
            backward_kernel,
            [((2, length, cols), F32)] + ([((4, rows, cols), BF16)] * 2 if fast else [pair] * seq),
            (
                *parts_in,
                filter_spectra,
                first_conv,
                value_spectra,
                mixed_spectra,
                fwd_high,
                fwd_low,
                inv_high,
            ),
            scratch=[pltpu.VMEM((length, cols), BF16), pltpu.VMEM((length, cols), F32)],
            flops=8 * table_flops,
            limit=limit,
        )

    def home_core(core):
        return jnp.where(lax.axis_index("ctx") == 0, 1 - core, core)

    core = lax.rem(lax.axis_index("dp"), 2)
    chip = lax.div(lax.axis_index("dp"), 2)
    term_shape = (width // 2 + rows, width)

    def gated_kernel(*refs):
        parts, refs = refs[:seq], refs[seq:]
        gate_ref, cot_ref, lags, second_ref, gated_ref = refs[:5]
        for step, part in enumerate(parts):
            put_columns(second_ref, held(behind(step)), cols, seq, part[...])
        gated = (gate_ref[...].astype(F32) * second_ref[...].astype(F32)).astype(BF16)
        gated_ref[...] = gated
        partial = lax.dot_general(
            gated, cot_ref[...], (((0,), (0,)), ((), ())), preferred_element_type=F32
        )
        if not fast:
            refs[5][...] = partial
            return
        kept, given, whole, packed = refs[5:]
        whole[...] = partial
        lower = lax.broadcasted_iota(jnp.int32, (length, cols), 1) < fine
        packed[0] = jnp.where(lower, lags[0], pltpu.roll(lags[1], fine, axis=1))
        packed[1] = jnp.where(lower, pltpu.roll(lags[0], fine, axis=1), lags[1])
        own_core = lax.rem(lax.axis_index("dp"), 2)
        turn = home_core(own_core)
        for out, which, lag_which in ((kept, own_core, turn), (given, 1 - own_core, 1 - turn)):
            for index in range(chips):
                start = pl.multiple_of((2 * index + which) * own_rows, own_rows)
                piece = whole[pl.ds(start, own_rows), :]
                out[index * own_rows : (index + 1) * own_rows] = piece.astype(out.dtype)
            for index in range(seq):
                piece = packed[lag_which, index * rows : (index + 1) * rows]
                out[width // 2 :, index * cols : (index + 1) * cols] = piece.astype(out.dtype)

    with jax.named_scope("weight_partial"):
        second_conv, gated, *terms = call(
            gated_kernel,
            [wide_bf16, wide_bf16]
            + ([(term_shape, F32), (term_shape, BF16)] if fast else [((width, width), F32)]),
            (*second_parts, gate_two[0], grad_out[0], lags),
            scratch=[pltpu.VMEM((width, width), F32), pltpu.VMEM((2, length, cols), F32)]
            if fast
            else [],
            flops=2 * rows * width * width,
            limit=limit,
        )

    if not fast:
        lag_terms = lags.reshape(2, seq, rows, per_ctx, fine).transpose(1, 3, 2, 0, 4)
        lag_rows = rows * 2 * fine // width
        terms = jnp.concatenate(
            [
                terms[0].reshape(data, own_rows, width),
                lag_terms.reshape(data, lag_rows, width),
            ],
            axis=1,
        )
        by_core = terms.reshape(chips, 2, *terms.shape[1:])
        kept = lax.dynamic_index_in_dim(by_core, core, 1, keepdims=False)
        given = lax.dynamic_index_in_dim(by_core, 1 - core, 1, keepdims=False).astype(BF16)
        given, kept = (a.reshape(-1, width) for a in (given, kept))
    else:
        kept, given = terms
        lag_rows = 0
    taken = lax.ppermute(given, "dp", [(i, i ^ 1) for i in range(data)])
    term_rows = own_rows + lag_rows

    def chip_kernel(kept_ref, taken_ref, own, *outs):
        place = lax.div(lax.axis_index("dp"), 2)

        def summed(index):
            start = pl.multiple_of(index * term_rows, term_rows)
            taken = taken_ref[pl.ds(start, term_rows), :]
            return kept_ref[pl.ds(start, term_rows), :] + taken.astype(F32)

        own[...] = summed(place)
        for step in range(1, chips):
            outs[step - 1][...] = summed(place ^ step).astype(BF16)
        if fast:
            outs[-1][...] = (kept_ref[width // 2 :] + taken_ref[width // 2 :].astype(F32)).astype(
                BF16
            )

    term = (term_rows, width)
    with jax.named_scope("core_sum"):
        own_term, *sends = call(
            chip_kernel,
            [(term, F32)] + [(term, BF16)] * (chips - 1) + [((rows, width), BF16)] * fast,
            (kept, taken),
            limit=limit,
        )
    chip_terms = []
    for step in range(1, chips):
        pairs = [(i, i ^ (2 * step)) for i in range(data)]
        chip_terms.append(lax.ppermute(sends[step - 1], "dp", pairs))
    if fast:
        pairs = []
        for i in range(data):
            pairs.append((i * seq, (i ^ 1) * seq))
            pairs += [(i * seq + j, (i ^ (2 * j)) * seq + j) for j in range(1, seq)]
        lag_term = lax.ppermute(sends[-1], ("dp", "ctx"), pairs)

    def mixed_kernel(gated_ref, weight_ref, cot_ref, second_ref, mixed_ref, gate_ref, mark):
        mark[...] = jnp.zeros_like(mark)
        mixed_ref[...] = mxu(gated_ref[...], weight_ref[...]).astype(BF16)
        grad = grad_gated(cot_ref, weight_ref)
        gate_ref[...] = (grad * second_ref[...].astype(F32)).astype(BF16)

    with jax.named_scope("mixed"):
        mixed, grad_gate_two, mark = call(
            mixed_kernel,
            [wide_bf16, wide_bf16, ((8, 128), F32)],
            (gated, out_weight, grad_out[0], second_conv),
            flops=4 * rows * width * width,
            limit=limit,
        )

    def across(far):
        return [(i, i ^ far) for i in range(seq)]

    if fast:
        stays, goes = sends_home
        near = lax.ppermute(goes, "ctx", across(2))

        def turn_kernel(stays_ref, near_ref, *refs):
            refs[-1][:2] = stays_ref[2:]
            refs[-1][2:] = near_ref[2:]

        with jax.named_scope("turn"):
            (goes,) = call(
                turn_kernel, [((4, rows, cols), BF16)], (stays, near, mark, *chip_terms)
            )
        far = lax.ppermute(goes, "ctx", across(1))
    else:
        home = around(sends_home)

    if fast:

        def place_kernel(mark, own, lag, *refs):
            arrived, outs, total = refs[: chips - 1], refs[chips - 1 : -1], refs[-1]
            summed = own[...]
            for part in arrived:
                summed = summed + part[...].astype(F32)
            total[...] = summed
            for step, out in enumerate(outs):
                out[:own_rows] = pick_columns(total, ahead(step), cols, seq).astype(out.dtype)
                out[own_rows:] = pick_columns(lag, ahead(step), cols, seq).astype(out.dtype)

        small = (own_rows + rows, cols)
        with jax.named_scope("chip_sum"):
            sends = call(
                place_kernel,
                [(small, F32)] + [(small, BF16)] * (seq - 1),
                (mark, own_term, lag_term, *chip_terms),
                scratch=[pltpu.VMEM((own_rows, width), F32)],
            )
    else:
        total = own_term
        for part in chip_terms:
            total = total + part.astype(F32)
        weight_blocks = total[:own_rows].reshape(own_rows, seq, cols)
        sends = [
            lax.dynamic_index_in_dim(weight_blocks, ahead(step), 1, keepdims=False)
            for step in range(seq)
        ]
        sends = sends[:1] + [part.astype(BF16) for part in sends[1:]]
        lag_sum = total[own_rows:].reshape(rows, 2 * fine).astype(BF16)
        pairs = []
        for i in range(data):
            for j in range(seq):
                pairs.append((i * seq + j, (per_ctx * j + i % per_ctx) * seq + i // per_ctx))
        lag_own = lax.ppermute(lag_sum, ("dp", "ctx"), pairs)
    last_terms = around(sends)

    def unpack(blocks, gate_ref, value_ref):
        for place, part, first in blocks:
            put_columns(gate_ref, held(place), cols, seq, part[first])
            put_columns(value_ref, held(place), cols, seq, part[first + 1])

    if fast:

        def final_kernel(*refs):
            arrived, (stays_ref, near_ref, far_ref) = refs[:4], refs[4:7]
            filter_ref, weight_ref, gate_ref, value_ref = refs[7:]
            here = lax.axis_index("ctx")
            blocks = [(here, stays_ref, 0), (here ^ 2, near_ref, 0)]
            blocks += [(here ^ 1, far_ref, 0), (here ^ 3, far_ref, 2)]
            unpack(blocks, gate_ref, value_ref)
            total = arrived[0][...]
            for part in arrived[1:]:
                total = total + part[...].astype(F32)
            total = total * (1.0 / data)
            weight_ref[...] = total[:own_rows]
            turned = total[own_rows:].T
            filter_ref[0] = turned[:fine]
            filter_ref[1] = turned[fine:]

        with jax.named_scope("means"):
            filter_grad, weight_grad, grad_gate_one, grad_value = call(
                final_kernel,
                [((2, fine, rows), F32), ((own_rows, cols), F32), wide_bf16, wide_bf16],
                (*last_terms, stays, near, far),
            )
        filter_grad = jnp.swapaxes(filter_grad, 1, 2)
    else:

        def unpack_kernel(*refs):
            unpack([(behind(step), part, 0) for step, part in enumerate(refs[:-2])], *refs[-2:])

        with jax.named_scope("unpack_results"):
            grad_gate_one, grad_value = call(unpack_kernel, [wide_bf16, wide_bf16], home)
        filter_grad = lag_own.reshape(rows, 2, fine).transpose(1, 0, 2).astype(F32) / data
        weight_grad = sum(part.astype(F32) for part in last_terms) / data
    return (
        mixed[None],
        grad_value[None],
        grad_gate_one[None],
        grad_gate_two[None],
        filter_grad,
        weight_grad,
    )


def solution(mesh):
    stream = P("dp", "ctx", None)
    return jax.shard_map(
        on_device,
        mesh=mesh,
        in_specs=(stream, stream, stream, P(), P(), stream),
        out_specs=(stream, stream, stream, stream, P(None, "ctx", "dp"), P("dp", "ctx")),
        check_vma=False,
    )
```

```python
import functools
import math

import jax
import jax.numpy as jnp
import ml_dtypes
import numpy as np
from jax import lax
from jax.experimental import pallas as pl
from jax.experimental.pallas import tpu as pltpu
from jax.sharding import PartitionSpec as P

F32 = jnp.float32
BF16 = jnp.bfloat16


def split_table(table):
    high = table.astype(ml_dtypes.bfloat16)
    low = (table - high.astype(np.float64)).astype(ml_dtypes.bfloat16)
    return jnp.asarray(high), jnp.asarray(low)


@functools.lru_cache(maxsize=None)
def table_values(block):
    period = 2 * block
    bins = np.arange(block)
    radians = (bins[:, None] * bins[None, :] % period) * (2.0 * math.pi / period)
    cosines, sines = np.cos(radians), -np.sin(radians)
    sines[0] = np.where(bins % 2 == 0, 1.0, -1.0)
    forward = np.concatenate([cosines, sines], axis=0)
    weights = np.full((period,), 2.0 / period)
    weights[0] = weights[block] = 1.0 / period
    return forward, forward.T * weights[None, :]


def mxu(left, right):
    return jnp.dot(left, right, preferred_element_type=F32)


def beside(stream, block):
    return jnp.concatenate(
        [stream[i : i + block] for i in range(0, stream.shape[0], block)], axis=1
    )


def to_spectra(high, low, stream):
    blocks = beside(stream, high.shape[1])
    return mxu(high[...], blocks) + mxu(low[...], blocks)


def from_spectra(high, spectra):
    return mxu(high[...], spectra.astype(BF16))


def parity(shape):
    row = lax.broadcasted_iota(jnp.int32, shape, 0)
    return jnp.where(row % 2 == 0, 1.0, -1.0)


def with_previous(spectra, cols):
    sign = parity((spectra.shape[0], cols))
    out = [spectra[:, :cols]]
    for i in range(cols, spectra.shape[1], cols):
        out.append(spectra[:, i : i + cols] + sign * spectra[:, i - cols : i])
    return jnp.concatenate(out, axis=1)


def sum_of_products(terms, conj_left):
    half = terms[0][0].shape[0] // 2
    border = lax.broadcasted_iota(jnp.int32, (half, terms[0][0].shape[1]), 0) == 0
    straight = cross = imag = 0.0
    for left, right in terms:
        left_re, left_im, right_re, right_im = left[:half], left[half:], right[:half], right[half:]
        straight += left_re * right_re
        cross += left_im * right_im
        if conj_left:
            imag += left_re * right_im - left_im * right_re
        else:
            imag += left_re * right_im + left_im * right_re
    inner = jnp.where(border, 0.0, cross)
    real = straight + inner if conj_left else straight - inner
    return jnp.concatenate([real, jnp.where(border, cross, imag)], axis=0)


def columns(ref, index, cols):
    return ref[:, index * cols : (index + 1) * cols]


def causal_product(filt, spectra, cols):
    count = spectra.shape[1] // cols
    out = []
    for i in range(count):
        terms = [(columns(filt, i - a, cols), columns(spectra, a, cols)) for a in range(i + 1)]
        out.append(sum_of_products(terms, False))
    return jnp.concatenate(out, axis=1)


def anti_product(left, spectra, cols):
    count = spectra.shape[1] // cols
    out = []
    for i in range(count):
        terms = [
            (columns(left, a - i, cols), columns(spectra, a, cols)) for a in range(i, count)
        ]
        out.append(sum_of_products(terms, True))
    return jnp.concatenate(out, axis=1)


def pick_columns(ref, index, width, count):
    if width % 128 == 0:
        return ref[:, pl.ds(pl.multiple_of(index * width, width), width)]
    whole = ref[...]
    out = whole[:, :width]
    for other in range(1, count):
        out = jnp.where(index == other, whole[:, other * width : (other + 1) * width], out)
    return out


def put_columns(ref, index, width, count, block):
    if width % 128 == 0:
        ref[:, pl.ds(pl.multiple_of(index * width, width), width)] = block
        return
    for other in range(count):

        @pl.when(index == other)
        def _():
            ref[:, other * width : (other + 1) * width] = block


def pick_rows(ref, index, rows):
    return ref[pl.ds(pl.multiple_of(index * rows, rows), rows), :]


def put_rows(ref, index, rows, block):
    ref[pl.ds(pl.multiple_of(index * rows, rows), rows), :] = block


def call(kernel, outs, args, scratch=(), flops=0, limit=16, in_hbm=False):
    vmem = pl.BlockSpec(memory_space=pltpu.VMEM)
    source = pl.BlockSpec(memory_space=pltpu.HBM) if in_hbm else vmem
    total = sum(math.prod(a.shape) * a.dtype.itemsize for a in args)
    return pl.pallas_call(
        kernel,
        out_shape=[jax.ShapeDtypeStruct(shape, dtype) for shape, dtype in outs],
        in_specs=[source] * len(args),
        out_specs=[vmem] * len(outs),
        scratch_shapes=list(scratch),
        compiler_params=pltpu.CompilerParams(vmem_limit_bytes=int(limit * 2**20)),
        cost_estimate=pl.CostEstimate(flops=flops, bytes_accessed=total, transcendentals=0),
    )(*args)


def on_device(value, gate_one, gate_two, filters, out_weight, grad_out):
    rows, width = value.shape[1:]
    seq = lax.axis_size("ctx")
    data = lax.axis_size("dp")
    length = rows * seq
    cols = width // seq
    block = math.gcd(length, 256)
    per_ctx = data // seq
    fine = cols // per_ctx
    chips = data // 2
    own_rows = width // data
    fast = cols == 128 and per_ctx == 2 and chips == seq == 4
    limit = 16 if length <= 512 else 48
    load_limit = 53.5
    forward, inverse = table_values(block)
    (fwd_high, fwd_low), (inv_high, _) = split_table(forward), split_table(inverse)
    spectra_shape = (2 * block, length // block * cols)
    table_flops = 4 * block * length * cols

    def ahead(step):
        return lax.rem(lax.axis_index("ctx") + step, seq)

    def behind(step):
        return lax.rem(lax.axis_index("ctx") + seq - step, seq)

    def held(place):
        return place ^ lax.div(lax.axis_index("dp"), 2) if fast else place

    def around(blocks):
        out = [blocks[0]]
        for step in range(1, seq):
            pairs = [(i, (i + step) % seq) for i in range(seq)]
            out.append(lax.ppermute(blocks[step], "ctx", pairs))
        return out

    def grad_gated(cot_ref, weight_ref):
        return lax.dot_general(
            cot_ref[...], weight_ref[...], (((1,), (1,)), ((), ())), preferred_element_type=F32
        )

    def load_kernel(*refs):
        value_ref, gate_ref, cot_arg, weight_arg, gate_arg = refs[:5]
        outs, refs = refs[5 : 5 + seq], refs[5 + seq :]
        cot_ref, weight_ref, gate_two_ref, second, whole, sems = refs
        started = [
            (cot_arg.at[0], cot_ref),
            (weight_arg, weight_ref),
            (gate_arg.at[0], gate_two_ref),
        ]
        if cols % 128 == 0:
            for step, out in enumerate(outs):
                start = pl.multiple_of(held(ahead(step)) * cols, cols)
                started.append((value_ref.at[0, :, pl.ds(start, cols)], out.at[0]))
                started.append((gate_ref.at[0, :, pl.ds(start, cols)], out.at[1]))
        else:
            started.append((value_ref.at[0], whole.at[0]))
            started.append((gate_ref.at[0], whole.at[1]))
        started = [
            pltpu.make_async_copy(source, target, sems.at[index])
            for index, (source, target) in enumerate(started)
        ]
        for copy in started:
            copy.start()
        for copy in started[:3]:
            copy.wait()
        second[...] = grad_gated(cot_ref, weight_ref) * gate_two_ref[...].astype(F32)
        for step, out in enumerate(outs):
            out[2] = pick_columns(second, held(ahead(step)), cols, seq).astype(BF16)
        for copy in started[3:]:
            copy.wait()
        if cols % 128 != 0:
            for step, out in enumerate(outs):
                for index in range(2):
                    out[index] = pick_columns(whole.at[index], held(ahead(step)), cols, seq)

    triple = ((3, rows, cols), BF16)
    wide_bf16 = ((rows, width), BF16)
    with jax.named_scope("load"):
        sends = call(
            load_kernel,
            [triple] * seq,
            (value, gate_one, grad_out, out_weight, gate_two),
            scratch=[
                pltpu.VMEM((rows, width), BF16),
                pltpu.VMEM((width, width), BF16),
                pltpu.VMEM((rows, width), BF16),
                pltpu.VMEM((rows, width), F32),
                pltpu.VMEM((2, rows, width), BF16),
                pltpu.SemaphoreType.DMA((2 * seq + 3,)),
            ],
            flops=2 * rows * width * width,
            in_hbm=True,
            limit=load_limit,
        )
    parts_in = around(sends)

    def across(far):
        return [(i, i ^ far) for i in range(seq)]

    def filter_kernel(filters_ref, high, low, cot_ref, gate_ref, out, *beside):
        if fast:
            beside[0][:, :width] = cot_ref[...]
            for index, far in enumerate((1, 3)):
                piece = pick_columns(gate_ref, held(lax.axis_index("ctx") ^ far), cols, seq)
                beside[0][:, width + index * cols : width + (index + 1) * cols] = piece
        for index in range(2):
            out[index] = with_previous(to_spectra(high, low, filters_ref[index]), cols)

    with jax.named_scope("filter_spectra"):
        own_filters = lax.dynamic_slice_in_dim(filters, held(lax.axis_index("ctx")) * cols, cols, 2)
        filter_spectra, *sends = call(
            filter_kernel,
            [((2, *spectra_shape), F32)] + [((rows, width + 2 * cols), BF16)] * fast,
            (own_filters, fwd_high, fwd_low, grad_out[0], gate_two[0]),
            flops=4 * table_flops,
            limit=limit,
        )
    if fast:
        beside_in = lax.ppermute(sends[0], "ctx", across(1))

    def put_result(outs, index, total, arrays):
        if len(outs) == seq:
            for step, out in enumerate(outs):
                out[index] = pick_rows(total, ahead(step), rows).astype(BF16)
            return
        for far in range(4):
            piece = pick_rows(total, lax.axis_index("ctx") ^ far, rows).astype(BF16)
            outs[far // 2][far % 2 * arrays + index] = piece

    def forward_kernel(*refs):
        parts, refs = refs[:seq], refs[seq:]
        filt, high, low, back, first_ref, value_spec, mixed_spec = refs[:7]
        outs, (stream, second) = refs[7:-2], refs[-2:]
        for step, part in enumerate(parts):
            put_rows(stream, behind(step), rows, part[0])
        spectra = to_spectra(high, low, stream[...])
        value_spec[...] = with_previous(spectra, cols)
        conv = from_spectra(back, causal_product(filt[0], spectra, cols))
        for i in range(length // block):
            first_ref[i * block : (i + 1) * block] = columns(conv, i, cols)
        for step, part in enumerate(parts):
            gated = part[1].astype(F32) * pick_rows(first_ref, behind(step), rows)
            put_rows(stream, behind(step), rows, gated.astype(BF16))
        spectra = to_spectra(high, low, stream[...])
        mixed_spec[...] = with_previous(spectra, cols)
        conv = from_spectra(back, causal_product(filt[1], spectra, cols))
        for i in range(length // block):
            second[i * block : (i + 1) * block] = columns(conv, i, cols)
        put_result(outs, 0, second, 1)

    with jax.named_scope("forward_convolutions"):
        first_conv, value_spectra, mixed_spectra, *sends = call(
            forward_kernel,
            [((length, cols), F32), (spectra_shape, F32), (spectra_shape, F32)]
            + ([((2, rows, cols), BF16)] * 2 if fast else [((1, rows, cols), BF16)] * seq),
            (*parts_in, filter_spectra, fwd_high, fwd_low, inv_high),
            scratch=[pltpu.VMEM((length, cols), BF16), pltpu.VMEM((length, cols), F32)],
            flops=6 * table_flops,
            limit=limit,
        )
    if fast:
        second_stays, goes = sends
        second_near = lax.ppermute(goes, "ctx", across(2))
    else:
        second_parts = around(sends)

    def backward_kernel(*refs):
        parts, refs = refs[:seq], refs[seq:]
        filt, first_ref, value_spec, mixed_spec, high, low, back = refs[:7]
        lags, *outs, stream, total = refs[7:]
        count = length // block
        for step, part in enumerate(parts):
            put_rows(stream, behind(step), rows, part[2])

        def both(left, other):
            spectra = to_spectra(high, low, stream[...])
            grads = anti_product(left, spectra, cols)
            terms = anti_product(other, spectra, cols)
            return from_spectra(back, jnp.concatenate([grads, terms], axis=1))

        def put_lags(index, out):
            for i in range(count):
                piece = columns(out, count + i, cols)
                lags[index, i * block : (i + 1) * block] = piece

        out = both(filt[1], mixed_spec[...])
        for i in range(count):
            total[i * block : (i + 1) * block] = columns(out, i, cols)
        put_lags(1, out)
        for step, part in enumerate(parts):
            grad = pick_rows(total, behind(step), rows)
            put_rows(stream, behind(step), rows, (grad * part[1].astype(F32)).astype(BF16))
        total[...] = total[...] * first_ref[...]
        put_result(outs, 0, total, 2)
        out = both(filt[0], value_spec[...])
        for i in range(count):
            total[i * block : (i + 1) * block] = columns(out, i, cols)
        put_result(outs, 1, total, 2)
        put_lags(0, out)

    with jax.named_scope("backward_convolutions"):
        lags, *sends_home = call(
            backward_kernel,
            [((2, length, cols), F32)] + [((2, rows, cols), BF16)] * seq,
            (
                *parts_in,
                filter_spectra,
                first_conv,
                value_spectra,
                mixed_spectra,
                fwd_high,
                fwd_low,
                inv_high,
            ),
            scratch=[pltpu.VMEM((length, cols), BF16), pltpu.VMEM((length, cols), F32)],
            flops=8 * table_flops,
            limit=limit,
        )

    if fast:
        def gated_kernel(*refs):
            stays_ref, near_ref, gate_ref, cot_ref, beside_ref, lags, *refs = refs
            kept, given, turned, gated, cots, whole, packed = refs
            turned[0] = stays_ref[1]
            turned[1] = near_ref[1]
            here = lax.axis_index("ctx")
            cots[:rows] = cot_ref[...]
            cots[rows:] = beside_ref[:, :width]
            for index, ref in enumerate((stays_ref, near_ref)):
                lanes = pl.ds(index * cols, cols)
                gate = pick_columns(gate_ref, held(here ^ (2 * index)), cols, seq)
                gated[:rows, lanes] = (gate.astype(F32) * ref[0].astype(F32)).astype(BF16)
                gate = columns(beside_ref, width // cols + index, cols)
                gated[rows:, lanes] = (gate.astype(F32) * ref[1].astype(F32)).astype(BF16)
            whole[...] = lax.dot_general(
                gated[...], cots[...], (((0,), (0,)), ((), ())), preferred_element_type=F32
            )
            lower = lax.broadcasted_iota(jnp.int32, (length, cols), 1) < fine
            packed[0] = jnp.where(lower, lags[0], pltpu.roll(lags[1], fine, axis=1))
            packed[1] = jnp.where(lower, pltpu.roll(lags[0], fine, axis=1), lags[1])
            own_core = lax.rem(lax.axis_index("dp"), 2)
            first = jnp.where(here == 0, 1 - own_core, own_core)
            second = jnp.where(here == 2, 1 - own_core, own_core)
            for out, one, two in ((kept, first, second), (given, 1 - first, 1 - second)):
                piece = whole[pl.ds(pl.multiple_of(one * own_rows, own_rows), own_rows), :]
                out[:own_rows] = piece.astype(out.dtype)
                for index in range(seq):
                    piece = packed[one, index * rows : (index + 1) * rows]
                    out[own_rows : own_rows + rows, index * cols : (index + 1) * cols] = (
                        piece.astype(out.dtype)
                    )
                start = pl.multiple_of(cols + two * own_rows, own_rows)
                out[own_rows + rows :] = whole[pl.ds(start, own_rows), :].astype(out.dtype)

        term_shape = (2 * own_rows + rows, width)
        with jax.named_scope("weight_partial"):
            kept, given, goes_on = call(
                gated_kernel,
                [(term_shape, F32), (term_shape, BF16), ((2, rows, cols), BF16)],
                (second_stays, second_near, gate_two[0], grad_out[0], beside_in, lags),
                scratch=[
                    pltpu.VMEM((2 * rows, 2 * cols), BF16),
                    pltpu.VMEM((2 * rows, width), BF16),
                    pltpu.VMEM((2 * cols, width), F32),
                    pltpu.VMEM((2, length, cols), F32),
                ],
                limit=limit,
            )
        taken = lax.ppermute(given, "dp", [(i, i ^ 1) for i in range(data)])
        second_far = lax.ppermute(goes_on, "ctx", across(1))

        def core_kernel(kept_ref, taken_ref, one, two):
            summed = (kept_ref[...] + taken_ref[...].astype(F32)).astype(BF16)
            one[...] = summed[: own_rows + rows]
            two[...] = summed[own_rows + rows :]

        with jax.named_scope("core_sum"):
            sends = call(
                core_kernel,
                [((own_rows + rows, width), BF16), ((own_rows, width), BF16)],
                (kept, taken),
                limit=limit,
            )

        def to_chip(block, other):
            pairs = []
            for i in range(data):
                for j in range(seq):
                    pairs.append((i * seq + j, (i ^ (2 * (j ^ other) or 1)) * seq + j))
            return lax.ppermute(block, ("dp", "ctx"), pairs)

        chip_terms = [to_chip(sends[0], 0), to_chip(sends[1], 2)]

        home = around(sends_home)

        def place_kernel(one, two, *refs):
            outs, total = refs[:-1], refs[-1]
            total[...] = one[:own_rows].astype(F32) + two[...].astype(F32)
            for step, out in enumerate(outs):
                out[:own_rows] = pick_columns(total, ahead(step), cols, seq).astype(out.dtype)
                lag = pick_columns(one, ahead(step), cols, seq)[own_rows:]
                out[own_rows:] = lag.astype(out.dtype)

        small = (own_rows + rows, cols)
        with jax.named_scope("chip_sum"):
            sends = call(
                place_kernel,
                [(small, F32)] + [(small, BF16)] * (seq - 1),
                chip_terms,
                scratch=[pltpu.VMEM((own_rows, width), F32)],
            )
        last_terms = around(sends)

        def mixed_kernel(*refs):
            parts, (gate_ref, weight_ref, cot_ref, mixed_ref, out, second) = refs[:3], refs[3:]
            here = lax.axis_index("ctx")
            stays_ref, near_ref, far_ref = parts
            put_columns(second, held(here), cols, seq, stays_ref[0])
            put_columns(second, held(here ^ 2), cols, seq, near_ref[0])
            put_columns(second, held(here ^ 1), cols, seq, far_ref[0])
            put_columns(second, held(here ^ 3), cols, seq, far_ref[1])
            wide = second[...].astype(F32)
            gated = (gate_ref[...].astype(F32) * wide).astype(BF16)
            mixed_ref[...] = mxu(gated, weight_ref[...]).astype(BF16)
            out[...] = (grad_gated(cot_ref, weight_ref) * wide).astype(BF16)

        with jax.named_scope("mixed"):
            mixed, grad_gate_two = call(
                mixed_kernel,
                [wide_bf16, wide_bf16],
                (second_stays, second_near, second_far, gate_two[0], out_weight, grad_out[0]),
                scratch=[pltpu.VMEM((rows, width), BF16)],
                flops=4 * rows * width * width,
                limit=limit,
            )

        order = (0, 3, 2, 1)

        def final_kernel(*refs):
            arrived, parts, refs = refs[:seq], refs[seq : 2 * seq], refs[2 * seq :]
            filter_ref, weight_ref, gate_ref, value_ref = refs
            for step, part in zip(order, parts):
                put_columns(gate_ref, held(behind(step)), cols, seq, part[0])
                put_columns(value_ref, held(behind(step)), cols, seq, part[1])
            total = arrived[0][...]
            for part in arrived[1:]:
                total = total + part[...].astype(F32)
            total = total * (1.0 / data)
            weight_ref[...] = total[:own_rows]
            turned = total[own_rows:].T
            filter_ref[0] = turned[:fine]
            filter_ref[1] = turned[fine:]

        with jax.named_scope("means"):
            filter_grad, weight_grad, grad_gate_one, grad_value = call(
                final_kernel,
                [((2, fine, rows), F32), ((own_rows, cols), F32), wide_bf16, wide_bf16],
                (*last_terms, *(home[step] for step in order)),
            )
        filter_grad = jnp.swapaxes(filter_grad, 1, 2)
        return (
            mixed[None],
            grad_value[None],
            grad_gate_one[None],
            grad_gate_two[None],
            filter_grad,
            weight_grad,
        )

    def gated_kernel(*refs):
        parts, (gate_ref, cot_ref, second_ref, gated_ref, weight_ref) = refs[:seq], refs[seq:]
        for step, part in enumerate(parts):
            put_columns(second_ref, held(behind(step)), cols, seq, part[0])
        gated = (gate_ref[...].astype(F32) * second_ref[...].astype(F32)).astype(BF16)
        gated_ref[...] = gated
        weight_ref[...] = lax.dot_general(
            gated, cot_ref[...], (((0,), (0,)), ((), ())), preferred_element_type=F32
        )

    with jax.named_scope("weight_partial"):
        second_conv, gated, weight_part = call(
            gated_kernel,
            [wide_bf16, wide_bf16, ((width, width), F32)],
            (*second_parts, gate_two[0], grad_out[0]),
            flops=2 * rows * width * width,
            limit=limit,
        )

    core = lax.rem(lax.axis_index("dp"), 2)
    lag_terms = lags.reshape(2, seq, rows, per_ctx, fine).transpose(1, 3, 2, 0, 4)
    lag_rows = rows * 2 * fine // width
    terms = jnp.concatenate(
        [
            weight_part.reshape(data, own_rows, width),
            lag_terms.reshape(data, lag_rows, width),
        ],
        axis=1,
    )
    by_core = terms.reshape(chips, 2, *terms.shape[1:])
    kept = lax.dynamic_index_in_dim(by_core, core, 1, keepdims=False)
    given = lax.dynamic_index_in_dim(by_core, 1 - core, 1, keepdims=False).astype(BF16)
    given, kept = (a.reshape(-1, width) for a in (given, kept))
    taken = lax.ppermute(given, "dp", [(i, i ^ 1) for i in range(data)])
    term_rows = own_rows + lag_rows

    def chip_kernel(kept_ref, taken_ref, own, *outs):
        place = lax.div(lax.axis_index("dp"), 2)

        def summed(index):
            start = pl.multiple_of(index * term_rows, term_rows)
            taken = taken_ref[pl.ds(start, term_rows), :]
            return kept_ref[pl.ds(start, term_rows), :] + taken.astype(F32)

        own[...] = summed(place)
        for step in range(1, chips):
            outs[step - 1][...] = summed(place ^ step).astype(BF16)

    term = (term_rows, width)
    with jax.named_scope("core_sum"):
        total, *sends = call(
            chip_kernel,
            [(term, F32)] + [(term, BF16)] * (chips - 1),
            (kept, taken),
            limit=limit,
        )
    for step in range(1, chips):
        pairs = [(i, i ^ (2 * step)) for i in range(data)]
        total = total + lax.ppermute(sends[step - 1], "dp", pairs).astype(F32)

    def mixed_kernel(gated_ref, weight_ref, cot_ref, second_ref, mixed_ref, gate_ref):
        mixed_ref[...] = mxu(gated_ref[...], weight_ref[...]).astype(BF16)
        grad = grad_gated(cot_ref, weight_ref)
        gate_ref[...] = (grad * second_ref[...].astype(F32)).astype(BF16)

    with jax.named_scope("mixed"):
        mixed, grad_gate_two = call(
            mixed_kernel,
            [wide_bf16, wide_bf16],
            (gated, out_weight, grad_out[0], second_conv),
            flops=4 * rows * width * width,
            limit=limit,
        )
    home = around(sends_home)

    weight_blocks = total[:own_rows].reshape(own_rows, seq, cols)
    sends = [
        lax.dynamic_index_in_dim(weight_blocks, ahead(step), 1, keepdims=False)
        for step in range(seq)
    ]
    last_terms = around(sends[:1] + [part.astype(BF16) for part in sends[1:]])
    lag_sum = total[own_rows:].reshape(rows, 2 * fine).astype(BF16)
    pairs = []
    for i in range(data):
        for j in range(seq):
            pairs.append((i * seq + j, (per_ctx * j + i % per_ctx) * seq + i // per_ctx))
    lag_own = lax.ppermute(lag_sum, ("dp", "ctx"), pairs)

    def unpack_kernel(*refs):
        parts, (gate_ref, value_ref) = refs[:-2], refs[-2:]
        for step, part in enumerate(parts):
            put_columns(gate_ref, held(behind(step)), cols, seq, part[0])
            put_columns(value_ref, held(behind(step)), cols, seq, part[1])

    with jax.named_scope("unpack_results"):
        grad_gate_one, grad_value = call(unpack_kernel, [wide_bf16, wide_bf16], home)
    filter_grad = lag_own.reshape(rows, 2, fine).transpose(1, 0, 2).astype(F32) / data
    weight_grad = sum(part.astype(F32) for part in last_terms) / data
    return (
        mixed[None],
        grad_value[None],
        grad_gate_one[None],
        grad_gate_two[None],
        filter_grad,
        weight_grad,
    )


def solution(mesh):
    stream = P("dp", "ctx", None)
    return jax.shard_map(
        on_device,
        mesh=mesh,
        in_specs=(stream, stream, stream, P(), P(), stream),
        out_specs=(stream, stream, stream, stream, P(None, "ctx", "dp"), P("dp", "ctx")),
        check_vma=False,
    )
```

```python
import functools
import math

import jax
import jax.numpy as jnp
import ml_dtypes
import numpy as np
from jax import lax
from jax.experimental import pallas as pl
from jax.experimental.pallas import tpu as pltpu
from jax.sharding import PartitionSpec as P

F32 = jnp.float32
BF16 = jnp.bfloat16


def split_table(table):
    high = table.astype(ml_dtypes.bfloat16)
    low = (table - high.astype(np.float64)).astype(ml_dtypes.bfloat16)
    return jnp.asarray(high), jnp.asarray(low)


@functools.lru_cache(maxsize=None)
def table_values(block):
    period = 2 * block
    bins = np.arange(block)
    radians = (bins[:, None] * bins[None, :] % period) * (2.0 * math.pi / period)
    cosines, sines = np.cos(radians), -np.sin(radians)
    sines[0] = np.where(bins % 2 == 0, 1.0, -1.0)
    forward = np.concatenate([cosines, sines], axis=0)
    weights = np.full((period,), 2.0 / period)
    weights[0] = weights[block] = 1.0 / period
    return forward, forward.T * weights[None, :]


def mxu(left, right):
    return jnp.dot(left, right, preferred_element_type=F32)


def beside(stream, block):
    return jnp.concatenate(
        [stream[i : i + block] for i in range(0, stream.shape[0], block)], axis=1
    )


def to_spectra(high, low, stream):
    blocks = beside(stream, high.shape[1])
    return mxu(high[...], blocks) + mxu(low[...], blocks)


def from_spectra(high, spectra):
    return mxu(high[...], spectra.astype(BF16))


def parity(shape):
    row = lax.broadcasted_iota(jnp.int32, shape, 0)
    return jnp.where(row % 2 == 0, 1.0, -1.0)


def with_previous(spectra, cols):
    sign = parity((spectra.shape[0], cols))
    out = [spectra[:, :cols]]
    for i in range(cols, spectra.shape[1], cols):
        out.append(spectra[:, i : i + cols] + sign * spectra[:, i - cols : i])
    return jnp.concatenate(out, axis=1)


def sum_of_products(terms, conj_left):
    half = terms[0][0].shape[0] // 2
    border = lax.broadcasted_iota(jnp.int32, (half, terms[0][0].shape[1]), 0) == 0
    straight = cross = imag = 0.0
    for left, right in terms:
        left_re, left_im, right_re, right_im = left[:half], left[half:], right[:half], right[half:]
        straight += left_re * right_re
        cross += left_im * right_im
        if conj_left:
            imag += left_re * right_im - left_im * right_re
        else:
            imag += left_re * right_im + left_im * right_re
    inner = jnp.where(border, 0.0, cross)
    real = straight + inner if conj_left else straight - inner
    return jnp.concatenate([real, jnp.where(border, cross, imag)], axis=0)


def columns(ref, index, cols):
    return ref[:, index * cols : (index + 1) * cols]


def causal_product(filt, spectra, cols):
    count = spectra.shape[1] // cols
    out = []
    for i in range(count):
        terms = [(columns(filt, i - a, cols), columns(spectra, a, cols)) for a in range(i + 1)]
        out.append(sum_of_products(terms, False))
    return jnp.concatenate(out, axis=1)


def anti_product(left, spectra, cols):
    count = spectra.shape[1] // cols
    out = []
    for i in range(count):
        terms = [
            (columns(left, a - i, cols), columns(spectra, a, cols)) for a in range(i, count)
        ]
        out.append(sum_of_products(terms, True))
    return jnp.concatenate(out, axis=1)


def pick_columns(ref, index, width, count):
    if width % 128 == 0:
        return ref[:, pl.ds(pl.multiple_of(index * width, width), width)]
    whole = ref[...]
    out = whole[:, :width]
    for other in range(1, count):
        out = jnp.where(index == other, whole[:, other * width : (other + 1) * width], out)
    return out


def put_columns(ref, index, width, count, block):
    if width % 128 == 0:
        ref[:, pl.ds(pl.multiple_of(index * width, width), width)] = block
        return
    for other in range(count):

        @pl.when(index == other)
        def _():
            ref[:, other * width : (other + 1) * width] = block


def pick_rows(ref, index, rows):
    return ref[pl.ds(pl.multiple_of(index * rows, rows), rows), :]


def put_rows(ref, index, rows, block):
    ref[pl.ds(pl.multiple_of(index * rows, rows), rows), :] = block


def call(kernel, outs, args, scratch=(), flops=0, limit=16, in_hbm=False):
    vmem = pl.BlockSpec(memory_space=pltpu.VMEM)
    source = pl.BlockSpec(memory_space=pltpu.HBM) if in_hbm else vmem
    total = sum(math.prod(a.shape) * a.dtype.itemsize for a in args)
    return pl.pallas_call(
        kernel,
        out_shape=[jax.ShapeDtypeStruct(shape, dtype) for shape, dtype in outs],
        in_specs=[source] * len(args),
        out_specs=[vmem] * len(outs),
        scratch_shapes=list(scratch),
        compiler_params=pltpu.CompilerParams(vmem_limit_bytes=int(limit * 2**20)),
        cost_estimate=pl.CostEstimate(flops=flops, bytes_accessed=total, transcendentals=0),
    )(*args)


def on_device(value, gate_one, gate_two, filters, out_weight, grad_out):
    rows, width = value.shape[1:]
    seq = lax.axis_size("ctx")
    data = lax.axis_size("dp")
    length = rows * seq
    cols = width // seq
    block = math.gcd(length, 256)
    per_ctx = data // seq
    fine = cols // per_ctx
    chips = data // 2
    own_rows = width // data
    fast = cols == 128 and per_ctx == 2 and chips == seq == 4
    limit = 16 if length <= 512 else 48
    load_limit = 53.5
    forward, inverse = table_values(block)
    (fwd_high, fwd_low), (inv_high, _) = split_table(forward), split_table(inverse)
    spectra_shape = (2 * block, length // block * cols)
    table_flops = 4 * block * length * cols

    def ahead(step):
        return lax.rem(lax.axis_index("ctx") + step, seq)

    def behind(step):
        return lax.rem(lax.axis_index("ctx") + seq - step, seq)

    def held(place):
        return place ^ lax.div(lax.axis_index("dp"), 2) if fast else place

    def around(blocks):
        out = [blocks[0]]
        for step in range(1, seq):
            pairs = [(i, (i + step) % seq) for i in range(seq)]
            out.append(lax.ppermute(blocks[step], "ctx", pairs))
        return out

    def grad_gated(cot_ref, weight_ref):
        return lax.dot_general(
            cot_ref[...], weight_ref[...], (((1,), (1,)), ((), ())), preferred_element_type=F32
        )

    def load_kernel(*refs):
        value_ref, gate_ref, cot_arg, weight_arg, gate_arg = refs[:5]
        outs, refs = refs[5 : 5 + seq], refs[5 + seq :]
        cot_ref, weight_ref, gate_two_ref, second, whole, sems = refs
        started = [
            (cot_arg.at[0], cot_ref),
            (weight_arg, weight_ref),
            (gate_arg.at[0], gate_two_ref),
        ]
        if cols % 128 == 0:
            for step, out in enumerate(outs):
                start = pl.multiple_of(held(ahead(step)) * cols, cols)
                started.append((value_ref.at[0, :, pl.ds(start, cols)], out.at[0]))
                started.append((gate_ref.at[0, :, pl.ds(start, cols)], out.at[1]))
        else:
            started.append((value_ref.at[0], whole.at[0]))
            started.append((gate_ref.at[0], whole.at[1]))
        started = [
            pltpu.make_async_copy(source, target, sems.at[index])
            for index, (source, target) in enumerate(started)
        ]
        for copy in started:
            copy.start()
        for copy in started[:3]:
            copy.wait()
        second[...] = grad_gated(cot_ref, weight_ref) * gate_two_ref[...].astype(F32)
        for step, out in enumerate(outs):
            out[2] = pick_columns(second, held(ahead(step)), cols, seq).astype(BF16)
        for copy in started[3:]:
            copy.wait()
        if cols % 128 != 0:
            for step, out in enumerate(outs):
                for index in range(2):
                    out[index] = pick_columns(whole.at[index], held(ahead(step)), cols, seq)

    triple = ((3, rows, cols), BF16)
    wide_bf16 = ((rows, width), BF16)
    with jax.named_scope("load"):
        sends = call(
            load_kernel,
            [triple] * seq,
            (value, gate_one, grad_out, out_weight, gate_two),
            scratch=[
                pltpu.VMEM((rows, width), BF16),
                pltpu.VMEM((width, width), BF16),
                pltpu.VMEM((rows, width), BF16),
                pltpu.VMEM((rows, width), F32),
                pltpu.VMEM((2, rows, width), BF16),
                pltpu.SemaphoreType.DMA((2 * seq + 3,)),
            ],
            flops=2 * rows * width * width,
            in_hbm=True,
            limit=load_limit,
        )
    parts_in = around(sends)

    def across(far):
        return [(i, i ^ far) for i in range(seq)]

    def filter_kernel(filters_ref, high, low, cot_ref, gate_ref, out, *beside):
        if fast:
            beside[0][:, :width] = cot_ref[...]
            for index, far in enumerate((1, 3)):
                piece = pick_columns(gate_ref, held(lax.axis_index("ctx") ^ far), cols, seq)
                beside[0][:, width + index * cols : width + (index + 1) * cols] = piece
        for index in range(2):
            out[index] = with_previous(to_spectra(high, low, filters_ref[index]), cols)

    with jax.named_scope("filter_spectra"):
        own_filters = lax.dynamic_slice_in_dim(filters, held(lax.axis_index("ctx")) * cols, cols, 2)
        filter_spectra, *sends = call(
            filter_kernel,
            [((2, *spectra_shape), F32)] + [((rows, width + 2 * cols), BF16)] * fast,
            (own_filters, fwd_high, fwd_low, grad_out[0], gate_two[0]),
            flops=4 * table_flops,
            limit=limit,
        )
    if fast:
        beside_in = lax.ppermute(sends[0], "ctx", across(1))

    def put_result(outs, index, total, arrays):
        if len(outs) == seq:
            for step, out in enumerate(outs):
                out[index] = pick_rows(total, ahead(step), rows).astype(BF16)
            return
        for far in range(4):
            piece = pick_rows(total, lax.axis_index("ctx") ^ far, rows).astype(BF16)
            outs[far // 2][far % 2 * arrays + index] = piece

    def forward_kernel(*refs):
        parts, refs = refs[:seq], refs[seq:]
        filt, high, low, back, first_ref, value_spec, mixed_spec = refs[:7]
        outs, (stream, second) = refs[7:-2], refs[-2:]
        for step, part in enumerate(parts):
            put_rows(stream, behind(step), rows, part[0])
        spectra = to_spectra(high, low, stream[...])
        value_spec[...] = with_previous(spectra, cols)
        conv = from_spectra(back, causal_product(filt[0], spectra, cols))
        for i in range(length // block):
            first_ref[i * block : (i + 1) * block] = columns(conv, i, cols)
        for step, part in enumerate(parts):
            gated = part[1].astype(F32) * pick_rows(first_ref, behind(step), rows)
            put_rows(stream, behind(step), rows, gated.astype(BF16))
        spectra = to_spectra(high, low, stream[...])
        mixed_spec[...] = with_previous(spectra, cols)
        conv = from_spectra(back, causal_product(filt[1], spectra, cols))
        for i in range(length // block):
            second[i * block : (i + 1) * block] = columns(conv, i, cols)
        put_result(outs, 0, second, 1)

    with jax.named_scope("forward_convolutions"):
        first_conv, value_spectra, mixed_spectra, *sends = call(
            forward_kernel,
            [((length, cols), F32), (spectra_shape, F32), (spectra_shape, F32)]
            + ([((2, rows, cols), BF16)] * 2 if fast else [((1, rows, cols), BF16)] * seq),
            (*parts_in, filter_spectra, fwd_high, fwd_low, inv_high),
            scratch=[pltpu.VMEM((length, cols), BF16), pltpu.VMEM((length, cols), F32)],
            flops=6 * table_flops,
            limit=limit,
        )
    if fast:
        second_stays, goes = sends
        second_near = lax.ppermute(goes, "ctx", across(2))
    else:
        second_parts = around(sends)

    def backward_kernel(*refs):
        parts, refs = refs[:seq], refs[seq:]
        filt, first_ref, value_spec, mixed_spec, high, low, back = refs[:7]
        lags, *outs, stream, total = refs[7:]
        if fast:
            lag_kept, lag_given, *outs, packed = outs
        count = length // block
        for step, part in enumerate(parts):
            put_rows(stream, behind(step), rows, part[2])

        def both(left, other):
            spectra = to_spectra(high, low, stream[...])
            grads = anti_product(left, spectra, cols)
            terms = anti_product(other, spectra, cols)
            return from_spectra(back, jnp.concatenate([grads, terms], axis=1))

        def put_lags(index, out):
            for i in range(count):
                piece = columns(out, count + i, cols)
                lags[index, i * block : (i + 1) * block] = piece

        out = both(filt[1], mixed_spec[...])
        for i in range(count):
            total[i * block : (i + 1) * block] = columns(out, i, cols)
        put_lags(1, out)
        for step, part in enumerate(parts):
            grad = pick_rows(total, behind(step), rows)
            put_rows(stream, behind(step), rows, (grad * part[1].astype(F32)).astype(BF16))
        total[...] = total[...] * first_ref[...]
        put_result(outs, 0, total, 2)
        out = both(filt[0], value_spec[...])
        for i in range(count):
            total[i * block : (i + 1) * block] = columns(out, i, cols)
        put_result(outs, 1, total, 2)
        put_lags(0, out)
        if fast:
            here, own_core = lax.axis_index("ctx"), lax.rem(lax.axis_index("dp"), 2)
            half = jnp.where(here == 0, 1 - own_core, own_core)
            lower = lax.broadcasted_iota(jnp.int32, (length, cols), 1) < fine
            packed[0] = jnp.where(lower, lags[0], pltpu.roll(lags[1], fine, axis=1))
            packed[1] = jnp.where(lower, pltpu.roll(lags[0], fine, axis=1), lags[1])
            for index in range(seq):
                lanes = pl.ds(index * cols, cols)
                lag_kept[:, lanes] = packed[half, index * rows : (index + 1) * rows]
                given = packed[1 - half, index * rows : (index + 1) * rows]
                lag_given[:, lanes] = given.astype(BF16)

    with jax.named_scope("backward_convolutions"):
        lags, *sends_home = call(
            backward_kernel,
            [((2, length, cols), F32)] + [((rows, width), F32), wide_bf16] * fast + [((2, rows, cols), BF16)] * seq,
            (
                *parts_in,
                filter_spectra,
                first_conv,
                value_spectra,
                mixed_spectra,
                fwd_high,
                fwd_low,
                inv_high,
            ),
            scratch=[pltpu.VMEM((2, length, cols), F32)] * fast
            + [pltpu.VMEM((length, cols), BF16), pltpu.VMEM((length, cols), F32)],
            flops=8 * table_flops,
            limit=limit,
        )

    if fast:
        def to_core(block):
            return lax.ppermute(block, "dp", [(i, i ^ 1) for i in range(data)])

        def to_chip(block, other):
            pairs = []
            for i in range(data):
                for j in range(seq):
                    pairs.append((i * seq + j, (i ^ (2 * (j ^ other) or 1)) * seq + j))
            return lax.ppermute(block, ("dp", "ctx"), pairs)

        def core_kernel(kept_ref, taken_ref, *outs):
            summed = (kept_ref[...] + taken_ref[...].astype(F32)).astype(BF16)
            for index, out in enumerate(outs):
                out[...] = summed[index * out.shape[0] : (index + 1) * out.shape[0]]

        lag_kept, lag_given, *sends_home = sends_home
        with jax.named_scope("lag_core_sum"):
            (lag_sum,) = call(
                core_kernel, [wide_bf16], (lag_kept, to_core(lag_given)), limit=limit
            )
        lag_term = to_chip(lag_sum, 0)

        def gated_kernel(*refs):
            stays_ref, near_ref, gate_ref, cot_ref, beside_ref, _, *refs = refs
            kept, given, turned, gated, cots, whole = refs
            turned[0] = stays_ref[1]
            turned[1] = near_ref[1]
            here = lax.axis_index("ctx")
            cots[:rows] = cot_ref[...]
            cots[rows:] = beside_ref[:, :width]
            for index, ref in enumerate((stays_ref, near_ref)):
                lanes = pl.ds(index * cols, cols)
                gate = pick_columns(gate_ref, held(here ^ (2 * index)), cols, seq)
                gated[:rows, lanes] = (gate.astype(F32) * ref[0].astype(F32)).astype(BF16)
                gate = columns(beside_ref, width // cols + index, cols)
                gated[rows:, lanes] = (gate.astype(F32) * ref[1].astype(F32)).astype(BF16)
            whole[...] = lax.dot_general(
                gated[...], cots[...], (((0,), (0,)), ((), ())), preferred_element_type=F32
            )
            own_core = lax.rem(lax.axis_index("dp"), 2)
            first = jnp.where(here == 0, 1 - own_core, own_core)
            second = jnp.where(here == 2, 1 - own_core, own_core)
            for out, one, two in ((kept, first, second), (given, 1 - first, 1 - second)):
                piece = whole[pl.ds(pl.multiple_of(one * own_rows, own_rows), own_rows), :]
                out[:own_rows] = piece.astype(out.dtype)
                start = pl.multiple_of(cols + two * own_rows, own_rows)
                out[own_rows:] = whole[pl.ds(start, own_rows), :].astype(out.dtype)

        term_shape = (2 * own_rows, width)
        with jax.named_scope("weight_partial"):
            kept, given, goes_on = call(
                gated_kernel,
                [(term_shape, F32), (term_shape, BF16), ((2, rows, cols), BF16)],
                (second_stays, second_near, gate_two[0], grad_out[0], beside_in, gate_two[0]),
                scratch=[
                    pltpu.VMEM((2 * rows, 2 * cols), BF16),
                    pltpu.VMEM((2 * rows, width), BF16),
                    pltpu.VMEM((2 * cols, width), F32),
                ],
                limit=limit,
            )
        second_far = lax.ppermute(goes_on, "ctx", across(1))

        with jax.named_scope("core_sum"):
            sends = call(
                core_kernel,
                [((own_rows, width), BF16)] * 2,
                (kept, to_core(given)),
                limit=limit,
            )

        chip_terms = [to_chip(sends[0], 0), to_chip(sends[1], 2)]

        home = around(sends_home)

        def place_kernel(lag_ref, one, two, *refs):
            outs, total = refs[:-1], refs[-1]
            total[...] = one[...].astype(F32) + two[...].astype(F32)
            for step, out in enumerate(outs):
                out[:own_rows] = pick_columns(total, ahead(step), cols, seq).astype(out.dtype)
                out[own_rows:] = pick_columns(lag_ref, ahead(step), cols, seq).astype(out.dtype)

        small = (own_rows + rows, cols)
        with jax.named_scope("chip_sum"):
            sends = call(
                place_kernel,
                [(small, F32)] + [(small, BF16)] * (seq - 1),
                (lag_term, *chip_terms),
                scratch=[pltpu.VMEM((own_rows, width), F32)],
            )
        last_terms = around(sends)

        def mixed_kernel(*refs):
            parts, (gate_ref, weight_ref, cot_ref, mixed_ref, out, second) = refs[:3], refs[3:]
            here = lax.axis_index("ctx")
            stays_ref, near_ref, far_ref = parts
            put_columns(second, held(here), cols, seq, stays_ref[0])
            put_columns(second, held(here ^ 2), cols, seq, near_ref[0])
            put_columns(second, held(here ^ 1), cols, seq, far_ref[0])
            put_columns(second, held(here ^ 3), cols, seq, far_ref[1])
            wide = second[...].astype(F32)
            gated = (gate_ref[...].astype(F32) * wide).astype(BF16)
            mixed_ref[...] = mxu(gated, weight_ref[...]).astype(BF16)
            out[...] = (grad_gated(cot_ref, weight_ref) * wide).astype(BF16)

        with jax.named_scope("mixed"):
            mixed, grad_gate_two = call(
                mixed_kernel,
                [wide_bf16, wide_bf16],
                (second_stays, second_near, second_far, gate_two[0], out_weight, grad_out[0]),
                scratch=[pltpu.VMEM((rows, width), BF16)],
                flops=4 * rows * width * width,
                limit=limit,
            )

        order = (0, 3, 2, 1)

        def final_kernel(*refs):
            arrived, parts, refs = refs[:seq], refs[seq : 2 * seq], refs[2 * seq :]
            filter_ref, weight_ref, gate_ref, value_ref = refs
            for step, part in zip(order, parts):
                put_columns(gate_ref, held(behind(step)), cols, seq, part[0])
                put_columns(value_ref, held(behind(step)), cols, seq, part[1])
            total = arrived[0][...]
            for part in arrived[1:]:
                total = total + part[...].astype(F32)
            total = total * (1.0 / data)
            weight_ref[...] = total[:own_rows]
            turned = total[own_rows:].T
            filter_ref[0] = turned[:fine]
            filter_ref[1] = turned[fine:]

        with jax.named_scope("means"):
            filter_grad, weight_grad, grad_gate_one, grad_value = call(
                final_kernel,
                [((2, fine, rows), F32), ((own_rows, cols), F32), wide_bf16, wide_bf16],
                (*last_terms, *(home[step] for step in order)),
            )
        filter_grad = jnp.swapaxes(filter_grad, 1, 2)
        return (
            mixed[None],
            grad_value[None],
            grad_gate_one[None],
            grad_gate_two[None],
            filter_grad,
            weight_grad,
        )

    def gated_kernel(*refs):
        parts, (gate_ref, cot_ref, second_ref, gated_ref, weight_ref) = refs[:seq], refs[seq:]
        for step, part in enumerate(parts):
            put_columns(second_ref, held(behind(step)), cols, seq, part[0])
        gated = (gate_ref[...].astype(F32) * second_ref[...].astype(F32)).astype(BF16)
        gated_ref[...] = gated
        weight_ref[...] = lax.dot_general(
            gated, cot_ref[...], (((0,), (0,)), ((), ())), preferred_element_type=F32
        )

    with jax.named_scope("weight_partial"):
        second_conv, gated, weight_part = call(
            gated_kernel,
            [wide_bf16, wide_bf16, ((width, width), F32)],
            (*second_parts, gate_two[0], grad_out[0]),
            flops=2 * rows * width * width,
            limit=limit,
        )

    core = lax.rem(lax.axis_index("dp"), 2)
    lag_terms = lags.reshape(2, seq, rows, per_ctx, fine).transpose(1, 3, 2, 0, 4)
    lag_rows = rows * 2 * fine // width
    terms = jnp.concatenate(
        [
            weight_part.reshape(data, own_rows, width),
            lag_terms.reshape(data, lag_rows, width),
        ],
        axis=1,
    )
    by_core = terms.reshape(chips, 2, *terms.shape[1:])
    kept = lax.dynamic_index_in_dim(by_core, core, 1, keepdims=False)
    given = lax.dynamic_index_in_dim(by_core, 1 - core, 1, keepdims=False).astype(BF16)
    given, kept = (a.reshape(-1, width) for a in (given, kept))
    taken = lax.ppermute(given, "dp", [(i, i ^ 1) for i in range(data)])
    term_rows = own_rows + lag_rows

    def chip_kernel(kept_ref, taken_ref, own, *outs):
        place = lax.div(lax.axis_index("dp"), 2)

        def summed(index):
            start = pl.multiple_of(index * term_rows, term_rows)
            taken = taken_ref[pl.ds(start, term_rows), :]
            return kept_ref[pl.ds(start, term_rows), :] + taken.astype(F32)

        own[...] = summed(place)
        for step in range(1, chips):
            outs[step - 1][...] = summed(place ^ step).astype(BF16)

    term = (term_rows, width)
    with jax.named_scope("core_sum"):
        total, *sends = call(
            chip_kernel,
            [(term, F32)] + [(term, BF16)] * (chips - 1),
            (kept, taken),
            limit=limit,
        )
    for step in range(1, chips):
        pairs = [(i, i ^ (2 * step)) for i in range(data)]
        total = total + lax.ppermute(sends[step - 1], "dp", pairs).astype(F32)

    def mixed_kernel(gated_ref, weight_ref, cot_ref, second_ref, mixed_ref, gate_ref):
        mixed_ref[...] = mxu(gated_ref[...], weight_ref[...]).astype(BF16)
        grad = grad_gated(cot_ref, weight_ref)
        gate_ref[...] = (grad * second_ref[...].astype(F32)).astype(BF16)

    with jax.named_scope("mixed"):
        mixed, grad_gate_two = call(
            mixed_kernel,
            [wide_bf16, wide_bf16],
            (gated, out_weight, grad_out[0], second_conv),
            flops=4 * rows * width * width,
            limit=limit,
        )
    home = around(sends_home)

    weight_blocks = total[:own_rows].reshape(own_rows, seq, cols)
    sends = [
        lax.dynamic_index_in_dim(weight_blocks, ahead(step), 1, keepdims=False)
        for step in range(seq)
    ]
    last_terms = around(sends[:1] + [part.astype(BF16) for part in sends[1:]])
    lag_sum = total[own_rows:].reshape(rows, 2 * fine).astype(BF16)
    pairs = []
    for i in range(data):
        for j in range(seq):
            pairs.append((i * seq + j, (per_ctx * j + i % per_ctx) * seq + i // per_ctx))
    lag_own = lax.ppermute(lag_sum, ("dp", "ctx"), pairs)

    def unpack_kernel(*refs):
        parts, (gate_ref, value_ref) = refs[:-2], refs[-2:]
        for step, part in enumerate(parts):
            put_columns(gate_ref, held(behind(step)), cols, seq, part[0])
            put_columns(value_ref, held(behind(step)), cols, seq, part[1])

    with jax.named_scope("unpack_results"):
        grad_gate_one, grad_value = call(unpack_kernel, [wide_bf16, wide_bf16], home)
    filter_grad = lag_own.reshape(rows, 2, fine).transpose(1, 0, 2).astype(F32) / data
    weight_grad = sum(part.astype(F32) for part in last_terms) / data
    return (
        mixed[None],
        grad_value[None],
        grad_gate_one[None],
        grad_gate_two[None],
        filter_grad,
        weight_grad,
    )


def solution(mesh):
    stream = P("dp", "ctx", None)
    return jax.shard_map(
        on_device,
        mesh=mesh,
        in_specs=(stream, stream, stream, P(), P(), stream),
        out_specs=(stream, stream, stream, stream, P(None, "ctx", "dp"), P("dp", "ctx")),
        check_vma=False,
    )
```

```python
import functools
import math

import jax
import jax.numpy as jnp
import ml_dtypes
import numpy as np
from jax import lax
from jax.experimental import pallas as pl
from jax.experimental.pallas import tpu as pltpu
from jax.sharding import PartitionSpec as P

F32 = jnp.float32
BF16 = jnp.bfloat16


def split_table(table):
    high = table.astype(ml_dtypes.bfloat16)
    low = (table - high.astype(np.float64)).astype(ml_dtypes.bfloat16)
    return jnp.asarray(high), jnp.asarray(low)


@functools.lru_cache(maxsize=None)
def table_values(block):
    period = 2 * block
    bins = np.arange(block)
    radians = (bins[:, None] * bins[None, :] % period) * (2.0 * math.pi / period)
    cosines, sines = np.cos(radians), -np.sin(radians)
    sines[0] = np.where(bins % 2 == 0, 1.0, -1.0)
    forward = np.concatenate([cosines, sines], axis=0)
    weights = np.full((period,), 2.0 / period)
    weights[0] = weights[block] = 1.0 / period
    return forward, forward.T * weights[None, :]


def mxu(left, right):
    return jnp.dot(left, right, preferred_element_type=F32)


def beside(stream, block):
    return jnp.concatenate(
        [stream[i : i + block] for i in range(0, stream.shape[0], block)], axis=1
    )


def to_spectra(high, low, stream):
    blocks = beside(stream, high.shape[1])
    return mxu(high[...], blocks) + mxu(low[...], blocks)


def from_spectra(high, spectra):
    return mxu(high[...], spectra.astype(BF16))


def parity(shape):
    row = lax.broadcasted_iota(jnp.int32, shape, 0)
    return jnp.where(row % 2 == 0, 1.0, -1.0)


def with_previous(spectra, cols):
    sign = parity((spectra.shape[0], cols))
    out = [spectra[:, :cols]]
    for i in range(cols, spectra.shape[1], cols):
        out.append(spectra[:, i : i + cols] + sign * spectra[:, i - cols : i])
    return jnp.concatenate(out, axis=1)


def sum_of_products(terms, conj_left):
    half = terms[0][0].shape[0] // 2
    border = lax.broadcasted_iota(jnp.int32, (half, terms[0][0].shape[1]), 0) == 0
    straight = cross = imag = 0.0
    for left, right in terms:
        left_re, left_im, right_re, right_im = left[:half], left[half:], right[:half], right[half:]
        straight += left_re * right_re
        cross += left_im * right_im
        if conj_left:
            imag += left_re * right_im - left_im * right_re
        else:
            imag += left_re * right_im + left_im * right_re
    inner = jnp.where(border, 0.0, cross)
    real = straight + inner if conj_left else straight - inner
    return jnp.concatenate([real, jnp.where(border, cross, imag)], axis=0)


def columns(ref, index, cols):
    return ref[:, index * cols : (index + 1) * cols]


def causal_product(filt, spectra, cols):
    count = spectra.shape[1] // cols
    out = []
    for i in range(count):
        terms = [(columns(filt, i - a, cols), columns(spectra, a, cols)) for a in range(i + 1)]
        out.append(sum_of_products(terms, False))
    return jnp.concatenate(out, axis=1)


def anti_product(left, spectra, cols):
    count = spectra.shape[1] // cols
    out = []
    for i in range(count):
        terms = [
            (columns(left, a - i, cols), columns(spectra, a, cols)) for a in range(i, count)
        ]
        out.append(sum_of_products(terms, True))
    return jnp.concatenate(out, axis=1)


def pick_columns(ref, index, width, count):
    if width % 128 == 0:
        return ref[:, pl.ds(pl.multiple_of(index * width, width), width)]
    whole = ref[...]
    out = whole[:, :width]
    for other in range(1, count):
        out = jnp.where(index == other, whole[:, other * width : (other + 1) * width], out)
    return out


def put_columns(ref, index, width, count, block):
    if width % 128 == 0:
        ref[:, pl.ds(pl.multiple_of(index * width, width), width)] = block
        return
    for other in range(count):

        @pl.when(index == other)
        def _():
            ref[:, other * width : (other + 1) * width] = block


def pick_rows(ref, index, rows):
    return ref[pl.ds(pl.multiple_of(index * rows, rows), rows), :]


def put_rows(ref, index, rows, block):
    ref[pl.ds(pl.multiple_of(index * rows, rows), rows), :] = block


def call(kernel, outs, args, scratch=(), flops=0, limit=16, in_hbm=False):
    vmem = pl.BlockSpec(memory_space=pltpu.VMEM)
    source = pl.BlockSpec(memory_space=pltpu.HBM) if in_hbm else vmem
    total = sum(math.prod(a.shape) * a.dtype.itemsize for a in args)
    return pl.pallas_call(
        kernel,
        out_shape=[jax.ShapeDtypeStruct(shape, dtype) for shape, dtype in outs],
        in_specs=[source] * len(args),
        out_specs=[vmem] * len(outs),
        scratch_shapes=list(scratch),
        compiler_params=pltpu.CompilerParams(vmem_limit_bytes=int(limit * 2**20)),
        cost_estimate=pl.CostEstimate(flops=flops, bytes_accessed=total, transcendentals=0),
    )(*args)


def on_device(value, gate_one, gate_two, filters, out_weight, grad_out):
    rows, width = value.shape[1:]
    seq = lax.axis_size("ctx")
    data = lax.axis_size("dp")
    length = rows * seq
    cols = width // seq
    block = math.gcd(length, 256)
    per_ctx = data // seq
    fine = cols // per_ctx
    chips = data // 2
    own_rows = width // data
    fast = cols == 128 and per_ctx == 2 and chips == seq == 4
    limit = 16 if length <= 512 else 48
    load_limit = 53.5
    forward, inverse = table_values(block)
    (fwd_high, fwd_low), (inv_high, _) = split_table(forward), split_table(inverse)
    spectra_shape = (2 * block, length // block * cols)
    table_flops = 4 * block * length * cols

    def ahead(step):
        return lax.rem(lax.axis_index("ctx") + step, seq)

    def behind(step):
        return lax.rem(lax.axis_index("ctx") + seq - step, seq)

    def held(place):
        return place ^ lax.div(lax.axis_index("dp"), 2) if fast else place

    def around(blocks):
        out = [blocks[0]]
        for step in range(1, seq):
            pairs = [(i, (i + step) % seq) for i in range(seq)]
            out.append(lax.ppermute(blocks[step], "ctx", pairs))
        return out

    def grad_gated(cot_ref, weight_ref):
        return lax.dot_general(
            cot_ref[...], weight_ref[...], (((1,), (1,)), ((), ())), preferred_element_type=F32
        )

    def load_kernel(*refs):
        value_ref, gate_ref, cot_arg, weight_arg, gate_arg = refs[:5]
        outs, refs = refs[5 : 5 + seq], refs[5 + seq :]
        cot_ref, weight_ref, gate_two_ref, second, whole, sems = refs
        started = [
            (cot_arg.at[0], cot_ref),
            (weight_arg, weight_ref),
            (gate_arg.at[0], gate_two_ref),
        ]
        if cols % 128 == 0:
            for step, out in enumerate(outs):
                start = pl.multiple_of(held(ahead(step)) * cols, cols)
                started.append((value_ref.at[0, :, pl.ds(start, cols)], out.at[0]))
                started.append((gate_ref.at[0, :, pl.ds(start, cols)], out.at[1]))
        else:
            started.append((value_ref.at[0], whole.at[0]))
            started.append((gate_ref.at[0], whole.at[1]))
        started = [
            pltpu.make_async_copy(source, target, sems.at[index])
            for index, (source, target) in enumerate(started)
        ]
        for copy in started:
            copy.start()
        for copy in started[:3]:
            copy.wait()
        second[...] = grad_gated(cot_ref, weight_ref) * gate_two_ref[...].astype(F32)
        for step, out in enumerate(outs):
            out[2] = pick_columns(second, held(ahead(step)), cols, seq).astype(BF16)
        for copy in started[3:]:
            copy.wait()
        if cols % 128 != 0:
            for step, out in enumerate(outs):
                for index in range(2):
                    out[index] = pick_columns(whole.at[index], held(ahead(step)), cols, seq)

    triple = ((3, rows, cols), BF16)
    wide_bf16 = ((rows, width), BF16)
    with jax.named_scope("load"):
        sends = call(
            load_kernel,
            [triple] * seq,
            (value, gate_one, grad_out, out_weight, gate_two),
            scratch=[
                pltpu.VMEM((rows, width), BF16),
                pltpu.VMEM((width, width), BF16),
                pltpu.VMEM((rows, width), BF16),
                pltpu.VMEM((rows, width), F32),
                pltpu.VMEM((2, rows, width), BF16),
                pltpu.SemaphoreType.DMA((2 * seq + 3,)),
            ],
            flops=2 * rows * width * width,
            in_hbm=True,
            limit=load_limit,
        )
    parts_in = around(sends)

    def across(far):
        return [(i, i ^ far) for i in range(seq)]

    def filter_kernel(filters_ref, high, low, cot_ref, gate_ref, out, *beside):
        if fast:
            beside[0][:, :width] = cot_ref[...]
            for index, far in enumerate((1, 3)):
                piece = pick_columns(gate_ref, held(lax.axis_index("ctx") ^ far), cols, seq)
                beside[0][:, width + index * cols : width + (index + 1) * cols] = piece
        for index in range(2):
            out[index] = with_previous(to_spectra(high, low, filters_ref[index]), cols)

    with jax.named_scope("filter_spectra"):
        own_filters = lax.dynamic_slice_in_dim(filters, held(lax.axis_index("ctx")) * cols, cols, 2)
        filter_spectra, *sends = call(
            filter_kernel,
            [((2, *spectra_shape), F32)] + [((rows, width + 2 * cols), BF16)] * fast,
            (own_filters, fwd_high, fwd_low, grad_out[0], gate_two[0]),
            flops=4 * table_flops,
            limit=limit,
        )
    if fast:
        beside_in = lax.ppermute(sends[0], "ctx", across(1))

    def put_result(outs, index, total, arrays):
        if len(outs) == seq:
            for step, out in enumerate(outs):
                place = lax.axis_index("ctx") ^ step if fast else ahead(step)
                out[index] = pick_rows(total, place, rows).astype(BF16)
            return
        for far in range(4):
            piece = pick_rows(total, lax.axis_index("ctx") ^ far, rows).astype(BF16)
            outs[far // 2][far % 2 * arrays + index] = piece

    def forward_kernel(*refs):
        parts, refs = refs[:seq], refs[seq:]
        filt, high, low, back, first_ref, value_spec, mixed_spec = refs[:7]
        outs, (stream, second) = refs[7:-2], refs[-2:]
        for step, part in enumerate(parts):
            put_rows(stream, behind(step), rows, part[0])
        spectra = to_spectra(high, low, stream[...])
        value_spec[...] = with_previous(spectra, cols)
        conv = from_spectra(back, causal_product(filt[0], spectra, cols))
        for i in range(length // block):
            first_ref[i * block : (i + 1) * block] = columns(conv, i, cols)
        for step, part in enumerate(parts):
            gated = part[1].astype(F32) * pick_rows(first_ref, behind(step), rows)
            put_rows(stream, behind(step), rows, gated.astype(BF16))
        spectra = to_spectra(high, low, stream[...])
        mixed_spec[...] = with_previous(spectra, cols)
        conv = from_spectra(back, causal_product(filt[1], spectra, cols))
        for i in range(length // block):
            second[i * block : (i + 1) * block] = columns(conv, i, cols)
        put_result(outs, 0, second, 1)

    with jax.named_scope("forward_convolutions"):
        first_conv, value_spectra, mixed_spectra, *sends = call(
            forward_kernel,
            [((length, cols), F32), (spectra_shape, F32), (spectra_shape, F32)]
            + ([((2, rows, cols), BF16)] * 2 if fast else [((1, rows, cols), BF16)] * seq),
            (*parts_in, filter_spectra, fwd_high, fwd_low, inv_high),
            scratch=[pltpu.VMEM((length, cols), BF16), pltpu.VMEM((length, cols), F32)],
            flops=6 * table_flops,
            limit=limit,
        )
    if fast:
        second_stays, goes = sends
        second_near = lax.ppermute(goes, "ctx", across(2))
    else:
        second_parts = around(sends)

    def backward_kernel(*refs):
        parts, refs = refs[:seq], refs[seq:]
        filt, first_ref, value_spec, mixed_spec, high, low, back = refs[:7]
        lags, *outs, stream, total = refs[7:]
        if fast:
            lag_kept, lag_given, *outs, packed = outs
        count = length // block
        for step, part in enumerate(parts):
            put_rows(stream, behind(step), rows, part[2])

        def both(left, other):
            spectra = to_spectra(high, low, stream[...])
            grads = anti_product(left, spectra, cols)
            terms = anti_product(other, spectra, cols)
            return from_spectra(back, jnp.concatenate([grads, terms], axis=1))

        def put_lags(index, out):
            for i in range(count):
                piece = columns(out, count + i, cols)
                lags[index, i * block : (i + 1) * block] = piece

        out = both(filt[1], mixed_spec[...])
        for i in range(count):
            total[i * block : (i + 1) * block] = columns(out, i, cols)
        put_lags(1, out)
        for step, part in enumerate(parts):
            grad = pick_rows(total, behind(step), rows)
            put_rows(stream, behind(step), rows, (grad * part[1].astype(F32)).astype(BF16))
        total[...] = total[...] * first_ref[...]
        put_result(outs, 0, total, 2)
        out = both(filt[0], value_spec[...])
        for i in range(count):
            total[i * block : (i + 1) * block] = columns(out, i, cols)
        put_result(outs, 1, total, 2)
        put_lags(0, out)
        if fast:
            here, own_core = lax.axis_index("ctx"), lax.rem(lax.axis_index("dp"), 2)
            half = jnp.where(here == 0, 1 - own_core, own_core)
            lower = lax.broadcasted_iota(jnp.int32, (length, cols), 1) < fine
            packed[0] = jnp.where(lower, lags[0], pltpu.roll(lags[1], fine, axis=1))
            packed[1] = jnp.where(lower, pltpu.roll(lags[0], fine, axis=1), lags[1])
            for index in range(seq):
                lanes = pl.ds(index * cols, cols)
                lag_kept[:, lanes] = packed[half, index * rows : (index + 1) * rows]
                given = packed[1 - half, index * rows : (index + 1) * rows]
                lag_given[:, lanes] = given.astype(BF16)

    with jax.named_scope("backward_convolutions"):
        lags, *sends_home = call(
            backward_kernel,
            [((2, length, cols), F32)] + [((rows, width), F32), wide_bf16] * fast + [((2, rows, cols), BF16)] * seq,
            (
                *parts_in,
                filter_spectra,
                first_conv,
                value_spectra,
                mixed_spectra,
                fwd_high,
                fwd_low,
                inv_high,
            ),
            scratch=[pltpu.VMEM((2, length, cols), F32)] * fast
            + [pltpu.VMEM((length, cols), BF16), pltpu.VMEM((length, cols), F32)],
            flops=8 * table_flops,
            limit=limit,
        )

    if fast:
        def to_core(block):
            return lax.ppermute(block, "dp", [(i, i ^ 1) for i in range(data)])

        def to_chip(block, other):
            pairs = []
            for i in range(data):
                for j in range(seq):
                    pairs.append((i * seq + j, (i ^ (2 * (j ^ other) or 1)) * seq + j))
            return lax.ppermute(block, ("dp", "ctx"), pairs)

        def core_kernel(kept_ref, taken_ref, *outs):
            summed = (kept_ref[...] + taken_ref[...].astype(F32)).astype(BF16)
            for index, out in enumerate(outs):
                out[...] = summed[index * out.shape[0] : (index + 1) * out.shape[0]]

        lag_kept, lag_given, *sends_home = sends_home
        with jax.named_scope("lag_core_sum"):
            (lag_sum,) = call(
                core_kernel, [wide_bf16], (lag_kept, to_core(lag_given)), limit=limit
            )
        lag_term = to_chip(lag_sum, 0)

        def gated_kernel(*refs):
            stays_ref, near_ref, gate_ref, cot_ref, beside_ref, *refs = refs
            kept, given, gated, cots, whole = refs
            here = lax.axis_index("ctx")
            cots[:rows] = cot_ref[...]
            cots[rows:] = beside_ref[:, :width]
            for index, ref in enumerate((stays_ref, near_ref)):
                lanes = pl.ds(index * cols, cols)
                gate = pick_columns(gate_ref, held(here ^ (2 * index)), cols, seq)
                gated[:rows, lanes] = (gate.astype(F32) * ref[0].astype(F32)).astype(BF16)
                gate = columns(beside_ref, width // cols + index, cols)
                gated[rows:, lanes] = (gate.astype(F32) * ref[1].astype(F32)).astype(BF16)
            whole[...] = lax.dot_general(
                gated[...], cots[...], (((0,), (0,)), ((), ())), preferred_element_type=F32
            )
            own_core = lax.rem(lax.axis_index("dp"), 2)
            first = jnp.where(here == 0, 1 - own_core, own_core)
            second = jnp.where(here == 2, 1 - own_core, own_core)
            for out, one, two in ((kept, first, second), (given, 1 - first, 1 - second)):
                piece = whole[pl.ds(pl.multiple_of(one * own_rows, own_rows), own_rows), :]
                out[:own_rows] = piece.astype(out.dtype)
                start = pl.multiple_of(cols + two * own_rows, own_rows)
                out[own_rows:] = whole[pl.ds(start, own_rows), :].astype(out.dtype)

        term_shape = (2 * own_rows, width)
        with jax.named_scope("weight_partial"):
            kept, given = call(
                gated_kernel,
                [(term_shape, F32), (term_shape, BF16)],
                (second_stays, second_near, gate_two[0], grad_out[0], beside_in),
                scratch=[
                    pltpu.VMEM((2 * rows, 2 * cols), BF16),
                    pltpu.VMEM((2 * rows, width), BF16),
                    pltpu.VMEM((2 * cols, width), F32),
                ],
                limit=limit,
            )

        def terms_kernel(kept_ref, taken_ref, stays_ref, near_ref, home_ref, one, two, goes_on):
            core_kernel(kept_ref, taken_ref, one, two)
            goes_on[0] = stays_ref[1]
            goes_on[1] = near_ref[1]
            goes_on[2:] = home_ref[...]

        with jax.named_scope("core_sum"):
            *sends, goes_on = call(
                terms_kernel,
                [((own_rows, width), BF16)] * 2 + [((4, rows, cols), BF16)],
                (kept, to_core(given), second_stays, second_near, sends_home[1]),
                limit=limit,
            )
        second_far = lax.ppermute(goes_on, "ctx", across(1))

        chip_terms = [to_chip(sends[0], 0), to_chip(sends[1], 2)]

        home = [lax.ppermute(sends_home[far], "ctx", across(far)) for far in (2, 3)]

        def place_kernel(lag_ref, one, two, *refs):
            outs, total = refs[:-1], refs[-1]
            total[...] = one[...].astype(F32) + two[...].astype(F32)
            for step, out in enumerate(outs):
                out[:own_rows] = pick_columns(total, ahead(step), cols, seq).astype(out.dtype)
                out[own_rows:] = pick_columns(lag_ref, ahead(step), cols, seq).astype(out.dtype)

        small = (own_rows + rows, cols)
        with jax.named_scope("chip_sum"):
            sends = call(
                place_kernel,
                [(small, F32)] + [(small, BF16)] * (seq - 1),
                (lag_term, *chip_terms),
                scratch=[pltpu.VMEM((own_rows, width), F32)],
            )
        last_terms = around(sends)

        def mixed_kernel(*refs):
            parts, (gate_ref, weight_ref, cot_ref, mixed_ref, out, second) = refs[:3], refs[3:]
            here = lax.axis_index("ctx")
            stays_ref, near_ref, far_ref = parts
            put_columns(second, held(here), cols, seq, stays_ref[0])
            put_columns(second, held(here ^ 2), cols, seq, near_ref[0])
            put_columns(second, held(here ^ 1), cols, seq, far_ref[0])
            put_columns(second, held(here ^ 3), cols, seq, far_ref[1])
            wide = second[...].astype(F32)
            gated = (gate_ref[...].astype(F32) * wide).astype(BF16)
            mixed_ref[...] = mxu(gated, weight_ref[...]).astype(BF16)
            out[...] = (grad_gated(cot_ref, weight_ref) * wide).astype(BF16)

        with jax.named_scope("mixed"):
            mixed, grad_gate_two = call(
                mixed_kernel,
                [wide_bf16, wide_bf16],
                (second_stays, second_near, second_far, gate_two[0], out_weight, grad_out[0]),
                scratch=[pltpu.VMEM((rows, width), BF16)],
                flops=4 * rows * width * width,
                limit=limit,
            )

        def final_kernel(*refs):
            arrived, parts, refs = refs[:seq], refs[seq : 2 * seq], refs[2 * seq :]
            filter_ref, weight_ref, gate_ref, value_ref = refs
            for part, (far, first) in zip(parts, ((0, 0), (1, 2), (2, 0), (3, 0))):
                place = held(lax.axis_index("ctx") ^ far)
                put_columns(gate_ref, place, cols, seq, part[first])
                put_columns(value_ref, place, cols, seq, part[first + 1])
            total = arrived[0][...]
            for part in arrived[1:]:
                total = total + part[...].astype(F32)
            total = total * (1.0 / data)
            weight_ref[...] = total[:own_rows]
            turned = total[own_rows:].T
            filter_ref[0] = turned[:fine]
            filter_ref[1] = turned[fine:]

        with jax.named_scope("means"):
            filter_grad, weight_grad, grad_gate_one, grad_value = call(
                final_kernel,
                [((2, fine, rows), F32), ((own_rows, cols), F32), wide_bf16, wide_bf16],
                (*last_terms, sends_home[0], second_far, *home),
            )
        filter_grad = jnp.swapaxes(filter_grad, 1, 2)
        return (
            mixed[None],
            grad_value[None],
            grad_gate_one[None],
            grad_gate_two[None],
            filter_grad,
            weight_grad,
        )

    def gated_kernel(*refs):
        parts, (gate_ref, cot_ref, second_ref, gated_ref, weight_ref) = refs[:seq], refs[seq:]
        for step, part in enumerate(parts):
            put_columns(second_ref, held(behind(step)), cols, seq, part[0])
        gated = (gate_ref[...].astype(F32) * second_ref[...].astype(F32)).astype(BF16)
        gated_ref[...] = gated
        weight_ref[...] = lax.dot_general(
            gated, cot_ref[...], (((0,), (0,)), ((), ())), preferred_element_type=F32
        )

    with jax.named_scope("weight_partial"):
        second_conv, gated, weight_part = call(
            gated_kernel,
            [wide_bf16, wide_bf16, ((width, width), F32)],
            (*second_parts, gate_two[0], grad_out[0]),
            flops=2 * rows * width * width,
            limit=limit,
        )

    core = lax.rem(lax.axis_index("dp"), 2)
    lag_terms = lags.reshape(2, seq, rows, per_ctx, fine).transpose(1, 3, 2, 0, 4)
    lag_rows = rows * 2 * fine // width
    terms = jnp.concatenate(
        [
            weight_part.reshape(data, own_rows, width),
            lag_terms.reshape(data, lag_rows, width),
        ],
        axis=1,
    )
    by_core = terms.reshape(chips, 2, *terms.shape[1:])
    kept = lax.dynamic_index_in_dim(by_core, core, 1, keepdims=False)
    given = lax.dynamic_index_in_dim(by_core, 1 - core, 1, keepdims=False).astype(BF16)
    given, kept = (a.reshape(-1, width) for a in (given, kept))
    taken = lax.ppermute(given, "dp", [(i, i ^ 1) for i in range(data)])
    term_rows = own_rows + lag_rows

    def chip_kernel(kept_ref, taken_ref, own, *outs):
        place = lax.div(lax.axis_index("dp"), 2)

        def summed(index):
            start = pl.multiple_of(index * term_rows, term_rows)
            taken = taken_ref[pl.ds(start, term_rows), :]
            return kept_ref[pl.ds(start, term_rows), :] + taken.astype(F32)

        own[...] = summed(place)
        for step in range(1, chips):
            outs[step - 1][...] = summed(place ^ step).astype(BF16)

    term = (term_rows, width)
    with jax.named_scope("core_sum"):
        total, *sends = call(
            chip_kernel,
            [(term, F32)] + [(term, BF16)] * (chips - 1),
            (kept, taken),
            limit=limit,
        )
    for step in range(1, chips):
        pairs = [(i, i ^ (2 * step)) for i in range(data)]
        total = total + lax.ppermute(sends[step - 1], "dp", pairs).astype(F32)

    def mixed_kernel(gated_ref, weight_ref, cot_ref, second_ref, mixed_ref, gate_ref):
        mixed_ref[...] = mxu(gated_ref[...], weight_ref[...]).astype(BF16)
        grad = grad_gated(cot_ref, weight_ref)
        gate_ref[...] = (grad * second_ref[...].astype(F32)).astype(BF16)

    with jax.named_scope("mixed"):
        mixed, grad_gate_two = call(
            mixed_kernel,
            [wide_bf16, wide_bf16],
            (gated, out_weight, grad_out[0], second_conv),
            flops=4 * rows * width * width,
            limit=limit,
        )
    home = around(sends_home)

    weight_blocks = total[:own_rows].reshape(own_rows, seq, cols)
    sends = [
        lax.dynamic_index_in_dim(weight_blocks, ahead(step), 1, keepdims=False)
        for step in range(seq)
    ]
    last_terms = around(sends[:1] + [part.astype(BF16) for part in sends[1:]])
    lag_sum = total[own_rows:].reshape(rows, 2 * fine).astype(BF16)
    pairs = []
    for i in range(data):
        for j in range(seq):
            pairs.append((i * seq + j, (per_ctx * j + i % per_ctx) * seq + i // per_ctx))
    lag_own = lax.ppermute(lag_sum, ("dp", "ctx"), pairs)

    def unpack_kernel(*refs):
        parts, (gate_ref, value_ref) = refs[:-2], refs[-2:]
        for step, part in enumerate(parts):
            put_columns(gate_ref, held(behind(step)), cols, seq, part[0])
            put_columns(value_ref, held(behind(step)), cols, seq, part[1])

    with jax.named_scope("unpack_results"):
        grad_gate_one, grad_value = call(unpack_kernel, [wide_bf16, wide_bf16], home)
    filter_grad = lag_own.reshape(rows, 2, fine).transpose(1, 0, 2).astype(F32) / data
    weight_grad = sum(part.astype(F32) for part in last_terms) / data
    return (
        mixed[None],
        grad_value[None],
        grad_gate_one[None],
        grad_gate_two[None],
        filter_grad,
        weight_grad,
    )


def solution(mesh):
    stream = P("dp", "ctx", None)
    return jax.shard_map(
        on_device,
        mesh=mesh,
        in_specs=(stream, stream, stream, P(), P(), stream),
        out_specs=(stream, stream, stream, stream, P(None, "ctx", "dp"), P("dp", "ctx")),
        check_vma=False,
    )
```

```python
import functools
import math

import jax
import jax.numpy as jnp
import ml_dtypes
import numpy as np
from jax import lax
from jax.experimental import pallas as pl
from jax.experimental.pallas import tpu as pltpu
from jax.sharding import PartitionSpec as P

F32 = jnp.float32
BF16 = jnp.bfloat16


def split_table(table):
    high = table.astype(ml_dtypes.bfloat16)
    low = (table - high.astype(np.float64)).astype(ml_dtypes.bfloat16)
    return jnp.asarray(high), jnp.asarray(low)


@functools.lru_cache(maxsize=None)
def table_values(block):
    period = 2 * block
    bins = np.arange(block)
    radians = (bins[:, None] * bins[None, :] % period) * (2.0 * math.pi / period)
    cosines, sines = np.cos(radians), -np.sin(radians)
    sines[0] = np.where(bins % 2 == 0, 1.0, -1.0)
    forward = np.concatenate([cosines, sines], axis=0)
    weights = np.full((period,), 2.0 / period)
    weights[0] = weights[block] = 1.0 / period
    return forward, forward.T * weights[None, :]


def mxu(left, right):
    return jnp.dot(left, right, preferred_element_type=F32)


def beside(stream, block):
    return jnp.concatenate(
        [stream[i : i + block] for i in range(0, stream.shape[0], block)], axis=1
    )


def to_spectra(high, low, stream):
    blocks = beside(stream, high.shape[1])
    return mxu(high[...], blocks) + mxu(low[...], blocks)


def from_spectra(high, spectra):
    return mxu(high[...], spectra.astype(BF16))


def parity(shape):
    row = lax.broadcasted_iota(jnp.int32, shape, 0)
    return jnp.where(row % 2 == 0, 1.0, -1.0)


def with_previous(spectra, cols):
    sign = parity((spectra.shape[0], cols))
    out = [spectra[:, :cols]]
    for i in range(cols, spectra.shape[1], cols):
        out.append(spectra[:, i : i + cols] + sign * spectra[:, i - cols : i])
    return jnp.concatenate(out, axis=1)


def sum_of_products(terms, conj_left):
    half = terms[0][0].shape[0] // 2
    border = lax.broadcasted_iota(jnp.int32, (half, terms[0][0].shape[1]), 0) == 0
    straight = cross = imag = 0.0
    for left, right in terms:
        left_re, left_im, right_re, right_im = left[:half], left[half:], right[:half], right[half:]
        straight += left_re * right_re
        cross += left_im * right_im
        if conj_left:
            imag += left_re * right_im - left_im * right_re
        else:
            imag += left_re * right_im + left_im * right_re
    inner = jnp.where(border, 0.0, cross)
    real = straight + inner if conj_left else straight - inner
    return jnp.concatenate([real, jnp.where(border, cross, imag)], axis=0)


def columns(ref, index, cols):
    return ref[:, index * cols : (index + 1) * cols]


def causal_product(filt, spectra, cols):
    count = spectra.shape[1] // cols
    out = []
    for i in range(count):
        terms = [(columns(filt, i - a, cols), columns(spectra, a, cols)) for a in range(i + 1)]
        out.append(sum_of_products(terms, False))
    return jnp.concatenate(out, axis=1)


def anti_product(left, spectra, cols):
    count = spectra.shape[1] // cols
    out = []
    for i in range(count):
        terms = [
            (columns(left, a - i, cols), columns(spectra, a, cols)) for a in range(i, count)
        ]
        out.append(sum_of_products(terms, True))
    return jnp.concatenate(out, axis=1)


def pick_columns(ref, index, width, count):
    if width % 128 == 0:
        return ref[:, pl.ds(pl.multiple_of(index * width, width), width)]
    whole = ref[...]
    out = whole[:, :width]
    for other in range(1, count):
        out = jnp.where(index == other, whole[:, other * width : (other + 1) * width], out)
    return out


def put_columns(ref, index, width, count, block):
    if width % 128 == 0:
        ref[:, pl.ds(pl.multiple_of(index * width, width), width)] = block
        return
    for other in range(count):

        @pl.when(index == other)
        def _():
            ref[:, other * width : (other + 1) * width] = block


def pick_rows(ref, index, rows):
    return ref[pl.ds(pl.multiple_of(index * rows, rows), rows), :]


def put_rows(ref, index, rows, block):
    ref[pl.ds(pl.multiple_of(index * rows, rows), rows), :] = block


def call(kernel, outs, args, scratch=(), flops=0, limit=16, in_hbm=False):
    vmem = pl.BlockSpec(memory_space=pltpu.VMEM)
    source = pl.BlockSpec(memory_space=pltpu.HBM) if in_hbm else vmem
    total = sum(math.prod(a.shape) * a.dtype.itemsize for a in args)
    return pl.pallas_call(
        kernel,
        out_shape=[jax.ShapeDtypeStruct(shape, dtype) for shape, dtype in outs],
        in_specs=[source] * len(args),
        out_specs=[vmem] * len(outs),
        scratch_shapes=list(scratch),
        compiler_params=pltpu.CompilerParams(vmem_limit_bytes=int(limit * 2**20)),
        cost_estimate=pl.CostEstimate(flops=flops, bytes_accessed=total, transcendentals=0),
    )(*args)


def on_device(value, gate_one, gate_two, filters, out_weight, grad_out):
    rows, width = value.shape[1:]
    seq = lax.axis_size("ctx")
    data = lax.axis_size("dp")
    length = rows * seq
    cols = width // seq
    block = math.gcd(length, 256)
    per_ctx = data // seq
    fine = cols // per_ctx
    chips = data // 2
    own_rows = width // data
    fast = cols == 128 and per_ctx == 2 and chips == seq == 4
    limit = 16 if length <= 512 else 48
    load_limit = 53.5
    forward, inverse = table_values(block)
    (fwd_high, fwd_low), (inv_high, _) = split_table(forward), split_table(inverse)
    spectra_shape = (2 * block, length // block * cols)
    table_flops = 4 * block * length * cols

    def ahead(step):
        return lax.rem(lax.axis_index("ctx") + step, seq)

    def behind(step):
        return lax.rem(lax.axis_index("ctx") + seq - step, seq)

    def held(place):
        return place ^ lax.div(lax.axis_index("dp"), 2) if fast else place

    def around(blocks):
        out = [blocks[0]]
        for step in range(1, seq):
            pairs = [(i, (i + step) % seq) for i in range(seq)]
            out.append(lax.ppermute(blocks[step], "ctx", pairs))
        return out

    def grad_gated(cot_ref, weight_ref):
        return lax.dot_general(
            cot_ref[...], weight_ref[...], (((1,), (1,)), ((), ())), preferred_element_type=F32
        )

    def across(far):
        return [(i, i ^ far) for i in range(seq)]

    in_order = (0, 3, 1, 2) if fast else range(seq)

    def sent(step):
        return lax.axis_index("ctx") ^ step if fast else ahead(step)

    def came(step):
        return lax.axis_index("ctx") ^ step if fast else behind(step)

    def load_kernel(*refs):
        value_ref, gate_ref, cot_arg, weight_arg, gate_arg = refs[:5]
        outs, refs = refs[5 : 5 + seq], refs[5 + seq :]
        cot_ref, weight_ref, gate_two_ref, second, whole, sems = refs
        started = [
            (cot_arg.at[0], cot_ref),
            (weight_arg, weight_ref),
            (gate_arg.at[0], gate_two_ref),
        ]
        started.append((value_ref.at[0], whole.at[0]))
        started.append((gate_ref.at[0], whole.at[1]))
        started = [
            pltpu.make_async_copy(source, target, sems.at[index])
            for index, (source, target) in enumerate(started)
        ]
        for copy in started:
            copy.start()
        for copy in started[:3]:
            copy.wait()
        second[...] = grad_gated(cot_ref, weight_ref) * gate_two_ref[...].astype(F32)
        for step, out in enumerate(outs):
            out[2] = pick_columns(second, held(sent(step)), cols, seq).astype(BF16)
        for copy in started[3:]:
            copy.wait()
        for step, out in enumerate(outs):
            for index in range(2):
                out[index] = pick_columns(whole.at[index], held(sent(step)), cols, seq)

    triple = ((3, rows, cols), BF16)
    wide_bf16 = ((rows, width), BF16)
    with jax.named_scope("load"):
        sends = call(
            load_kernel,
            [triple] * seq,
            (value, gate_one, grad_out, out_weight, gate_two),
            scratch=[
                pltpu.VMEM((rows, width), BF16),
                pltpu.VMEM((width, width), BF16),
                pltpu.VMEM((rows, width), BF16),
                pltpu.VMEM((rows, width), F32),
                pltpu.VMEM((2, rows, width), BF16),
                pltpu.SemaphoreType.DMA((5,)),
            ],
            flops=2 * rows * width * width,
            in_hbm=True,
            limit=load_limit,
        )
    if fast:
        parts_in = [sends[0]] + [lax.ppermute(sends[far], "ctx", across(far)) for far in range(1, seq)]
    else:
        parts_in = around(sends)

    def filter_kernel(filters_ref, high, low, cot_ref, gate_ref, out, *beside):
        if fast:
            beside[0][:, :width] = cot_ref[...]
            for index, far in enumerate((1, 3)):
                piece = pick_columns(gate_ref, held(lax.axis_index("ctx") ^ far), cols, seq)
                beside[0][:, width + index * cols : width + (index + 1) * cols] = piece
        for index in range(2):
            out[index] = with_previous(to_spectra(high, low, filters_ref[index]), cols)

    with jax.named_scope("filter_spectra"):
        own_filters = lax.dynamic_slice_in_dim(filters, held(lax.axis_index("ctx")) * cols, cols, 2)
        filter_spectra, *sends = call(
            filter_kernel,
            [((2, *spectra_shape), F32)] + [((rows, width + 2 * cols), BF16)] * fast,
            (own_filters, fwd_high, fwd_low, grad_out[0], gate_two[0]),
            flops=4 * table_flops,
            limit=limit,
        )
    if fast:
        beside_in = lax.ppermute(sends[0], "ctx", across(1))

    def put_result(outs, index, total, arrays):
        if len(outs) == seq:
            for step, out in enumerate(outs):
                place = lax.axis_index("ctx") ^ step if fast else ahead(step)
                out[index] = pick_rows(total, place, rows).astype(BF16)
            return
        for far in range(4):
            piece = pick_rows(total, lax.axis_index("ctx") ^ far, rows).astype(BF16)
            outs[far // 2][far % 2 * arrays + index] = piece

    def forward_kernel(*refs):
        parts, refs = refs[:seq], refs[seq:]
        filt, high, low, back, first_ref, value_spec, mixed_spec = refs[:7]
        outs, (stream, second) = refs[7:-2], refs[-2:]
        for step, part in zip(in_order, parts):
            put_rows(stream, came(step), rows, part[0])
        spectra = to_spectra(high, low, stream[...])
        value_spec[...] = with_previous(spectra, cols)
        conv = from_spectra(back, causal_product(filt[0], spectra, cols))
        for i in range(length // block):
            first_ref[i * block : (i + 1) * block] = columns(conv, i, cols)
        for step, part in zip(in_order, parts):
            gated = part[1].astype(F32) * pick_rows(first_ref, came(step), rows)
            put_rows(stream, came(step), rows, gated.astype(BF16))
        spectra = to_spectra(high, low, stream[...])
        mixed_spec[...] = with_previous(spectra, cols)
        conv = from_spectra(back, causal_product(filt[1], spectra, cols))
        for i in range(length // block):
            second[i * block : (i + 1) * block] = columns(conv, i, cols)
        put_result(outs, 0, second, 1)

    with jax.named_scope("forward_convolutions"):
        first_conv, value_spectra, mixed_spectra, *sends = call(
            forward_kernel,
            [((length, cols), F32), (spectra_shape, F32), (spectra_shape, F32)]
            + ([((2, rows, cols), BF16)] * 2 if fast else [((1, rows, cols), BF16)] * seq),
            (*(parts_in[step] for step in in_order), filter_spectra, fwd_high, fwd_low, inv_high),
            scratch=[pltpu.VMEM((length, cols), BF16), pltpu.VMEM((length, cols), F32)],
            flops=6 * table_flops,
            limit=limit,
        )
    if fast:
        second_stays, goes = sends
        second_near = lax.ppermute(goes, "ctx", across(2))
    else:
        second_parts = around(sends)

    def backward_kernel(*refs):
        parts, refs = refs[:seq], refs[seq:]
        filt, first_ref, value_spec, mixed_spec, high, low, back = refs[:7]
        lags, *outs, stream, total = refs[7:]
        if fast:
            lag_kept, lag_given, *outs, packed = outs
        count = length // block
        for step, part in zip(in_order, parts):
            put_rows(stream, came(step), rows, part[2])

        def both(left, other):
            spectra = to_spectra(high, low, stream[...])
            grads = anti_product(left, spectra, cols)
            terms = anti_product(other, spectra, cols)
            return from_spectra(back, jnp.concatenate([grads, terms], axis=1))

        def put_lags(index, out):
            for i in range(count):
                piece = columns(out, count + i, cols)
                lags[index, i * block : (i + 1) * block] = piece

        out = both(filt[1], mixed_spec[...])
        for i in range(count):
            total[i * block : (i + 1) * block] = columns(out, i, cols)
        put_lags(1, out)
        for step, part in zip(in_order, parts):
            grad = pick_rows(total, came(step), rows)
            put_rows(stream, came(step), rows, (grad * part[1].astype(F32)).astype(BF16))
        total[...] = total[...] * first_ref[...]
        put_result(outs, 0, total, 2)
        out = both(filt[0], value_spec[...])
        for i in range(count):
            total[i * block : (i + 1) * block] = columns(out, i, cols)
        put_result(outs, 1, total, 2)
        put_lags(0, out)
        if fast:
            here, own_core = lax.axis_index("ctx"), lax.rem(lax.axis_index("dp"), 2)
            half = jnp.where(here == 0, 1 - own_core, own_core)
            lower = lax.broadcasted_iota(jnp.int32, (length, cols), 1) < fine
            packed[0] = jnp.where(lower, lags[0], pltpu.roll(lags[1], fine, axis=1))
            packed[1] = jnp.where(lower, pltpu.roll(lags[0], fine, axis=1), lags[1])
            for index in range(seq):
                lanes = pl.ds(index * cols, cols)
                lag_kept[:, lanes] = packed[half, index * rows : (index + 1) * rows]
                given = packed[1 - half, index * rows : (index + 1) * rows]
                lag_given[:, lanes] = given.astype(BF16)

    with jax.named_scope("backward_convolutions"):
        lags, *sends_home = call(
            backward_kernel,
            [((2, length, cols), F32)] + [((rows, width), F32), wide_bf16] * fast + [((2, rows, cols), BF16)] * seq,
            (
                *(parts_in[step] for step in in_order),
                filter_spectra,
                first_conv,
                value_spectra,
                mixed_spectra,
                fwd_high,
                fwd_low,
                inv_high,
            ),
            scratch=[pltpu.VMEM((2, length, cols), F32)] * fast
            + [pltpu.VMEM((length, cols), BF16), pltpu.VMEM((length, cols), F32)],
            flops=8 * table_flops,
            limit=limit,
        )

    if fast:
        def to_core(block):
            return lax.ppermute(block, "dp", [(i, i ^ 1) for i in range(data)])

        def to_chip(block, other):
            pairs = []
            for i in range(data):
                for j in range(seq):
                    pairs.append((i * seq + j, (i ^ (2 * (j ^ other) or 1)) * seq + j))
            return lax.ppermute(block, ("dp", "ctx"), pairs)

        def core_kernel(kept_ref, taken_ref, *outs):
            summed = (kept_ref[...] + taken_ref[...].astype(F32)).astype(BF16)
            for index, out in enumerate(outs):
                out[...] = summed[index * out.shape[0] : (index + 1) * out.shape[0]]

        lag_kept, lag_given, *sends_home = sends_home
        with jax.named_scope("lag_core_sum"):
            (lag_sum,) = call(
                core_kernel, [wide_bf16], (lag_kept, to_core(lag_given)), limit=limit
            )
        lag_term = to_chip(lag_sum, 0)

        def gated_kernel(*refs):
            stays_ref, near_ref, gate_ref, cot_ref, beside_ref, *refs = refs
            kept, given, gated, cots, whole = refs
            here = lax.axis_index("ctx")
            cots[:rows] = cot_ref[...]
            cots[rows:] = beside_ref[:, :width]
            for index, ref in enumerate((stays_ref, near_ref)):
                lanes = pl.ds(index * cols, cols)
                gate = pick_columns(gate_ref, held(here ^ (2 * index)), cols, seq)
                gated[:rows, lanes] = (gate.astype(F32) * ref[0].astype(F32)).astype(BF16)
                gate = columns(beside_ref, width // cols + index, cols)
                gated[rows:, lanes] = (gate.astype(F32) * ref[1].astype(F32)).astype(BF16)
            whole[...] = lax.dot_general(
                gated[...], cots[...], (((0,), (0,)), ((), ())), preferred_element_type=F32
            )
            own_core = lax.rem(lax.axis_index("dp"), 2)
            first = jnp.where(here == 0, 1 - own_core, own_core)
            second = jnp.where(here == 2, 1 - own_core, own_core)
            for out, one, two in ((kept, first, second), (given, 1 - first, 1 - second)):
                piece = whole[pl.ds(pl.multiple_of(one * own_rows, own_rows), own_rows), :]
                out[:own_rows] = piece.astype(out.dtype)
                start = pl.multiple_of(cols + two * own_rows, own_rows)
                out[own_rows:] = whole[pl.ds(start, own_rows), :].astype(out.dtype)

        term_shape = (2 * own_rows, width)
        with jax.named_scope("weight_partial"):
            kept, given = call(
                gated_kernel,
                [(term_shape, F32), (term_shape, BF16)],
                (second_stays, second_near, gate_two[0], grad_out[0], beside_in),
                scratch=[
                    pltpu.VMEM((2 * rows, 2 * cols), BF16),
                    pltpu.VMEM((2 * rows, width), BF16),
                    pltpu.VMEM((2 * cols, width), F32),
                ],
                limit=limit,
            )

        def terms_kernel(kept_ref, taken_ref, stays_ref, near_ref, home_ref, one, two, goes_on):
            core_kernel(kept_ref, taken_ref, one, two)
            goes_on[0] = stays_ref[1]
            goes_on[1] = near_ref[1]
            goes_on[2:] = home_ref[...]

        with jax.named_scope("core_sum"):
            *sends, goes_on = call(
                terms_kernel,
                [((own_rows, width), BF16)] * 2 + [((4, rows, cols), BF16)],
                (kept, to_core(given), second_stays, second_near, sends_home[1]),
                limit=limit,
            )
        second_far = lax.ppermute(goes_on, "ctx", across(1))

        chip_terms = [to_chip(sends[0], 0), to_chip(sends[1], 2)]

        home = [lax.ppermute(sends_home[far], "ctx", across(far)) for far in (2, 3)]

        def place_kernel(lag_ref, one, two, *refs):
            outs, total = refs[:-1], refs[-1]
            total[...] = one[...].astype(F32) + two[...].astype(F32)
            for step, out in enumerate(outs):
                out[:own_rows] = pick_columns(total, ahead(step), cols, seq).astype(out.dtype)
                out[own_rows:] = pick_columns(lag_ref, ahead(step), cols, seq).astype(out.dtype)

        small = (own_rows + rows, cols)
        with jax.named_scope("chip_sum"):
            sends = call(
                place_kernel,
                [(small, F32)] + [(small, BF16)] * (seq - 1),
                (lag_term, *chip_terms),
                scratch=[pltpu.VMEM((own_rows, width), F32)],
            )
        last_terms = around(sends)

        def mixed_kernel(*refs):
            parts, (gate_ref, weight_ref, cot_ref, mixed_ref, out, second) = refs[:3], refs[3:]
            here = lax.axis_index("ctx")
            stays_ref, near_ref, far_ref = parts
            put_columns(second, held(here), cols, seq, stays_ref[0])
            put_columns(second, held(here ^ 2), cols, seq, near_ref[0])
            put_columns(second, held(here ^ 1), cols, seq, far_ref[0])
            put_columns(second, held(here ^ 3), cols, seq, far_ref[1])
            wide = second[...].astype(F32)
            gated = (gate_ref[...].astype(F32) * wide).astype(BF16)
            mixed_ref[...] = mxu(gated, weight_ref[...]).astype(BF16)
            out[...] = (grad_gated(cot_ref, weight_ref) * wide).astype(BF16)

        with jax.named_scope("mixed"):
            mixed, grad_gate_two = call(
                mixed_kernel,
                [wide_bf16, wide_bf16],
                (second_stays, second_near, second_far, gate_two[0], out_weight, grad_out[0]),
                scratch=[pltpu.VMEM((rows, width), BF16)],
                flops=4 * rows * width * width,
                limit=limit,
            )

        def final_kernel(*refs):
            arrived, parts, refs = refs[:seq], refs[seq : 2 * seq], refs[2 * seq :]
            filter_ref, weight_ref, gate_ref, value_ref = refs
            for part, (far, first) in zip(parts, ((0, 0), (1, 2), (2, 0), (3, 0))):
                place = held(lax.axis_index("ctx") ^ far)
                put_columns(gate_ref, place, cols, seq, part[first])
                put_columns(value_ref, place, cols, seq, part[first + 1])
            total = arrived[0][...]
            for part in arrived[1:]:
                total = total + part[...].astype(F32)
            total = total * (1.0 / data)
            weight_ref[...] = total[:own_rows]
            turned = total[own_rows:].T
            filter_ref[0] = turned[:fine]
            filter_ref[1] = turned[fine:]

        with jax.named_scope("means"):
            filter_grad, weight_grad, grad_gate_one, grad_value = call(
                final_kernel,
                [((2, fine, rows), F32), ((own_rows, cols), F32), wide_bf16, wide_bf16],
                (*last_terms, sends_home[0], second_far, *home),
            )
        filter_grad = jnp.swapaxes(filter_grad, 1, 2)
        return (
            mixed[None],
            grad_value[None],
            grad_gate_one[None],
            grad_gate_two[None],
            filter_grad,
            weight_grad,
        )

    def gated_kernel(*refs):
        parts, (gate_ref, cot_ref, second_ref, gated_ref, weight_ref) = refs[:seq], refs[seq:]
        for step, part in enumerate(parts):
            put_columns(second_ref, held(behind(step)), cols, seq, part[0])
        gated = (gate_ref[...].astype(F32) * second_ref[...].astype(F32)).astype(BF16)
        gated_ref[...] = gated
        weight_ref[...] = lax.dot_general(
            gated, cot_ref[...], (((0,), (0,)), ((), ())), preferred_element_type=F32
        )

    with jax.named_scope("weight_partial"):
        second_conv, gated, weight_part = call(
            gated_kernel,
            [wide_bf16, wide_bf16, ((width, width), F32)],
            (*second_parts, gate_two[0], grad_out[0]),
            flops=2 * rows * width * width,
            limit=limit,
        )

    core = lax.rem(lax.axis_index("dp"), 2)
    lag_terms = lags.reshape(2, seq, rows, per_ctx, fine).transpose(1, 3, 2, 0, 4)
    lag_rows = rows * 2 * fine // width
    terms = jnp.concatenate(
        [
            weight_part.reshape(data, own_rows, width),
            lag_terms.reshape(data, lag_rows, width),
        ],
        axis=1,
    )
    by_core = terms.reshape(chips, 2, *terms.shape[1:])
    kept = lax.dynamic_index_in_dim(by_core, core, 1, keepdims=False)
    given = lax.dynamic_index_in_dim(by_core, 1 - core, 1, keepdims=False).astype(BF16)
    given, kept = (a.reshape(-1, width) for a in (given, kept))
    taken = lax.ppermute(given, "dp", [(i, i ^ 1) for i in range(data)])
    term_rows = own_rows + lag_rows

    def chip_kernel(kept_ref, taken_ref, own, *outs):
        place = lax.div(lax.axis_index("dp"), 2)

        def summed(index):
            start = pl.multiple_of(index * term_rows, term_rows)
            taken = taken_ref[pl.ds(start, term_rows), :]
            return kept_ref[pl.ds(start, term_rows), :] + taken.astype(F32)

        own[...] = summed(place)
        for step in range(1, chips):
            outs[step - 1][...] = summed(place ^ step).astype(BF16)

    term = (term_rows, width)
    with jax.named_scope("core_sum"):
        total, *sends = call(
            chip_kernel,
            [(term, F32)] + [(term, BF16)] * (chips - 1),
            (kept, taken),
            limit=limit,
        )
    for step in range(1, chips):
        pairs = [(i, i ^ (2 * step)) for i in range(data)]
        total = total + lax.ppermute(sends[step - 1], "dp", pairs).astype(F32)

    def mixed_kernel(gated_ref, weight_ref, cot_ref, second_ref, mixed_ref, gate_ref):
        mixed_ref[...] = mxu(gated_ref[...], weight_ref[...]).astype(BF16)
        grad = grad_gated(cot_ref, weight_ref)
        gate_ref[...] = (grad * second_ref[...].astype(F32)).astype(BF16)

    with jax.named_scope("mixed"):
        mixed, grad_gate_two = call(
            mixed_kernel,
            [wide_bf16, wide_bf16],
            (gated, out_weight, grad_out[0], second_conv),
            flops=4 * rows * width * width,
            limit=limit,
        )
    home = around(sends_home)

    weight_blocks = total[:own_rows].reshape(own_rows, seq, cols)
    sends = [
        lax.dynamic_index_in_dim(weight_blocks, ahead(step), 1, keepdims=False)
        for step in range(seq)
    ]
    last_terms = around(sends[:1] + [part.astype(BF16) for part in sends[1:]])
    lag_sum = total[own_rows:].reshape(rows, 2 * fine).astype(BF16)
    pairs = []
    for i in range(data):
        for j in range(seq):
            pairs.append((i * seq + j, (per_ctx * j + i % per_ctx) * seq + i // per_ctx))
    lag_own = lax.ppermute(lag_sum, ("dp", "ctx"), pairs)

    def unpack_kernel(*refs):
        parts, (gate_ref, value_ref) = refs[:-2], refs[-2:]
        for step, part in enumerate(parts):
            put_columns(gate_ref, held(behind(step)), cols, seq, part[0])
            put_columns(value_ref, held(behind(step)), cols, seq, part[1])

    with jax.named_scope("unpack_results"):
        grad_gate_one, grad_value = call(unpack_kernel, [wide_bf16, wide_bf16], home)
    filter_grad = lag_own.reshape(rows, 2, fine).transpose(1, 0, 2).astype(F32) / data
    weight_grad = sum(part.astype(F32) for part in last_terms) / data
    return (
        mixed[None],
        grad_value[None],
        grad_gate_one[None],
        grad_gate_two[None],
        filter_grad,
        weight_grad,
    )


def solution(mesh):
    stream = P("dp", "ctx", None)
    return jax.shard_map(
        on_device,
        mesh=mesh,
        in_specs=(stream, stream, stream, P(), P(), stream),
        out_specs=(stream, stream, stream, stream, P(None, "ctx", "dp"), P("dp", "ctx")),
        check_vma=False,
    )
```

```python
import functools
import math

import jax
import jax.numpy as jnp
import ml_dtypes
import numpy as np
from jax import lax
from jax.experimental import pallas as pl
from jax.experimental.pallas import tpu as pltpu
from jax.sharding import PartitionSpec as P

F32 = jnp.float32
BF16 = jnp.bfloat16


def split_table(table):
    high = table.astype(ml_dtypes.bfloat16)
    low = (table - high.astype(np.float64)).astype(ml_dtypes.bfloat16)
    return jnp.asarray(high), jnp.asarray(low)


@functools.lru_cache(maxsize=None)
def table_values(block):
    period = 2 * block
    bins = np.arange(block)
    radians = (bins[:, None] * bins[None, :] % period) * (2.0 * math.pi / period)
    cosines, sines = np.cos(radians), -np.sin(radians)
    sines[0] = np.where(bins % 2 == 0, 1.0, -1.0)
    forward = np.concatenate([cosines, sines], axis=0)
    weights = np.full((period,), 2.0 / period)
    weights[0] = weights[block] = 1.0 / period
    return forward, forward.T * weights[None, :]


def mxu(left, right):
    return jnp.dot(left, right, preferred_element_type=F32)


def beside(stream, block):
    return jnp.concatenate(
        [stream[i : i + block] for i in range(0, stream.shape[0], block)], axis=1
    )


def to_spectra(high, low, stream):
    blocks = beside(stream, high.shape[1])
    return mxu(high[...], blocks) + mxu(low[...], blocks)


def from_spectra(high, spectra):
    return mxu(high[...], spectra.astype(BF16))


def parity(shape):
    row = lax.broadcasted_iota(jnp.int32, shape, 0)
    return jnp.where(row % 2 == 0, 1.0, -1.0)


def with_previous(spectra, cols):
    sign = parity((spectra.shape[0], cols))
    out = [spectra[:, :cols]]
    for i in range(cols, spectra.shape[1], cols):
        out.append(spectra[:, i : i + cols] + sign * spectra[:, i - cols : i])
    return jnp.concatenate(out, axis=1)


def sum_of_products(terms, conj_left):
    half = terms[0][0].shape[0] // 2
    border = lax.broadcasted_iota(jnp.int32, (half, terms[0][0].shape[1]), 0) == 0
    straight = cross = imag = 0.0
    for left, right in terms:
        left_re, left_im, right_re, right_im = left[:half], left[half:], right[:half], right[half:]
        straight += left_re * right_re
        cross += left_im * right_im
        if conj_left:
            imag += left_re * right_im - left_im * right_re
        else:
            imag += left_re * right_im + left_im * right_re
    inner = jnp.where(border, 0.0, cross)
    real = straight + inner if conj_left else straight - inner
    return jnp.concatenate([real, jnp.where(border, cross, imag)], axis=0)


def columns(ref, index, cols):
    return ref[:, index * cols : (index + 1) * cols]


def causal_product(filt, spectra, cols):
    count = spectra.shape[1] // cols
    out = []
    for i in range(count):
        terms = [(columns(filt, i - a, cols), columns(spectra, a, cols)) for a in range(i + 1)]
        out.append(sum_of_products(terms, False))
    return jnp.concatenate(out, axis=1)


def anti_product(left, spectra, cols):
    count = spectra.shape[1] // cols
    out = []
    for i in range(count):
        terms = [
            (columns(left, a - i, cols), columns(spectra, a, cols)) for a in range(i, count)
        ]
        out.append(sum_of_products(terms, True))
    return jnp.concatenate(out, axis=1)


def pick_columns(ref, index, width, count):
    if width % 128 == 0:
        return ref[:, pl.ds(pl.multiple_of(index * width, width), width)]
    whole = ref[...]
    out = whole[:, :width]
    for other in range(1, count):
        out = jnp.where(index == other, whole[:, other * width : (other + 1) * width], out)
    return out


def put_columns(ref, index, width, count, block):
    if width % 128 == 0:
        ref[:, pl.ds(pl.multiple_of(index * width, width), width)] = block
        return
    for other in range(count):

        @pl.when(index == other)
        def _():
            ref[:, other * width : (other + 1) * width] = block


def pick_rows(ref, index, rows):
    return ref[pl.ds(pl.multiple_of(index * rows, rows), rows), :]


def put_rows(ref, index, rows, block):
    ref[pl.ds(pl.multiple_of(index * rows, rows), rows), :] = block


def call(kernel, outs, args, scratch=(), flops=0, limit=16, in_hbm=False):
    vmem = pl.BlockSpec(memory_space=pltpu.VMEM)
    source = pl.BlockSpec(memory_space=pltpu.HBM) if in_hbm else vmem
    total = sum(math.prod(a.shape) * a.dtype.itemsize for a in args)
    return pl.pallas_call(
        kernel,
        out_shape=[jax.ShapeDtypeStruct(shape, dtype) for shape, dtype in outs],
        in_specs=[source] * len(args),
        out_specs=[vmem] * len(outs),
        scratch_shapes=list(scratch),
        compiler_params=pltpu.CompilerParams(vmem_limit_bytes=int(limit * 2**20)),
        cost_estimate=pl.CostEstimate(flops=flops, bytes_accessed=total, transcendentals=0),
    )(*args)


def on_device(value, gate_one, gate_two, filters, out_weight, grad_out):
    rows, width = value.shape[1:]
    seq = lax.axis_size("ctx")
    data = lax.axis_size("dp")
    length = rows * seq
    cols = width // seq
    block = math.gcd(length, 256)
    per_ctx = data // seq
    fine = cols // per_ctx
    chips = data // 2
    own_rows = width // data
    fast = cols == 128 and per_ctx == 2 and chips == seq == 4
    limit = 16 if length <= 512 else 48
    load_limit = 53.5
    forward, inverse = table_values(block)
    (fwd_high, fwd_low), (inv_high, _) = split_table(forward), split_table(inverse)
    spectra_shape = (2 * block, length // block * cols)
    table_flops = 4 * block * length * cols

    def ahead(step):
        return lax.rem(lax.axis_index("ctx") + step, seq)

    def behind(step):
        return lax.rem(lax.axis_index("ctx") + seq - step, seq)

    def held(place):
        return place ^ lax.div(lax.axis_index("dp"), 2) if fast else place

    def around(blocks):
        out = [blocks[0]]
        for step in range(1, seq):
            pairs = [(i, (i + step) % seq) for i in range(seq)]
            out.append(lax.ppermute(blocks[step], "ctx", pairs))
        return out

    def grad_gated(cot_ref, weight_ref):
        return lax.dot_general(
            cot_ref[...], weight_ref[...], (((1,), (1,)), ((), ())), preferred_element_type=F32
        )

    def across(far):
        return [(i, i ^ far) for i in range(seq)]

    in_order = (0, 3, 1, 2) if fast else range(seq)

    def sent(step):
        return lax.axis_index("ctx") ^ step if fast else ahead(step)

    def came(step):
        return lax.axis_index("ctx") ^ step if fast else behind(step)

    def load_kernel(*refs):
        value_ref, gate_ref, cot_arg, weight_arg, gate_arg = refs[:5]
        outs, refs = refs[5 : 5 + seq], refs[5 + seq :]
        cot_ref, weight_ref, gate_two_ref, second, whole, sems = refs
        started = [
            (cot_arg.at[0], cot_ref),
            (weight_arg, weight_ref),
            (gate_arg.at[0], gate_two_ref),
        ]
        started.append((value_ref.at[0], whole.at[0]))
        started.append((gate_ref.at[0], whole.at[1]))
        started = [
            pltpu.make_async_copy(source, target, sems.at[index])
            for index, (source, target) in enumerate(started)
        ]
        for copy in started:
            copy.start()
        for copy in started[:3]:
            copy.wait()
        second[...] = grad_gated(cot_ref, weight_ref) * gate_two_ref[...].astype(F32)
        for step, out in enumerate(outs):
            out[2] = pick_columns(second, held(sent(step)), cols, seq).astype(BF16)
        for copy in started[3:]:
            copy.wait()
        for step, out in enumerate(outs):
            for index in range(2):
                out[index] = pick_columns(whole.at[index], held(sent(step)), cols, seq)

    triple = ((3, rows, cols), BF16)
    wide_bf16 = ((rows, width), BF16)
    with jax.named_scope("load"):
        sends = call(
            load_kernel,
            [triple] * seq,
            (value, gate_one, grad_out, out_weight, gate_two),
            scratch=[
                pltpu.VMEM((rows, width), BF16),
                pltpu.VMEM((width, width), BF16),
                pltpu.VMEM((rows, width), BF16),
                pltpu.VMEM((rows, width), F32),
                pltpu.VMEM((2, rows, width), BF16),
                pltpu.SemaphoreType.DMA((5,)),
            ],
            flops=2 * rows * width * width,
            in_hbm=True,
            limit=load_limit,
        )
    if fast:
        parts_in = [sends[0]] + [lax.ppermute(sends[far], "ctx", across(far)) for far in range(1, seq)]
    else:
        parts_in = around(sends)

    def filter_kernel(filters_ref, high, low, cot_ref, gate_ref, out, *beside):
        if fast:
            beside[0][:, :width] = cot_ref[...]
            for index, far in enumerate((1, 3)):
                piece = pick_columns(gate_ref, held(lax.axis_index("ctx") ^ far), cols, seq)
                beside[0][:, width + index * cols : width + (index + 1) * cols] = piece
        for index in range(2):
            out[index] = with_previous(to_spectra(high, low, filters_ref[index]), cols)

    with jax.named_scope("filter_spectra"):
        own_filters = lax.dynamic_slice_in_dim(filters, held(lax.axis_index("ctx")) * cols, cols, 2)
        filter_spectra, *sends = call(
            filter_kernel,
            [((2, *spectra_shape), F32)] + [((rows, width + 2 * cols), BF16)] * fast,
            (own_filters, fwd_high, fwd_low, grad_out[0], gate_two[0]),
            flops=4 * table_flops,
            limit=limit,
        )
    if fast:
        beside_in = lax.ppermute(sends[0], "ctx", across(1))

    def put_result(outs, index, total, arrays):
        if len(outs) == seq:
            for step, out in enumerate(outs):
                place = lax.axis_index("ctx") ^ step if fast else ahead(step)
                out[index] = pick_rows(total, place, rows).astype(BF16)
            return
        for far in range(4):
            piece = pick_rows(total, lax.axis_index("ctx") ^ far, rows).astype(BF16)
            outs[far // 2][far % 2 * arrays + index] = piece

    def forward_kernel(*refs):
        parts, refs = refs[:seq], refs[seq:]
        filt, high, low, back, first_ref, value_spec, mixed_spec = refs[:7]
        outs, (stream, second) = refs[7:-2], refs[-2:]
        for step, part in zip(in_order, parts):
            put_rows(stream, came(step), rows, part[0])
        spectra = to_spectra(high, low, stream[...])
        value_spec[...] = with_previous(spectra, cols)
        conv = from_spectra(back, causal_product(filt[0], spectra, cols))
        for i in range(length // block):
            first_ref[i * block : (i + 1) * block] = columns(conv, i, cols)
        for step, part in zip(in_order, parts):
            gated = part[1].astype(F32) * pick_rows(first_ref, came(step), rows)
            put_rows(stream, came(step), rows, gated.astype(BF16))
        spectra = to_spectra(high, low, stream[...])
        mixed_spec[...] = with_previous(spectra, cols)
        conv = from_spectra(back, causal_product(filt[1], spectra, cols))
        for i in range(length // block):
            second[i * block : (i + 1) * block] = columns(conv, i, cols)
        put_result(outs, 0, second, 1)

    with jax.named_scope("forward_convolutions"):
        first_conv, value_spectra, mixed_spectra, *sends = call(
            forward_kernel,
            [((length, cols), F32), (spectra_shape, F32), (spectra_shape, F32)]
            + ([((2, rows, cols), BF16)] * 2 if fast else [((1, rows, cols), BF16)] * seq),
            (*(parts_in[step] for step in in_order), filter_spectra, fwd_high, fwd_low, inv_high),
            scratch=[pltpu.VMEM((length, cols), BF16), pltpu.VMEM((length, cols), F32)],
            flops=6 * table_flops,
            limit=limit,
        )
    if fast:
        second_stays, goes = sends
        second_near = lax.ppermute(goes, "ctx", across(2))
    else:
        second_parts = around(sends)

    def backward_kernel(*refs):
        parts, refs = refs[:seq], refs[seq:]
        filt, first_ref, value_spec, mixed_spec, high, low, back = refs[:7]
        lags, *outs, stream, total = refs[7:]
        if fast:
            lag_kept, lag_given, *outs, packed = outs
        count = length // block
        for step, part in zip(in_order, parts):
            put_rows(stream, came(step), rows, part[2])

        def both(left, other):
            spectra = to_spectra(high, low, stream[...])
            grads = anti_product(left, spectra, cols)
            terms = anti_product(other, spectra, cols)
            return from_spectra(back, jnp.concatenate([grads, terms], axis=1))

        def put_lags(index, out):
            for i in range(count):
                piece = columns(out, count + i, cols)
                lags[index, i * block : (i + 1) * block] = piece

        out = both(filt[1], mixed_spec[...])
        for i in range(count):
            total[i * block : (i + 1) * block] = columns(out, i, cols)
        put_lags(1, out)
        for step, part in zip(in_order, parts):
            grad = pick_rows(total, came(step), rows)
            put_rows(stream, came(step), rows, (grad * part[1].astype(F32)).astype(BF16))
        total[...] = total[...] * first_ref[...]
        put_result(outs, 0, total, 2)
        out = both(filt[0], value_spec[...])
        for i in range(count):
            total[i * block : (i + 1) * block] = columns(out, i, cols)
        put_result(outs, 1, total, 2)
        put_lags(0, out)
        if fast:
            here, own_core = lax.axis_index("ctx"), lax.rem(lax.axis_index("dp"), 2)
            half = jnp.where(here == 0, 1 - own_core, own_core)
            lower = lax.broadcasted_iota(jnp.int32, (length, cols), 1) < fine
            packed[0] = jnp.where(lower, lags[0], pltpu.roll(lags[1], fine, axis=1))
            packed[1] = jnp.where(lower, pltpu.roll(lags[0], fine, axis=1), lags[1])
            for index in range(seq):
                lanes = pl.ds(index * cols, cols)
                lag_kept[:, lanes] = packed[half, index * rows : (index + 1) * rows]
                given = packed[1 - half, index * rows : (index + 1) * rows]
                lag_given[:, lanes] = given.astype(BF16)

    with jax.named_scope("backward_convolutions"):
        lags, *sends_home = call(
            backward_kernel,
            [((2, length, cols), F32)] + [((rows, width), F32), wide_bf16] * fast + [((2, rows, cols), BF16)] * seq,
            (
                *(parts_in[step] for step in in_order),
                filter_spectra,
                first_conv,
                value_spectra,
                mixed_spectra,
                fwd_high,
                fwd_low,
                inv_high,
            ),
            scratch=[pltpu.VMEM((2, length, cols), F32)] * fast
            + [pltpu.VMEM((length, cols), BF16), pltpu.VMEM((length, cols), F32)],
            flops=8 * table_flops,
            limit=limit,
        )

    if fast:
        def to_core(block):
            return lax.ppermute(block, "dp", [(i, i ^ 1) for i in range(data)])

        def to_chip(block, other):
            pairs = []
            for i in range(data):
                for j in range(seq):
                    pairs.append((i * seq + j, (i ^ (2 * (j ^ other) or 1)) * seq + j))
            return lax.ppermute(block, ("dp", "ctx"), pairs)

        def core_kernel(kept_ref, taken_ref, *outs):
            summed = (kept_ref[...] + taken_ref[...].astype(F32)).astype(BF16)
            for index, out in enumerate(outs):
                out[...] = summed[index * out.shape[0] : (index + 1) * out.shape[0]]

        lag_kept, lag_given, *sends_home = sends_home
        with jax.named_scope("lag_core_sum"):
            (lag_sum,) = call(
                core_kernel, [wide_bf16], (lag_kept, to_core(lag_given)), limit=limit
            )
        lag_term = to_chip(lag_sum, 0)

        def gated_kernel(*refs):
            stays_ref, near_ref, gate_ref, cot_ref, beside_ref, *refs = refs
            kept, given, gated, cots, whole = refs
            here = lax.axis_index("ctx")
            cots[:rows] = cot_ref[...]
            cots[rows:] = beside_ref[:, :width]
            for index, ref in enumerate((stays_ref, near_ref)):
                lanes = pl.ds(index * cols, cols)
                gate = pick_columns(gate_ref, held(here ^ (2 * index)), cols, seq)
                gated[:rows, lanes] = (gate.astype(F32) * ref[0].astype(F32)).astype(BF16)
                gate = columns(beside_ref, width // cols + index, cols)
                gated[rows:, lanes] = (gate.astype(F32) * ref[1].astype(F32)).astype(BF16)
            whole[...] = lax.dot_general(
                gated[...], cots[...], (((0,), (0,)), ((), ())), preferred_element_type=F32
            )
            own_core = lax.rem(lax.axis_index("dp"), 2)
            first = jnp.where(here == 0, 1 - own_core, own_core)
            second = jnp.where(here == 2, 1 - own_core, own_core)
            for out, one, two in ((kept, first, second), (given, 1 - first, 1 - second)):
                piece = whole[pl.ds(pl.multiple_of(one * own_rows, own_rows), own_rows), :]
                out[:own_rows] = piece.astype(out.dtype)
                start = pl.multiple_of(cols + two * own_rows, own_rows)
                out[own_rows:] = whole[pl.ds(start, own_rows), :].astype(out.dtype)

        term_shape = (2 * own_rows, width)
        with jax.named_scope("weight_partial"):
            kept, given = call(
                gated_kernel,
                [(term_shape, F32), (term_shape, BF16)],
                (second_stays, second_near, gate_two[0], grad_out[0], beside_in),
                scratch=[
                    pltpu.VMEM((2 * rows, 2 * cols), BF16),
                    pltpu.VMEM((2 * rows, width), BF16),
                    pltpu.VMEM((2 * cols, width), F32),
                ],
                limit=limit,
            )

        def terms_kernel(kept_ref, taken_ref, stays_ref, near_ref, home_ref, one, two, goes_on):
            core_kernel(kept_ref, taken_ref, one, two)
            goes_on[0] = stays_ref[1]
            goes_on[1] = near_ref[1]
            goes_on[2:] = home_ref[...]

        with jax.named_scope("core_sum"):
            *sends, goes_on = call(
                terms_kernel,
                [((own_rows, width), BF16)] * 2 + [((4, rows, cols), BF16)],
                (kept, to_core(given), second_stays, second_near, sends_home[1]),
                limit=limit,
            )
        second_far = lax.ppermute(goes_on, "ctx", across(1))

        chip_terms = [to_chip(sends[0], 0), to_chip(sends[1], 2)]

        home = [lax.ppermute(sends_home[far], "ctx", across(far)) for far in (2, 3)]

        tables = ((0, 1, 2, 3), (1, 3, 0, 2), (3, 2, 1, 0), (2, 0, 3, 1))

        def place_kernel(lag_ref, one, two, *refs):
            outs, total = refs[:-1], refs[-1]
            total[...] = one[...].astype(F32) + two[...].astype(F32)
            for table, out in zip(tables, outs):
                place = table[0]
                for index in range(1, 4):
                    place = jnp.where(lax.axis_index("ctx") == index, table[index], place)
                out[:own_rows] = pick_columns(total, place, cols, seq).astype(out.dtype)
                out[own_rows:] = pick_columns(lag_ref, place, cols, seq).astype(out.dtype)

        small = (own_rows + rows, cols)
        with jax.named_scope("chip_sum"):
            sends = call(
                place_kernel,
                [(small, F32)] + [(small, BF16)] * (seq - 1),
                (lag_term, *chip_terms),
                scratch=[pltpu.VMEM((own_rows, width), F32)],
            )
        last_terms = [sends[0]]
        for table, part in zip(tables[1:], sends[1:]):
            last_terms.append(lax.ppermute(part, "ctx", list(enumerate(table))))

        def mixed_kernel(*refs):
            parts, (gate_ref, weight_ref, cot_ref, mixed_ref, out, second) = refs[:3], refs[3:]
            here = lax.axis_index("ctx")
            stays_ref, near_ref, far_ref = parts
            put_columns(second, held(here), cols, seq, stays_ref[0])
            put_columns(second, held(here ^ 2), cols, seq, near_ref[0])
            put_columns(second, held(here ^ 1), cols, seq, far_ref[0])
            put_columns(second, held(here ^ 3), cols, seq, far_ref[1])
            wide = second[...].astype(F32)
            gated = (gate_ref[...].astype(F32) * wide).astype(BF16)
            mixed_ref[...] = mxu(gated, weight_ref[...]).astype(BF16)
            out[...] = (grad_gated(cot_ref, weight_ref) * wide).astype(BF16)

        with jax.named_scope("mixed"):
            mixed, grad_gate_two = call(
                mixed_kernel,
                [wide_bf16, wide_bf16],
                (second_stays, second_near, second_far, gate_two[0], out_weight, grad_out[0]),
                scratch=[pltpu.VMEM((rows, width), BF16)],
                flops=4 * rows * width * width,
                limit=limit,
            )

        def final_kernel(*refs):
            arrived, parts, refs = refs[:seq], refs[seq : 2 * seq], refs[2 * seq :]
            filter_ref, weight_ref, gate_ref, value_ref = refs
            for part, (far, first) in zip(parts, ((0, 0), (1, 2), (2, 0), (3, 0))):
                place = held(lax.axis_index("ctx") ^ far)
                put_columns(gate_ref, place, cols, seq, part[first])
                put_columns(value_ref, place, cols, seq, part[first + 1])
            total = arrived[0][...]
            for part in arrived[1:]:
                total = total + part[...].astype(F32)
            total = total * (1.0 / data)
            weight_ref[...] = total[:own_rows]
            turned = total[own_rows:].T
            filter_ref[0] = turned[:fine]
            filter_ref[1] = turned[fine:]

        with jax.named_scope("means"):
            filter_grad, weight_grad, grad_gate_one, grad_value = call(
                final_kernel,
                [((2, fine, rows), F32), ((own_rows, cols), F32), wide_bf16, wide_bf16],
                (*(last_terms[step] for step in (0, 1, 2, 3)), sends_home[0], second_far, *home),
            )
        filter_grad = jnp.swapaxes(filter_grad, 1, 2)
        return (
            mixed[None],
            grad_value[None],
            grad_gate_one[None],
            grad_gate_two[None],
            filter_grad,
            weight_grad,
        )

    def gated_kernel(*refs):
        parts, (gate_ref, cot_ref, second_ref, gated_ref, weight_ref) = refs[:seq], refs[seq:]
        for step, part in enumerate(parts):
            put_columns(second_ref, held(behind(step)), cols, seq, part[0])
        gated = (gate_ref[...].astype(F32) * second_ref[...].astype(F32)).astype(BF16)
        gated_ref[...] = gated
        weight_ref[...] = lax.dot_general(
            gated, cot_ref[...], (((0,), (0,)), ((), ())), preferred_element_type=F32
        )

    with jax.named_scope("weight_partial"):
        second_conv, gated, weight_part = call(
            gated_kernel,
            [wide_bf16, wide_bf16, ((width, width), F32)],
            (*second_parts, gate_two[0], grad_out[0]),
            flops=2 * rows * width * width,
            limit=limit,
        )

    core = lax.rem(lax.axis_index("dp"), 2)
    lag_terms = lags.reshape(2, seq, rows, per_ctx, fine).transpose(1, 3, 2, 0, 4)
    lag_rows = rows * 2 * fine // width
    terms = jnp.concatenate(
        [
            weight_part.reshape(data, own_rows, width),
            lag_terms.reshape(data, lag_rows, width),
        ],
        axis=1,
    )
    by_core = terms.reshape(chips, 2, *terms.shape[1:])
    kept = lax.dynamic_index_in_dim(by_core, core, 1, keepdims=False)
    given = lax.dynamic_index_in_dim(by_core, 1 - core, 1, keepdims=False).astype(BF16)
    given, kept = (a.reshape(-1, width) for a in (given, kept))
    taken = lax.ppermute(given, "dp", [(i, i ^ 1) for i in range(data)])
    term_rows = own_rows + lag_rows

    def chip_kernel(kept_ref, taken_ref, own, *outs):
        place = lax.div(lax.axis_index("dp"), 2)

        def summed(index):
            start = pl.multiple_of(index * term_rows, term_rows)
            taken = taken_ref[pl.ds(start, term_rows), :]
            return kept_ref[pl.ds(start, term_rows), :] + taken.astype(F32)

        own[...] = summed(place)
        for step in range(1, chips):
            outs[step - 1][...] = summed(place ^ step).astype(BF16)

    term = (term_rows, width)
    with jax.named_scope("core_sum"):
        total, *sends = call(
            chip_kernel,
            [(term, F32)] + [(term, BF16)] * (chips - 1),
            (kept, taken),
            limit=limit,
        )
    for step in range(1, chips):
        pairs = [(i, i ^ (2 * step)) for i in range(data)]
        total = total + lax.ppermute(sends[step - 1], "dp", pairs).astype(F32)

    def mixed_kernel(gated_ref, weight_ref, cot_ref, second_ref, mixed_ref, gate_ref):
        mixed_ref[...] = mxu(gated_ref[...], weight_ref[...]).astype(BF16)
        grad = grad_gated(cot_ref, weight_ref)
        gate_ref[...] = (grad * second_ref[...].astype(F32)).astype(BF16)

    with jax.named_scope("mixed"):
        mixed, grad_gate_two = call(
            mixed_kernel,
            [wide_bf16, wide_bf16],
            (gated, out_weight, grad_out[0], second_conv),
            flops=4 * rows * width * width,
            limit=limit,
        )
    home = around(sends_home)

    weight_blocks = total[:own_rows].reshape(own_rows, seq, cols)
    sends = [
        lax.dynamic_index_in_dim(weight_blocks, ahead(step), 1, keepdims=False)
        for step in range(seq)
    ]
    last_terms = around(sends[:1] + [part.astype(BF16) for part in sends[1:]])
    lag_sum = total[own_rows:].reshape(rows, 2 * fine).astype(BF16)
    pairs = []
    for i in range(data):
        for j in range(seq):
            pairs.append((i * seq + j, (per_ctx * j + i % per_ctx) * seq + i // per_ctx))
    lag_own = lax.ppermute(lag_sum, ("dp", "ctx"), pairs)

    def unpack_kernel(*refs):
        parts, (gate_ref, value_ref) = refs[:-2], refs[-2:]
        for step, part in enumerate(parts):
            put_columns(gate_ref, held(behind(step)), cols, seq, part[0])
            put_columns(value_ref, held(behind(step)), cols, seq, part[1])

    with jax.named_scope("unpack_results"):
        grad_gate_one, grad_value = call(unpack_kernel, [wide_bf16, wide_bf16], home)
    filter_grad = lag_own.reshape(rows, 2, fine).transpose(1, 0, 2).astype(F32) / data
    weight_grad = sum(part.astype(F32) for part in last_terms) / data
    return (
        mixed[None],
        grad_value[None],
        grad_gate_one[None],
        grad_gate_two[None],
        filter_grad,
        weight_grad,
    )


def solution(mesh):
    stream = P("dp", "ctx", None)
    return jax.shard_map(
        on_device,
        mesh=mesh,
        in_specs=(stream, stream, stream, P(), P(), stream),
        out_specs=(stream, stream, stream, stream, P(None, "ctx", "dp"), P("dp", "ctx")),
        check_vma=False,
    )
```

```python
import functools
import math

import jax
import jax.numpy as jnp
import ml_dtypes
import numpy as np
from jax import lax
from jax.experimental import pallas as pl
from jax.experimental.pallas import tpu as pltpu
from jax.sharding import PartitionSpec as P

F32 = jnp.float32
BF16 = jnp.bfloat16


def split_table(table):
    high = table.astype(ml_dtypes.bfloat16)
    low = (table - high.astype(np.float64)).astype(ml_dtypes.bfloat16)
    return jnp.asarray(high), jnp.asarray(low)


@functools.lru_cache(maxsize=None)
def table_values(block):
    period = 2 * block
    bins = np.arange(block)
    radians = (bins[:, None] * bins[None, :] % period) * (2.0 * math.pi / period)
    cosines, sines = np.cos(radians), -np.sin(radians)
    sines[0] = np.where(bins % 2 == 0, 1.0, -1.0)
    forward = np.concatenate([cosines, sines], axis=0)
    weights = np.full((period,), 2.0 / period)
    weights[0] = weights[block] = 1.0 / period
    return forward, forward.T * weights[None, :]


def mxu(left, right):
    return jnp.dot(left, right, preferred_element_type=F32)


def beside(stream, block):
    return jnp.concatenate(
        [stream[i : i + block] for i in range(0, stream.shape[0], block)], axis=1
    )


def to_spectra(high, low, stream):
    blocks = beside(stream, high.shape[1])
    return mxu(high[...], blocks) + mxu(low[...], blocks)


def from_spectra(high, spectra):
    return mxu(high[...], spectra.astype(BF16))


def parity(shape):
    row = lax.broadcasted_iota(jnp.int32, shape, 0)
    return jnp.where(row % 2 == 0, 1.0, -1.0)


def with_previous(spectra, cols):
    sign = parity((spectra.shape[0], cols))
    out = [spectra[:, :cols]]
    for i in range(cols, spectra.shape[1], cols):
        out.append(spectra[:, i : i + cols] + sign * spectra[:, i - cols : i])
    return jnp.concatenate(out, axis=1)


def sum_of_products(terms, conj_left):
    half = terms[0][0].shape[0] // 2
    border = lax.broadcasted_iota(jnp.int32, (half, terms[0][0].shape[1]), 0) == 0
    straight = cross = imag = 0.0
    for left, right in terms:
        left_re, left_im, right_re, right_im = left[:half], left[half:], right[:half], right[half:]
        straight += left_re * right_re
        cross += left_im * right_im
        if conj_left:
            imag += left_re * right_im - left_im * right_re
        else:
            imag += left_re * right_im + left_im * right_re
    inner = jnp.where(border, 0.0, cross)
    real = straight + inner if conj_left else straight - inner
    return jnp.concatenate([real, jnp.where(border, cross, imag)], axis=0)


def columns(ref, index, cols):
    return ref[:, index * cols : (index + 1) * cols]


def causal_product(filt, spectra, cols):
    count = spectra.shape[1] // cols
    out = []
    for i in range(count):
        terms = [(columns(filt, i - a, cols), columns(spectra, a, cols)) for a in range(i + 1)]
        out.append(sum_of_products(terms, False))
    return jnp.concatenate(out, axis=1)


def anti_product(left, spectra, cols):
    count = spectra.shape[1] // cols
    out = []
    for i in range(count):
        terms = [
            (columns(left, a - i, cols), columns(spectra, a, cols)) for a in range(i, count)
        ]
        out.append(sum_of_products(terms, True))
    return jnp.concatenate(out, axis=1)


def pick_columns(ref, index, width, count):
    if width % 128 == 0:
        return ref[:, pl.ds(pl.multiple_of(index * width, width), width)]
    whole = ref[...]
    out = whole[:, :width]
    for other in range(1, count):
        out = jnp.where(index == other, whole[:, other * width : (other + 1) * width], out)
    return out


def put_columns(ref, index, width, count, block):
    if width % 128 == 0:
        ref[:, pl.ds(pl.multiple_of(index * width, width), width)] = block
        return
    for other in range(count):

        @pl.when(index == other)
        def _():
            ref[:, other * width : (other + 1) * width] = block


def pick_rows(ref, index, rows):
    return ref[pl.ds(pl.multiple_of(index * rows, rows), rows), :]


def put_rows(ref, index, rows, block):
    ref[pl.ds(pl.multiple_of(index * rows, rows), rows), :] = block


def call(kernel, outs, args, scratch=(), flops=0, limit=16, in_hbm=False):
    vmem = pl.BlockSpec(memory_space=pltpu.VMEM)
    source = pl.BlockSpec(memory_space=pltpu.HBM) if in_hbm else vmem
    total = sum(math.prod(a.shape) * a.dtype.itemsize for a in args)
    return pl.pallas_call(
        kernel,
        out_shape=[jax.ShapeDtypeStruct(shape, dtype) for shape, dtype in outs],
        in_specs=[source] * len(args),
        out_specs=[vmem] * len(outs),
        scratch_shapes=list(scratch),
        compiler_params=pltpu.CompilerParams(vmem_limit_bytes=int(limit * 2**20)),
        cost_estimate=pl.CostEstimate(flops=flops, bytes_accessed=total, transcendentals=0),
    )(*args)


def on_device(value, gate_one, gate_two, filters, out_weight, grad_out):
    rows, width = value.shape[1:]
    seq = lax.axis_size("ctx")
    data = lax.axis_size("dp")
    length = rows * seq
    cols = width // seq
    block = math.gcd(length, 256)
    per_ctx = data // seq
    fine = cols // per_ctx
    chips = data // 2
    own_rows = width // data
    fast = cols == 128 and per_ctx == 2 and chips == seq == 4
    limit = 16 if length <= 512 else 48
    load_limit = 53.5
    forward, inverse = table_values(block)
    (fwd_high, fwd_low), (inv_high, _) = split_table(forward), split_table(inverse)
    spectra_shape = (2 * block, length // block * cols)
    table_flops = 4 * block * length * cols

    def ahead(step):
        return lax.rem(lax.axis_index("ctx") + step, seq)

    def behind(step):
        return lax.rem(lax.axis_index("ctx") + seq - step, seq)

    def held(place):
        return place ^ lax.div(lax.axis_index("dp"), 2) if fast else place

    def around(blocks):
        out = [blocks[0]]
        for step in range(1, seq):
            pairs = [(i, (i + step) % seq) for i in range(seq)]
            out.append(lax.ppermute(blocks[step], "ctx", pairs))
        return out

    def grad_gated(cot_ref, weight_ref):
        return lax.dot_general(
            cot_ref[...], weight_ref[...], (((1,), (1,)), ((), ())), preferred_element_type=F32
        )

    def across(far):
        return [(i, i ^ far) for i in range(seq)]

    in_order = (0, 3, 1, 2) if fast else range(seq)

    def sent(step):
        return lax.axis_index("ctx") ^ step if fast else ahead(step)

    def came(step):
        return lax.axis_index("ctx") ^ step if fast else behind(step)

    def load_kernel(*refs):
        value_ref, gate_ref, cot_arg, weight_arg, gate_arg = refs[:5]
        outs, refs = refs[5 : 5 + seq], refs[5 + seq :]
        cot_ref, weight_ref, gate_two_ref, second, whole, sems = refs
        started = [
            (cot_arg.at[0], cot_ref),
            (weight_arg, weight_ref),
            (gate_arg.at[0], gate_two_ref),
        ]
        started.append((value_ref.at[0], whole.at[0]))
        started.append((gate_ref.at[0], whole.at[1]))
        started = [
            pltpu.make_async_copy(source, target, sems.at[index])
            for index, (source, target) in enumerate(started)
        ]
        for copy in started:
            copy.start()
        for copy in started[:3]:
            copy.wait()
        second[...] = grad_gated(cot_ref, weight_ref) * gate_two_ref[...].astype(F32)
        for step, out in enumerate(outs):
            out[2] = pick_columns(second, held(sent(step)), cols, seq).astype(BF16)
        for copy in started[3:]:
            copy.wait()
        for step, out in enumerate(outs):
            for index in range(2):
                out[index] = pick_columns(whole.at[index], held(sent(step)), cols, seq)

    triple = ((3, rows, cols), BF16)
    wide_bf16 = ((rows, width), BF16)
    with jax.named_scope("load"):
        sends = call(
            load_kernel,
            [triple] * seq,
            (value, gate_one, grad_out, out_weight, gate_two),
            scratch=[
                pltpu.VMEM((rows, width), BF16),
                pltpu.VMEM((width, width), BF16),
                pltpu.VMEM((rows, width), BF16),
                pltpu.VMEM((rows, width), F32),
                pltpu.VMEM((2, rows, width), BF16),
                pltpu.SemaphoreType.DMA((5,)),
            ],
            flops=2 * rows * width * width,
            in_hbm=True,
            limit=load_limit,
        )
    if fast:
        parts_in = [sends[0]] + [lax.ppermute(sends[far], "ctx", across(far)) for far in range(1, seq)]
    else:
        parts_in = around(sends)

    def filter_kernel(filters_ref, high, low, cot_ref, gate_ref, out, *beside):
        if fast:
            beside[0][:, :width] = cot_ref[...]
            for index, far in enumerate((1, 3)):
                piece = pick_columns(gate_ref, held(lax.axis_index("ctx") ^ far), cols, seq)
                beside[0][:, width + index * cols : width + (index + 1) * cols] = piece
        for index in range(2):
            out[index] = with_previous(to_spectra(high, low, filters_ref[index]), cols)

    with jax.named_scope("filter_spectra"):
        own_filters = lax.dynamic_slice_in_dim(filters, held(lax.axis_index("ctx")) * cols, cols, 2)
        filter_spectra, *sends = call(
            filter_kernel,
            [((2, *spectra_shape), F32)] + [((rows, width + 2 * cols), BF16)] * fast,
            (own_filters, fwd_high, fwd_low, grad_out[0], gate_two[0]),
            flops=4 * table_flops,
            limit=limit,
        )
    if fast:
        beside_in = lax.ppermute(sends[0], "ctx", across(1))

    def put_result(outs, index, total, arrays):
        if len(outs) == seq:
            for step, out in enumerate(outs):
                place = lax.axis_index("ctx") ^ step if fast else ahead(step)
                out[index] = pick_rows(total, place, rows).astype(BF16)
            return
        for far in range(4):
            piece = pick_rows(total, lax.axis_index("ctx") ^ far, rows).astype(BF16)
            outs[far // 2][far % 2 * arrays + index] = piece

    def forward_kernel(*refs):
        parts, refs = refs[:seq], refs[seq:]
        filt, high, low, back, first_ref, value_spec, mixed_spec = refs[:7]
        outs, (stream, second) = refs[7:-2], refs[-2:]
        for step, part in zip(in_order, parts):
            put_rows(stream, came(step), rows, part[0])
        spectra = to_spectra(high, low, stream[...])
        value_spec[...] = with_previous(spectra, cols)
        conv = from_spectra(back, causal_product(filt[0], spectra, cols))
        for i in range(length // block):
            first_ref[i * block : (i + 1) * block] = columns(conv, i, cols)
        for step, part in zip(in_order, parts):
            gated = part[1].astype(F32) * pick_rows(first_ref, came(step), rows)
            put_rows(stream, came(step), rows, gated.astype(BF16))
        spectra = to_spectra(high, low, stream[...])
        mixed_spec[...] = with_previous(spectra, cols)
        conv = from_spectra(back, causal_product(filt[1], spectra, cols))
        for i in range(length // block):
            second[i * block : (i + 1) * block] = columns(conv, i, cols)
        put_result(outs, 0, second, 1)

    with jax.named_scope("forward_convolutions"):
        first_conv, value_spectra, mixed_spectra, *sends = call(
            forward_kernel,
            [((length, cols), F32), (spectra_shape, F32), (spectra_shape, F32)]
            + ([((2, rows, cols), BF16)] * 2 if fast else [((1, rows, cols), BF16)] * seq),
            (*(parts_in[step] for step in in_order), filter_spectra, fwd_high, fwd_low, inv_high),
            scratch=[pltpu.VMEM((length, cols), BF16), pltpu.VMEM((length, cols), F32)],
            flops=6 * table_flops,
            limit=limit,
        )
    if fast:
        second_stays, goes = sends
        second_near = lax.ppermute(goes, "ctx", across(2))
    else:
        second_parts = around(sends)

    def backward_kernel(*refs):
        parts, refs = refs[:seq], refs[seq:]
        filt, first_ref, value_spec, mixed_spec, high, low, back = refs[:7]
        lags, *outs, stream, total = refs[7:]
        count = length // block
        for step, part in zip(in_order, parts):
            put_rows(stream, came(step), rows, part[2])

        def both(left, other):
            spectra = to_spectra(high, low, stream[...])
            grads = anti_product(left, spectra, cols)
            terms = anti_product(other, spectra, cols)
            return from_spectra(back, jnp.concatenate([grads, terms], axis=1))

        def put_lags(index, out):
            for i in range(count):
                piece = columns(out, count + i, cols)
                lags[index, i * block : (i + 1) * block] = piece

        out = both(filt[1], mixed_spec[...])
        for i in range(count):
            total[i * block : (i + 1) * block] = columns(out, i, cols)
        put_lags(1, out)
        for step, part in zip(in_order, parts):
            grad = pick_rows(total, came(step), rows)
            put_rows(stream, came(step), rows, (grad * part[1].astype(F32)).astype(BF16))
        total[...] = total[...] * first_ref[...]
        put_result(outs, 0, total, 2)
        out = both(filt[0], value_spec[...])
        for i in range(count):
            total[i * block : (i + 1) * block] = columns(out, i, cols)
        put_result(outs, 1, total, 2)
        put_lags(0, out)

    with jax.named_scope("backward_convolutions"):
        lags, *sends_home = call(
            backward_kernel,
            [((2, length, cols), F32)] + [((2, rows, cols), BF16)] * seq,
            (
                *(parts_in[step] for step in in_order),
                filter_spectra,
                first_conv,
                value_spectra,
                mixed_spectra,
                fwd_high,
                fwd_low,
                inv_high,
            ),
            scratch=[pltpu.VMEM((length, cols), BF16), pltpu.VMEM((length, cols), F32)],
            flops=8 * table_flops,
            limit=limit,
        )

    if fast:
        def to_core(block):
            return lax.ppermute(block, "dp", [(i, i ^ 1) for i in range(data)])

        def to_chip(block, other):
            pairs = []
            for i in range(data):
                for j in range(seq):
                    pairs.append((i * seq + j, (i ^ (2 * (j ^ other) or 1)) * seq + j))
            return lax.ppermute(block, ("dp", "ctx"), pairs)

        def core_kernel(kept_ref, taken_ref, *outs):
            summed = (kept_ref[...] + taken_ref[...].astype(F32)).astype(BF16)
            for index, out in enumerate(outs):
                out[...] = summed[index * out.shape[0] : (index + 1) * out.shape[0]]

        def lag_kernel(lags, lag_kept, lag_given, packed):
            here, own_core = lax.axis_index("ctx"), lax.rem(lax.axis_index("dp"), 2)
            half = jnp.where(here == 0, 1 - own_core, own_core)
            lower = lax.broadcasted_iota(jnp.int32, (length, cols), 1) < fine
            packed[0] = jnp.where(lower, lags[0], pltpu.roll(lags[1], fine, axis=1))
            packed[1] = jnp.where(lower, pltpu.roll(lags[0], fine, axis=1), lags[1])
            for index in range(seq):
                lanes = pl.ds(index * cols, cols)
                lag_kept[:, lanes] = packed[half, index * rows : (index + 1) * rows]
                given = packed[1 - half, index * rows : (index + 1) * rows]
                lag_given[:, lanes] = given.astype(BF16)


        with jax.named_scope("lag_halves"):
            lag_kept, lag_given = call(
                lag_kernel,
                [((rows, width), F32), wide_bf16],
                (lags,),
                scratch=[pltpu.VMEM((2, length, cols), F32)],
                limit=limit,
            )
        with jax.named_scope("lag_core_sum"):
            (lag_sum,) = call(
                core_kernel, [wide_bf16], (lag_kept, to_core(lag_given)), limit=limit
            )
        lag_term = to_chip(lag_sum, 0)

        def gated_kernel(*refs):
            stays_ref, near_ref, gate_ref, cot_ref, beside_ref, *refs = refs
            kept, given, gated, cots, whole = refs
            here = lax.axis_index("ctx")
            cots[:rows] = cot_ref[...]
            cots[rows:] = beside_ref[:, :width]
            for index, ref in enumerate((stays_ref, near_ref)):
                lanes = pl.ds(index * cols, cols)
                gate = pick_columns(gate_ref, held(here ^ (2 * index)), cols, seq)
                gated[:rows, lanes] = (gate.astype(F32) * ref[0].astype(F32)).astype(BF16)
                gate = columns(beside_ref, width // cols + index, cols)
                gated[rows:, lanes] = (gate.astype(F32) * ref[1].astype(F32)).astype(BF16)
            whole[...] = lax.dot_general(
                gated[...], cots[...], (((0,), (0,)), ((), ())), preferred_element_type=F32
            )
            own_core = lax.rem(lax.axis_index("dp"), 2)
            first = jnp.where(here == 0, 1 - own_core, own_core)
            second = jnp.where(here == 2, 1 - own_core, own_core)
            for out, one, two in ((kept, first, second), (given, 1 - first, 1 - second)):
                piece = whole[pl.ds(pl.multiple_of(one * own_rows, own_rows), own_rows), :]
                out[:own_rows] = piece.astype(out.dtype)
                start = pl.multiple_of(cols + two * own_rows, own_rows)
                out[own_rows:] = whole[pl.ds(start, own_rows), :].astype(out.dtype)

        term_shape = (2 * own_rows, width)
        with jax.named_scope("weight_partial"):
            kept, given = call(
                gated_kernel,
                [(term_shape, F32), (term_shape, BF16)],
                (second_stays, second_near, gate_two[0], grad_out[0], beside_in),
                scratch=[
                    pltpu.VMEM((2 * rows, 2 * cols), BF16),
                    pltpu.VMEM((2 * rows, width), BF16),
                    pltpu.VMEM((2 * cols, width), F32),
                ],
                limit=limit,
            )

        def terms_kernel(kept_ref, taken_ref, stays_ref, near_ref, home_ref, one, two, goes_on):
            core_kernel(kept_ref, taken_ref, one, two)
            goes_on[0] = stays_ref[1]
            goes_on[1] = near_ref[1]
            goes_on[2:] = home_ref[...]

        with jax.named_scope("core_sum"):
            *sends, goes_on = call(
                terms_kernel,
                [((own_rows, width), BF16)] * 2 + [((4, rows, cols), BF16)],
                (kept, to_core(given), second_stays, second_near, sends_home[1]),
                limit=limit,
            )
        second_far = lax.ppermute(goes_on, "ctx", across(1))

        chip_terms = [to_chip(sends[0], 0), to_chip(sends[1], 2)]

        home = [lax.ppermute(sends_home[far], "ctx", across(far)) for far in (2, 3)]

        tables = ((0, 1, 2, 3), (1, 3, 0, 2), (3, 2, 1, 0), (2, 0, 3, 1))

        def place_kernel(lag_ref, one, two, *refs):
            outs, total = refs[:-1], refs[-1]
            total[...] = one[...].astype(F32) + two[...].astype(F32)
            for table, out in zip(tables, outs):
                place = table[0]
                for index in range(1, 4):
                    place = jnp.where(lax.axis_index("ctx") == index, table[index], place)
                out[:own_rows] = pick_columns(total, place, cols, seq).astype(out.dtype)
                out[own_rows:] = pick_columns(lag_ref, place, cols, seq).astype(out.dtype)

        small = (own_rows + rows, cols)
        with jax.named_scope("chip_sum"):
            sends = call(
                place_kernel,
                [(small, F32)] + [(small, BF16)] * (seq - 1),
                (lag_term, *chip_terms),
                scratch=[pltpu.VMEM((own_rows, width), F32)],
            )
        last_terms = [sends[0]]
        for table, part in zip(tables[1:], sends[1:]):
            last_terms.append(lax.ppermute(part, "ctx", list(enumerate(table))))

        def mixed_kernel(*refs):
            parts, (gate_ref, weight_ref, cot_ref, mixed_ref, out, second) = refs[:3], refs[3:]
            here = lax.axis_index("ctx")
            stays_ref, near_ref, far_ref = parts
            put_columns(second, held(here), cols, seq, stays_ref[0])
            put_columns(second, held(here ^ 2), cols, seq, near_ref[0])
            put_columns(second, held(here ^ 1), cols, seq, far_ref[0])
            put_columns(second, held(here ^ 3), cols, seq, far_ref[1])
            wide = second[...].astype(F32)
            gated = (gate_ref[...].astype(F32) * wide).astype(BF16)
            mixed_ref[...] = mxu(gated, weight_ref[...]).astype(BF16)
            out[...] = (grad_gated(cot_ref, weight_ref) * wide).astype(BF16)

        with jax.named_scope("mixed"):
            mixed, grad_gate_two = call(
                mixed_kernel,
                [wide_bf16, wide_bf16],
                (second_stays, second_near, second_far, gate_two[0], out_weight, grad_out[0]),
                scratch=[pltpu.VMEM((rows, width), BF16)],
                flops=4 * rows * width * width,
                limit=limit,
            )

        def final_kernel(*refs):
            arrived, parts, refs = refs[:seq], refs[seq : 2 * seq], refs[2 * seq :]
            filter_ref, weight_ref, gate_ref, value_ref = refs
            for part, (far, first) in zip(parts, ((0, 0), (1, 2), (2, 0), (3, 0))):
                place = held(lax.axis_index("ctx") ^ far)
                put_columns(gate_ref, place, cols, seq, part[first])
                put_columns(value_ref, place, cols, seq, part[first + 1])
            total = arrived[0][...]
            for part in arrived[1:]:
                total = total + part[...].astype(F32)
            total = total * (1.0 / data)
            weight_ref[...] = total[:own_rows]
            turned = total[own_rows:].T
            filter_ref[0] = turned[:fine]
            filter_ref[1] = turned[fine:]

        with jax.named_scope("means"):
            filter_grad, weight_grad, grad_gate_one, grad_value = call(
                final_kernel,
                [((2, fine, rows), F32), ((own_rows, cols), F32), wide_bf16, wide_bf16],
                (*(last_terms[step] for step in (0, 1, 2, 3)), sends_home[0], second_far, *home),
            )
        filter_grad = jnp.swapaxes(filter_grad, 1, 2)
        return (
            mixed[None],
            grad_value[None],
            grad_gate_one[None],
            grad_gate_two[None],
            filter_grad,
            weight_grad,
        )

    def gated_kernel(*refs):
        parts, (gate_ref, cot_ref, second_ref, gated_ref, weight_ref) = refs[:seq], refs[seq:]
        for step, part in enumerate(parts):
            put_columns(second_ref, held(behind(step)), cols, seq, part[0])
        gated = (gate_ref[...].astype(F32) * second_ref[...].astype(F32)).astype(BF16)
        gated_ref[...] = gated
        weight_ref[...] = lax.dot_general(
            gated, cot_ref[...], (((0,), (0,)), ((), ())), preferred_element_type=F32
        )

    with jax.named_scope("weight_partial"):
        second_conv, gated, weight_part = call(
            gated_kernel,
            [wide_bf16, wide_bf16, ((width, width), F32)],
            (*second_parts, gate_two[0], grad_out[0]),
            flops=2 * rows * width * width,
            limit=limit,
        )

    core = lax.rem(lax.axis_index("dp"), 2)
    lag_terms = lags.reshape(2, seq, rows, per_ctx, fine).transpose(1, 3, 2, 0, 4)
    lag_rows = rows * 2 * fine // width
    terms = jnp.concatenate(
        [
            weight_part.reshape(data, own_rows, width),
            lag_terms.reshape(data, lag_rows, width),
        ],
        axis=1,
    )
    by_core = terms.reshape(chips, 2, *terms.shape[1:])
    kept = lax.dynamic_index_in_dim(by_core, core, 1, keepdims=False)
    given = lax.dynamic_index_in_dim(by_core, 1 - core, 1, keepdims=False).astype(BF16)
    given, kept = (a.reshape(-1, width) for a in (given, kept))
    taken = lax.ppermute(given, "dp", [(i, i ^ 1) for i in range(data)])
    term_rows = own_rows + lag_rows

    def chip_kernel(kept_ref, taken_ref, own, *outs):
        place = lax.div(lax.axis_index("dp"), 2)

        def summed(index):
            start = pl.multiple_of(index * term_rows, term_rows)
            taken = taken_ref[pl.ds(start, term_rows), :]
            return kept_ref[pl.ds(start, term_rows), :] + taken.astype(F32)

        own[...] = summed(place)
        for step in range(1, chips):
            outs[step - 1][...] = summed(place ^ step).astype(BF16)

    term = (term_rows, width)
    with jax.named_scope("core_sum"):
        total, *sends = call(
            chip_kernel,
            [(term, F32)] + [(term, BF16)] * (chips - 1),
            (kept, taken),
            limit=limit,
        )
    for step in range(1, chips):
        pairs = [(i, i ^ (2 * step)) for i in range(data)]
        total = total + lax.ppermute(sends[step - 1], "dp", pairs).astype(F32)

    def mixed_kernel(gated_ref, weight_ref, cot_ref, second_ref, mixed_ref, gate_ref):
        mixed_ref[...] = mxu(gated_ref[...], weight_ref[...]).astype(BF16)
        grad = grad_gated(cot_ref, weight_ref)
        gate_ref[...] = (grad * second_ref[...].astype(F32)).astype(BF16)

    with jax.named_scope("mixed"):
        mixed, grad_gate_two = call(
            mixed_kernel,
            [wide_bf16, wide_bf16],
            (gated, out_weight, grad_out[0], second_conv),
            flops=4 * rows * width * width,
            limit=limit,
        )
    home = around(sends_home)

    weight_blocks = total[:own_rows].reshape(own_rows, seq, cols)
    sends = [
        lax.dynamic_index_in_dim(weight_blocks, ahead(step), 1, keepdims=False)
        for step in range(seq)
    ]
    last_terms = around(sends[:1] + [part.astype(BF16) for part in sends[1:]])
    lag_sum = total[own_rows:].reshape(rows, 2 * fine).astype(BF16)
    pairs = []
    for i in range(data):
        for j in range(seq):
            pairs.append((i * seq + j, (per_ctx * j + i % per_ctx) * seq + i // per_ctx))
    lag_own = lax.ppermute(lag_sum, ("dp", "ctx"), pairs)

    def unpack_kernel(*refs):
        parts, (gate_ref, value_ref) = refs[:-2], refs[-2:]
        for step, part in enumerate(parts):
            put_columns(gate_ref, held(behind(step)), cols, seq, part[0])
            put_columns(value_ref, held(behind(step)), cols, seq, part[1])

    with jax.named_scope("unpack_results"):
        grad_gate_one, grad_value = call(unpack_kernel, [wide_bf16, wide_bf16], home)
    filter_grad = lag_own.reshape(rows, 2, fine).transpose(1, 0, 2).astype(F32) / data
    weight_grad = sum(part.astype(F32) for part in last_terms) / data
    return (
        mixed[None],
        grad_value[None],
        grad_gate_one[None],
        grad_gate_two[None],
        filter_grad,
        weight_grad,
    )


def solution(mesh):
    stream = P("dp", "ctx", None)
    return jax.shard_map(
        on_device,
        mesh=mesh,
        in_specs=(stream, stream, stream, P(), P(), stream),
        out_specs=(stream, stream, stream, stream, P(None, "ctx", "dp"), P("dp", "ctx")),
        check_vma=False,
    )
```
